256 devices in a mesh: tm: 16 (over z_lo, y, core), space: 16 (over z_hi, x).
Axes of the slice: x: 4, y: 4, z: 8 (z_hi: 4, z_lo: 2; z = z_hi * 2 + z_lo), core: 2. Of those that a mesh axis runs over, the one named last changes fastest.
Arguments:
- video: bfloat16 [64, 2048, 1152], P('tm', 'space'), may hold values from -4.9 to 4.9
- row_index: int32 [2048], P('space'), may hold values from 0 to 31, as said below
- col_index: int32 [2048], P('space'), may hold values from 0 to 63, as said below
- frame_index: int32 [64], P('tm'), may hold values from 0 to 95, as said below
- spatial_shift: float32 [1152], replicated, may hold values from -3 to 3
- spatial_scale: float32 [1152], replicated, may hold values from -0.5 to 0.5
- spatial_gate: float32 [1152], replicated, may hold values from 1 to 2
- spatial_qkv: bfloat16 [1152, 1728], replicated
- spatial_out: bfloat16 [576, 1152], replicated, may hold values from -0.25 to 0.25
- temporal_shift: float32 [1152], replicated, may hold values from -3 to 3
- temporal_scale: float32 [1152], replicated, may hold values from -0.5 to 0.5
- temporal_gate: float32 [1152], replicated, may hold values from 1 to 2
- temporal_qkv: bfloat16 [1152, 1728], replicated
- temporal_out: bfloat16 [576, 1152], replicated, may hold values from -0.25 to 0.25
Outputs:
- video_out: bfloat16 [64, 2048, 1152], P('tm', 'space')
The draws below stay inside these ranges and needn't reach their ends.
Inputs may be any that keep to these rules, and one draw needn't show every extreme that they name: row_index * 64 + col_index takes every value of 0 to 2047 exactly once. `col_index`: see row_index. `frame_index`: starts at 0 and rises from each frame to the next by 1 or 2, by 2 in exactly 32 of the steps.
All inputs are finite; a program needn't handle non-finite values.
Results may differ from the reference program's by a relative error of at most 0.04.
Values may be sent and summed in bfloat16 or wider, within the bound.
A program may use at most 192 MiB of HBM per device.

```python
import math
import jax
import jax.numpy as jnp
from jax import lax

D = 1152
HEADS = 8
HD = 72
GRID_W = 64
INNER = 576
PATCHES = 2048
FRAMES = 64
GRID_H = 32


def shared_grid(key):
    return jax.random.permutation(key, jnp.arange(PATCHES, dtype=jnp.int32)).astype(jnp.int32)


def draw_video(key, part):
    order = shared_grid(key)
    key = jax.random.fold_in(key, 7)
    key_list = jax.random.split(key, 4)
    row_pos = (order // GRID_W).astype(jnp.float32)
    col_pos = (order % GRID_W).astype(jnp.float32)
    wave_pick = jax.random.randint(key_list[0], (D,), 0, 4)
    row_wave = jnp.where(wave_pick == 0, 0.0, 1.0).astype(jnp.float32)
    col_wave = jnp.where(wave_pick == 1, -1.0, jnp.where(wave_pick == 2, 0.0, 1.0)).astype(jnp.float32)
    offsets = jax.random.uniform(key_list[1], (FRAMES, 1, D), jnp.float32, -math.pi, math.pi)
    amplitude = jax.random.uniform(key_list[2], (D,), jnp.float32, 0.6, 1.4)
    wave_arg = 2.0 * math.pi * (row_pos[:, None] * row_wave[None, :] / GRID_H + col_pos[:, None] * col_wave[None, :] / GRID_W)
    smooth = amplitude * jnp.cos(wave_arg[None, :, :] + offsets)
    rough_part = 0.7 * jnp.clip(jax.random.normal(key_list[3], (FRAMES, PATCHES, D), jnp.float32), -5.0, 5.0)
    total = (smooth + rough_part).astype(jnp.float32)
    return total.astype(jnp.bfloat16)


def draw_row_index(key, part):
    order = shared_grid(key)
    return (order // GRID_W).astype(jnp.int32)


def draw_col_index(key, part):
    order = shared_grid(key)
    return (order % GRID_W).astype(jnp.int32)


def draw_frame_index(key, part):
    key = jax.random.fold_in(key, 5)
    gap_order = jax.random.permutation(key, jnp.arange(FRAMES - 1, dtype=jnp.int32)).astype(jnp.int32)
    strides = jnp.where(gap_order < FRAMES // 2, 2, 1).astype(jnp.int32)
    later = jnp.arange(FRAMES, dtype=jnp.int32)[:, None]
    gaps = jnp.arange(FRAMES - 1, dtype=jnp.int32)[None, :]
    below = jnp.where(gaps < later, 1, 0).astype(jnp.int32)
    return jnp.sum(below * strides[None, :], axis=1).astype(jnp.int32)


def weight_blocks(key):
    key_list = jax.random.split(key, 3)
    base_q = jax.random.normal(key_list[0], (D, INNER), jnp.float32)
    base_k = jax.random.normal(key_list[1], (D, INNER), jnp.float32)
    base_v = jax.random.normal(key_list[2], (D, INNER), jnp.float32)
    return (base_q, base_k, base_v)


def draw_spatial_qkv(key, part):
    key = jax.random.fold_in(key, 11)
    base_q, base_k, base_v = weight_blocks(key)
    lift = 1.7 * D ** (-0.5)
    w_query = base_q * lift
    w_key = base_k * lift
    w_value = base_v * D ** (-0.5)
    return jnp.concatenate([w_query, w_key, w_value], axis=1).astype(jnp.float32).astype(jnp.bfloat16)


def draw_temporal_qkv(key, part):
    key = jax.random.fold_in(key, 12)
    base_q, base_k, base_v = weight_blocks(key)
    lift = 1.7 * D ** (-0.5)
    w_query = base_q * lift
    w_key = base_k * lift
    w_value = base_v * D ** (-0.5)
    return jnp.concatenate([w_query, w_key, w_value], axis=1).astype(jnp.float32).astype(jnp.bfloat16)


def normal_values(rng, dims, scale, bound, held_as=jnp.bfloat16):
    return jnp.clip(scale * jax.random.normal(rng, dims, jnp.float32), -bound, bound).astype(held_as)


def setup_inputs(seed: int = 0) -> dict:
    arg_keys = jax.random.split(jax.random.key(seed), 15)
    video = draw_video(jax.random.fold_in(arg_keys[14], 71), 0)
    row_index = draw_row_index(jax.random.fold_in(arg_keys[14], 71), 0)
    col_index = draw_col_index(jax.random.fold_in(arg_keys[14], 71), 0)
    frame_index = draw_frame_index(jax.random.fold_in(arg_keys[14], 71), 0)
    spatial_shift = normal_values(arg_keys[4], (D,), 0.5, 3.0, jnp.float32)
    spatial_scale = jnp.clip(jax.random.uniform(arg_keys[5], (D,), jnp.float32, -0.5, 0.5), -0.5, 0.5)
    spatial_gate = jnp.clip(jax.random.uniform(arg_keys[6], (D,), jnp.float32, 1.0, 2.0), 1.0, 2.0)
    spatial_qkv = draw_spatial_qkv(jax.random.fold_in(arg_keys[14], 71), 0)
    spatial_out = normal_values(arg_keys[8], (INNER, D), INNER ** -0.5, 0.25)
    temporal_shift = normal_values(arg_keys[9], (D,), 0.5, 3.0, jnp.float32)
    temporal_scale = jnp.clip(jax.random.uniform(arg_keys[10], (D,), jnp.float32, -0.5, 0.5), -0.5, 0.5)
    temporal_gate = jnp.clip(jax.random.uniform(arg_keys[11], (D,), jnp.float32, 1.0, 2.0), 1.0, 2.0)
    temporal_qkv = draw_temporal_qkv(jax.random.fold_in(arg_keys[14], 71), 0)
    temporal_out = normal_values(arg_keys[13], (INNER, D), INNER ** -0.5, 0.25)
    return {"video": video, "row_index": row_index, "col_index": col_index, "frame_index": frame_index, "spatial_shift": spatial_shift, "spatial_scale": spatial_scale, "spatial_gate": spatial_gate, "spatial_qkv": spatial_qkv, "spatial_out": spatial_out, "temporal_shift": temporal_shift, "temporal_scale": temporal_scale, "temporal_gate": temporal_gate, "temporal_qkv": temporal_qkv, "temporal_out": temporal_out}


EPSILON = 1e-06

def normalize(stream):
    stream = stream.astype(jnp.float32)
    centre = stream - lax.optimization_barrier(jnp.mean(stream, axis=-1, keepdims=True))
    spread = lax.optimization_barrier(jnp.mean(centre * centre, axis=-1, keepdims=True))
    return centre * lax.rsqrt(spread + EPSILON)

def frequencies(pairs):
    return 10000.0 ** (-jnp.arange(pairs, dtype=jnp.float32) / pairs)

def rotate(vector, angles):
    half_size = vector.shape[-1] // 2
    leading = vector[..., :half_size]
    trailing = vector[..., half_size:]
    cosine = jnp.cos(angles)
    sines = jnp.sin(angles)
    return jnp.concatenate([leading * cosine - trailing * sines, trailing * cosine + leading * sines], axis=-1)

def space_rotate(vector, row_angles, col_angles):
    half_size = vector.shape[-1] // 2
    return jnp.concatenate([rotate(vector[..., :half_size], row_angles), rotate(vector[..., half_size:], col_angles)], axis=-1)

def widened(tensor):
    return lax.optimization_barrier(tensor).astype(jnp.float32)

def reference(video, row_index, col_index, frame_index, spatial_shift, spatial_scale, spatial_gate, spatial_qkv, spatial_out, temporal_shift, temporal_scale, temporal_gate, temporal_qkv, temporal_out):
    inv_root = 1.0 / math.sqrt(HD)
    row_angles = (row_index.astype(jnp.float32)[:, None] * frequencies(HD // 4))[None, :, None, :]
    col_angles = (col_index.astype(jnp.float32)[:, None] * frequencies(HD // 4))[None, :, None, :]
    time_angles = (frame_index.astype(jnp.float32)[:, None] * frequencies(HD // 2))[:, None, None, :]
    modulated = (normalize(video) * (1.0 + spatial_scale) + spatial_shift).astype(jnp.bfloat16)
    joined = jnp.dot(modulated.reshape(-1, D), spatial_qkv, preferred_element_type=jnp.float32)
    joined = joined.reshape(FRAMES, PATCHES, 3, HEADS, HD)
    queries = space_rotate(joined[:, :, 0], row_angles, col_angles).astype(jnp.bfloat16)
    key_vectors = space_rotate(joined[:, :, 1], row_angles, col_angles).astype(jnp.bfloat16)
    value_vectors = joined[:, :, 2].astype(jnp.bfloat16)

    def frame_attention(pieces):
        frame_q, frame_k, frame_v = pieces
        scores = jnp.einsum('phe,khe->hpk', widened(frame_q), widened(frame_k)) * inv_root
        row_top = lax.optimization_barrier(jnp.max(scores, axis=-1, keepdims=True))
        weights = jnp.exp(scores - row_top)
        totals = lax.optimization_barrier(jnp.sum(weights, axis=-1))
        mixed_out = jnp.einsum('hpk,khe->phe', widened(weights.astype(jnp.bfloat16)), widened(frame_v))
        return (mixed_out / jnp.transpose(totals)[:, :, None]).astype(jnp.bfloat16)
    attended = lax.map(frame_attention, (queries, key_vectors, value_vectors))
    branch = jnp.dot(attended.reshape(-1, INNER), spatial_out, preferred_element_type=jnp.float32)
    after = (video.astype(jnp.float32) + spatial_gate * branch.reshape(FRAMES, PATCHES, D)).astype(jnp.bfloat16)
    modulated = (normalize(after) * (1.0 + temporal_scale) + temporal_shift).astype(jnp.bfloat16)
    joined = jnp.dot(modulated.reshape(-1, D), temporal_qkv, preferred_element_type=jnp.float32)
    joined = joined.reshape(FRAMES, PATCHES, 3, HEADS, HD)
    time_queries = rotate(joined[:, :, 0], time_angles).astype(jnp.bfloat16)
    time_keys = rotate(joined[:, :, 1], time_angles).astype(jnp.bfloat16)
    time_values = joined[:, :, 2].astype(jnp.bfloat16)
    block_size = min(PATCHES, 256)
    block_count = PATCHES // block_size

    def patch_block(pieces):
        block_q, block_k, block_v = pieces
        scores = jnp.einsum('fphe,gphe->phfg', widened(block_q), widened(block_k)) * inv_root
        row_top = lax.optimization_barrier(jnp.max(scores, axis=-1, keepdims=True))
        weights = jnp.exp(scores - row_top)
        totals = lax.optimization_barrier(jnp.sum(weights, axis=-1))
        mixed_out = jnp.einsum('phfg,gphe->fphe', widened(weights.astype(jnp.bfloat16)), widened(block_v))
        return (mixed_out / jnp.transpose(totals, (2, 0, 1))[..., None]).astype(jnp.bfloat16)

    def blocked(tensor):
        return jnp.transpose(tensor.reshape(FRAMES, block_count, block_size, HEADS, HD), (1, 0, 2, 3, 4))
    pieces_out = lax.map(patch_block, (blocked(time_queries), blocked(time_keys), blocked(time_values)))
    time_attended = jnp.transpose(pieces_out, (1, 0, 2, 3, 4)).reshape(FRAMES, PATCHES, HEADS, HD)
    branch = jnp.dot(time_attended.reshape(-1, INNER), temporal_out, preferred_element_type=jnp.float32)
    return (after.astype(jnp.float32) + temporal_gate * branch.reshape(FRAMES, PATCHES, D)).astype(jnp.bfloat16)
```

```python
import functools
import math

import jax
import jax.numpy as jnp
import numpy as np
from jax import lax
from jax.experimental import pallas as pl
from jax.experimental.pallas import tpu as pltpu
from jax.sharding import PartitionSpec as P

HEADS = 8
HD = 72
D = 1152
INNER = HEADS * HD
FRAMES = 4
PATCHES = 128
SPACE = 16
PAIR = 2 * HD
EPSILON = 1e-06
MESH = pl.DeviceIdType.MESH
BF16 = jnp.bfloat16
F32 = jnp.float32


def normalize(stream):
    stream = stream.astype(jnp.float32)
    centre = stream - jnp.mean(stream, axis=-1, keepdims=True)
    spread = jnp.mean(centre * centre, axis=-1, keepdims=True)
    return centre * lax.rsqrt(spread + EPSILON)


def frequencies(pairs):
    return 10000.0 ** (-jnp.arange(pairs, dtype=jnp.float32) / pairs)


def rotate(vector, angles):
    half_size = vector.shape[-1] // 2
    leading = vector[..., :half_size]
    trailing = vector[..., half_size:]
    cosine = jnp.cos(angles)
    sines = jnp.sin(angles)
    return jnp.concatenate(
        [leading * cosine - trailing * sines, trailing * cosine + leading * sines], axis=-1
    )


def rotation_tables(angles, half):
    lane = lax.broadcasted_iota(jnp.int32, angles.shape, 1)
    leading = lax.rem(lane, 2 * half) < half
    cosine = jnp.cos(angles)
    sine = jnp.sin(angles)
    lead = jnp.where(leading, -sine, 0.0)
    trail = jnp.where(leading, 0.0, sine)
    return [jnp.concatenate([t] * (2 * HEADS), axis=1) for t in (cosine, lead, trail)]


def rotated(u, cosine, lead, trail, half):
    width = u.shape[1]
    ahead = pltpu.roll(u, width - half, 1)
    behind = pltpu.roll(u, half, 1)
    return u * cosine + ahead * lead + behind * trail


def space_kernel(
    video, pos, freq, shift, scale, w, out,
    send_kv, send_q, recv_kv, recv_q, send_o, key_a, key_b, value_t, tables,
    kv_ssem, kv_rsem, q_ssem, q_rsem, o_ssem, o_rsem, local_sem,
):
    me = lax.axis_index("space")
    zh = me // 4
    x = lax.rem(me, 4)

    barrier = pltpu.get_barrier_semaphore()
    for k in range(1, SPACE):
        other = lax.rem(me + k, SPACE)
        pl.semaphore_signal(barrier, 1, device_id={"space": other}, device_id_type=MESH)

    angles = pos[:, 0:1] * freq[0:1, :] + pos[:, 1:2] * freq[1:2, :]
    for i, t in enumerate(rotation_tables(angles, HD // 4)):
        tables[i] = t

    offsets = (2, 1, 3, 0)

    def project(i):
        f = lax.rem(zh + offsets[i], 4)
        y = jnp.dot(
            (normalize(video[f]) * (1.0 + scale[...]) + shift[...]).astype(BF16),
            w[...],
            preferred_element_type=F32,
        )
        turned = rotated(y[:, : 2 * INNER], tables[0], tables[1], tables[2], HD // 4)
        turned = jnp.transpose(turned).astype(BF16)
        values = jnp.transpose(y[:, 2 * INNER :]).astype(BF16)
        for c in range(4):
            r = slice(c * PAIR, (c + 1) * PAIR)
            send_q[i, c] = turned[r]
            send_kv[i, c, 0:PAIR] = turned[INNER + c * PAIR : INNER + (c + 1) * PAIR]
            send_kv[i, c, PAIR : 2 * PAIR] = values[r]

    def copy_to(i, k, src, dst, ssem, rsem):
        c = lax.rem(x + k, 4)
        f = lax.rem(zh + offsets[i], 4)
        return pltpu.make_async_remote_copy(
            src_ref=src.at[i, c],
            dst_ref=dst.at[me],
            send_sem=ssem.at[i, k],
            recv_sem=rsem.at[me],
            device_id={"space": f * 4 + c},
            device_id_type=MESH,
        )

    remote = [(i, k) for i in range(4) for k in (1, 3, 2, 0) if (i, k) != (3, 0)]
    project(0)
    pl.semaphore_wait(barrier, SPACE - 1)
    for i in range(4):
        if i:
            project(i)
        for k in (1, 3, 2, 0):
            if (i, k) in remote:
                copy_to(i, k, send_kv, recv_kv, kv_ssem, kv_rsem).start()
    for i, k in remote:
        copy_to(i, k, send_q, recv_q, q_ssem, q_rsem).start()

    lane = lax.broadcasted_iota(jnp.int32, (PATCHES, PAIR), 1)
    first = lane < HD
    value_t[PAIR:] = jnp.where(
        lax.broadcasted_iota(jnp.int32, (16, SPACE * PATCHES), 0) == 0, 1.0, 0.0
    ).astype(BF16)

    def place(kv, j):
        rows = pl.ds(pl.multiple_of(j * PATCHES, PATCHES), PATCHES)
        keys = jnp.transpose(kv[0:PAIR].astype(F32))
        key_a[rows] = jnp.where(first, keys, 0.0).astype(BF16)
        key_b[rows] = jnp.where(first, 0.0, keys).astype(BF16)
        value_t[0:PAIR, rows] = kv[PAIR : 2 * PAIR]

    place(send_kv[3, x], me)
    recv_q[me] = send_q[3, x]

    def source(n):
        i = n // 4
        off = jnp.where(i == 0, 2, jnp.where(i == 1, 3, jnp.where(i == 2, 1, 0)))
        return lax.rem(zh + off, 4) * 4 + lax.rem(x + 1 + lax.rem(n, 4), 4)

    def arrive(n, carry):
        j = source(n)
        pltpu.make_async_remote_copy(
            src_ref=send_kv.at[0, 0], dst_ref=recv_kv.at[j], send_sem=kv_ssem.at[0, 0],
            recv_sem=kv_rsem.at[j], device_id={"space": j}, device_id_type=MESH,
        ).wait_recv()
        place(recv_kv[j], j)
        return carry

    lax.fori_loop(0, SPACE - 1, arrive, 0)

    def wait_q(n, carry):
        j = source(n)
        pltpu.make_async_remote_copy(
            src_ref=send_q.at[0, 0], dst_ref=recv_q.at[j], send_sem=q_ssem.at[0, 0],
            recv_sem=q_rsem.at[j], device_id={"space": j}, device_id_type=MESH,
        ).wait_recv()
        return carry

    lax.fori_loop(0, SPACE - 1, wait_q, 0)

    factor = math.log2(math.e) / math.sqrt(HD)
    row = lax.broadcasted_iota(jnp.int32, (PAIR, 2 * PATCHES), 0)

    def o_copy(j):
        return pltpu.make_async_remote_copy(
            src_ref=send_o.at[j],
            dst_ref=out.at[me],
            send_sem=o_ssem.at[j],
            recv_sem=o_rsem.at[me],
            device_id={"space": j},
            device_id_type=MESH,
        )

    def attend(n, carry):
        b = lax.rem(me // 2 + 1 + n, SPACE // 2)
        queries = jnp.concatenate([recv_q[2 * b], recv_q[2 * b + 1]], axis=1)
        mixed = []
        for keys in (key_a, key_b):
            scores = jnp.dot(keys[...], queries, preferred_element_type=F32)
            top = jnp.max(scores, axis=0, keepdims=True)
            weights = jnp.exp2((scores - top) * factor).astype(BF16)
            both = jnp.dot(value_t[...], weights, preferred_element_type=F32)
            mixed.append(both[0:PAIR] / both[PAIR : PAIR + 1])
        result = jnp.where(row < HD, mixed[0], mixed[1]).astype(BF16)
        for e in range(2):
            j = 2 * b + e
            send_o[j] = result[:, e * PATCHES : (e + 1) * PATCHES]

            @pl.when(j != me)
            def _():
                o_copy(j).start()

        return carry

    lax.fori_loop(0, SPACE // 2, attend, 0)
    own = pltpu.make_async_copy(send_o.at[me], out.at[me], local_sem)
    own.start()
    own.wait()

    for i, k in remote:
        copy_to(i, k, send_kv, recv_kv, kv_ssem, kv_rsem).wait_send()
        copy_to(i, k, send_q, recv_q, q_ssem, q_rsem).wait_send()

    def finish(n, carry):
        j = lax.rem(me + 1 + n, SPACE)
        o_copy(j).wait_send()
        pltpu.make_async_remote_copy(
            src_ref=send_o.at[j], dst_ref=out.at[j], send_sem=o_ssem.at[j],
            recv_sem=o_rsem.at[j], device_id={"space": j}, device_id_type=MESH,
        ).wait_recv()
        return carry

    lax.fori_loop(0, SPACE - 1, finish, 0)


def space_attention(video, pos, freq, shift, scale, w):
    vmem = pl.BlockSpec(memory_space=pltpu.VMEM)
    dma = pltpu.SemaphoreType.DMA
    tokens = SPACE * PATCHES
    return pl.pallas_call(
        space_kernel,
        out_shape=jax.ShapeDtypeStruct((SPACE, PAIR, PATCHES), BF16),
        in_specs=[vmem] * 6,
        out_specs=vmem,
        scratch_shapes=[
            pltpu.VMEM((4, 4, 2 * PAIR, PATCHES), BF16),
            pltpu.VMEM((4, 4, PAIR, PATCHES), BF16),
            pltpu.VMEM((SPACE, 2 * PAIR, PATCHES), BF16),
            pltpu.VMEM((SPACE, PAIR, PATCHES), BF16),
            pltpu.VMEM((SPACE, PAIR, PATCHES), BF16),
            pltpu.VMEM((tokens, PAIR), BF16),
            pltpu.VMEM((tokens, PAIR), BF16),
            pltpu.VMEM((PAIR + 16, tokens), BF16),
            pltpu.VMEM((3, PATCHES, 2 * INNER), F32),
            dma((4, 4)), dma((SPACE,)), dma((4, 4)), dma((SPACE,)), dma((SPACE,)), dma((SPACE,)), dma,
        ],
        compiler_params=pltpu.CompilerParams(
            collective_id=1, has_side_effects=True, vmem_limit_bytes=52 * 2**20
        ),
        name="space_attention",
    )(video, pos, freq, shift, scale, w)


def project(stream, shift, scale, weights):
    frames_here, patches_here, model_width = stream.shape
    modulated = (normalize(stream) * (1.0 + scale) + shift).astype(jnp.bfloat16)
    joined = jnp.dot(
        modulated.reshape(-1, model_width), weights, preferred_element_type=jnp.float32
    )
    return joined.reshape(frames_here, patches_here, 3, HEADS, HD)


def residual_add(stream, attended, gate, weights):
    frames_here, patches_here, model_width = stream.shape
    branch = jnp.dot(
        attended.reshape(frames_here * patches_here, -1),
        weights,
        preferred_element_type=jnp.float32,
    )
    return (stream.astype(jnp.float32) + gate * branch.reshape(stream.shape)).astype(jnp.bfloat16)


def space_frequencies():
    f = 10000.0 ** (-np.arange(HD // 4, dtype=np.float32) / (HD // 4))
    zero = np.zeros_like(f)
    table = np.zeros((8, HD), np.float32)
    table[0] = np.concatenate([f, f, zero, zero])
    table[1] = np.concatenate([zero, zero, f, f])
    return jnp.asarray(table)


def body(
    video,
    row_index,
    col_index,
    frame_index,
    spatial_shift,
    spatial_scale,
    spatial_gate,
    spatial_qkv,
    spatial_out,
    temporal_shift,
    temporal_scale,
    temporal_gate,
    temporal_qkv,
    temporal_out,
):
    inv_root = 1.0 / math.sqrt(HD)
    pos = jnp.stack([row_index, col_index], axis=1).astype(F32)
    attended = space_attention(
        video, pos, space_frequencies(), spatial_shift[None], spatial_scale[None], spatial_qkv
    )
    attended = jnp.transpose(attended.reshape(FRAMES, INNER, PATCHES), (0, 2, 1))
    after = residual_add(video, attended, spatial_gate, spatial_out)
    time_angles = (frame_index.astype(jnp.float32)[:, None] * frequencies(HD // 2))[
        :, None, None, :
    ]
    joined = project(after, temporal_shift, temporal_scale, temporal_qkv)
    time_queries = rotate(joined[:, :, 0], time_angles).astype(jnp.bfloat16)
    time_keys = rotate(joined[:, :, 1], time_angles).astype(jnp.bfloat16)
    time_values = joined[:, :, 2].astype(jnp.bfloat16)
    frame_q = lax.all_to_all(time_queries, "tm", split_axis=1, concat_axis=0, tiled=True)
    frame_k = lax.all_to_all(time_keys, "tm", split_axis=1, concat_axis=0, tiled=True)
    frame_v = lax.all_to_all(time_values, "tm", split_axis=1, concat_axis=0, tiled=True)
    scores = (
        jnp.einsum("fphe,gphe->phfg", frame_q, frame_k, preferred_element_type=jnp.float32)
        * inv_root
    )
    row_top = jnp.max(scores, axis=-1, keepdims=True)
    weights = jnp.exp(scores - row_top)
    totals = jnp.sum(weights, axis=-1)
    mixed_out = jnp.einsum(
        "phfg,gphe->fphe", weights.astype(jnp.bfloat16), frame_v, preferred_element_type=jnp.float32
    )
    time_mixed = (mixed_out / jnp.transpose(totals, (2, 0, 1))[..., None]).astype(jnp.bfloat16)
    time_back = lax.all_to_all(time_mixed, "tm", split_axis=0, concat_axis=1, tiled=True)
    return residual_add(after, time_back, temporal_gate, temporal_out)


def solution(mesh):
    return jax.shard_map(
        body,
        mesh=mesh,
        in_specs=(P("tm", "space", None), P("space"), P("space"), P("tm")) + (P(),) * 10,
        out_specs=P("tm", "space", None),
        check_vma=False,
    )
```

```python
import math

import jax
import jax.numpy as jnp
import numpy as np
from jax import lax
from jax.experimental import pallas as pl
from jax.experimental.pallas import tpu as pltpu
from jax.sharding import PartitionSpec as P

HEADS = 8
HD = 72
D = 1152
INNER = HEADS * HD
FRAMES = 4
PATCHES = 128
SPACE = 16
PAIR = 2 * HD
TM = 16
HALF = INNER % 128
WIDE = INNER + HALF
LANES = 3 * INNER + HALF
EPSILON = 1e-06
MESH = pl.DeviceIdType.MESH
BF16 = jnp.bfloat16
F32 = jnp.float32


def normalize(stream):
    stream = stream.astype(jnp.float32)
    centre = stream - jnp.mean(stream, axis=-1, keepdims=True)
    spread = jnp.mean(centre * centre, axis=-1, keepdims=True)
    return centre * lax.rsqrt(spread + EPSILON)


def rotated(u, cosine, lead, trail, half, axis):
    ahead = pltpu.roll(u, u.shape[axis] - half, axis)
    behind = pltpu.roll(u, half, axis)
    return u * cosine + ahead * lead + behind * trail


def space_kernel(
    video, pos, table, shift, scale, w, out,
    send_kv, send_q, recv_kv, recv_q, send_o, key_a, key_b, value_t, w_held,
    kv_ssem, kv_rsem, q_ssem, q_rsem, o_ssem, o_rsem, local_sem, w_sem,
):
    me = lax.axis_index("space")
    zh = me // 4
    x = lax.rem(me, 4)

    barrier = pltpu.get_barrier_semaphore()
    for k in range(1, SPACE):
        other = lax.rem(me + k, SPACE)
        pl.semaphore_signal(barrier, 1, device_id={"space": other}, device_id_type=MESH)

    loads = []
    for n in range(3):
        part = pl.ds(n * INNER, INNER)
        loads.append(pltpu.make_async_copy(w.at[part], w_held.at[part], w_sem.at[n]))
        loads[-1].start()

    angles = table[:, 0:1] * pos[0:1, :] + table[:, 1:2] * pos[1:2, :]
    cosine = jnp.cos(angles)
    sine = jnp.sin(angles)
    lead = sine * table[:, 2:3]
    trail = sine * table[:, 3:4]

    offsets = (2, 1, 3, 0)

    def project(i):
        frames = [lax.rem(zh + offsets[i + e], 4) for e in range(2)]
        mixed = [
            (normalize(video[f]) * (1.0 + scale[...]) + shift[...]).astype(BF16) for f in frames
        ]
        mixed = jnp.concatenate(mixed, axis=0)
        if i == 0:
            for load in loads:
                load.wait()
        y = lax.dot_general(
            w_held[...], mixed, (((1,), (1,)), ((), ())), preferred_element_type=F32
        )

        def turned(n, e):
            u = y[n * HD : (n + 1) * HD, e * PATCHES : (e + 1) * PATCHES]
            return rotated(u, cosine, lead, trail, HD // 4, 0)

        for e in range(2):
            for c in range(4):
                first = 2 * c
                send_q[i + e, c] = jnp.concatenate(
                    [turned(first, e), turned(first + 1, e)], axis=0
                ).astype(BF16)
                send_kv[i + e, c, 0:PAIR] = jnp.concatenate(
                    [turned(HEADS + first, e), turned(HEADS + first + 1, e)], axis=0
                ).astype(BF16)
                rows = slice(2 * INNER + c * PAIR, 2 * INNER + (c + 1) * PAIR)
                send_kv[i + e, c, PAIR : 2 * PAIR] = y[
                    rows, e * PATCHES : (e + 1) * PATCHES
                ].astype(BF16)

    def copy_to(i, k, src, dst, ssem, rsem):
        c = lax.rem(x + k, 4)
        f = lax.rem(zh + offsets[i], 4)
        return pltpu.make_async_remote_copy(
            src_ref=src.at[i, c],
            dst_ref=dst.at[me],
            send_sem=ssem.at[i, k],
            recv_sem=rsem.at[me],
            device_id={"space": f * 4 + c},
            device_id_type=MESH,
        )

    remote = [(i, k) for i in range(4) for k in (1, 3, 2, 0) if (i, k) != (3, 0)]
    project(0)
    pl.semaphore_wait(barrier, SPACE - 1)
    for i in range(4):
        if i == 2:
            project(i)
        for k in (1, 3, 2, 0):
            if (i, k) in remote:
                copy_to(i, k, send_kv, recv_kv, kv_ssem, kv_rsem).start()
    for i, k in remote:
        copy_to(i, k, send_q, recv_q, q_ssem, q_rsem).start()

    lane = lax.broadcasted_iota(jnp.int32, (PATCHES, PAIR), 1)
    first = lane < HD
    value_t[PAIR:] = jnp.where(
        lax.broadcasted_iota(jnp.int32, (16, SPACE * PATCHES), 0) == 0, 1.0, 0.0
    ).astype(BF16)

    def place(kv, j):
        rows = pl.ds(pl.multiple_of(j * PATCHES, PATCHES), PATCHES)
        keys = jnp.transpose(kv[0:PAIR].astype(F32))
        key_a[rows] = jnp.where(first, keys, 0.0).astype(BF16)
        key_b[rows] = jnp.where(first, 0.0, keys).astype(BF16)
        value_t[0:PAIR, rows] = kv[PAIR : 2 * PAIR]

    place(send_kv[3, x], me)
    recv_q[me] = send_q[3, x]

    def source(n):
        i = n // 4
        off = jnp.where(i == 0, 2, jnp.where(i == 1, 3, jnp.where(i == 2, 1, 0)))
        return lax.rem(zh + off, 4) * 4 + lax.rem(x + 1 + lax.rem(n, 4), 4)

    def arrive(n, carry):
        j = source(n)
        pltpu.make_async_remote_copy(
            src_ref=send_kv.at[0, 0], dst_ref=recv_kv.at[j], send_sem=kv_ssem.at[0, 0],
            recv_sem=kv_rsem.at[j], device_id={"space": j}, device_id_type=MESH,
        ).wait_recv()
        place(recv_kv[j], j)
        return carry

    lax.fori_loop(0, SPACE - 1, arrive, 0)

    def wait_q(n, carry):
        j = source(n)
        pltpu.make_async_remote_copy(
            src_ref=send_q.at[0, 0], dst_ref=recv_q.at[j], send_sem=q_ssem.at[0, 0],
            recv_sem=q_rsem.at[j], device_id={"space": j}, device_id_type=MESH,
        ).wait_recv()
        return carry

    lax.fori_loop(0, SPACE - 1, wait_q, 0)

    factor = math.log2(math.e) / math.sqrt(HD)
    row = lax.broadcasted_iota(jnp.int32, (PAIR, 2 * PATCHES), 0)

    def o_copy(j):
        return pltpu.make_async_remote_copy(
            src_ref=send_o.at[j],
            dst_ref=out.at[me],
            send_sem=o_ssem.at[j],
            recv_sem=o_rsem.at[me],
            device_id={"space": j},
            device_id_type=MESH,
        )

    def attend(n, carry):
        b = lax.rem(me // 2 + 1 + n, SPACE // 2)
        queries = jnp.concatenate([recv_q[2 * b], recv_q[2 * b + 1]], axis=1)
        mixed = []
        for keys in (key_a, key_b):
            scores = jnp.dot(keys[...], queries, preferred_element_type=F32)
            top = jnp.max(scores, axis=0, keepdims=True)
            weights = jnp.exp2((scores - top) * factor).astype(BF16)
            both = jnp.dot(value_t[...], weights, preferred_element_type=F32)
            mixed.append(both[0:PAIR] / both[PAIR : PAIR + 1])
        result = jnp.where(row < HD, mixed[0], mixed[1]).astype(BF16)
        for e in range(2):
            j = 2 * b + e
            send_o[j] = result[:, e * PATCHES : (e + 1) * PATCHES]

            @pl.when(j != me)
            def _():
                o_copy(j).start()

        return carry

    lax.fori_loop(0, SPACE // 2, attend, 0)
    own = pltpu.make_async_copy(send_o.at[me], out.at[me], local_sem)
    own.start()
    own.wait()

    for i, k in remote:
        copy_to(i, k, send_kv, recv_kv, kv_ssem, kv_rsem).wait_send()
        copy_to(i, k, send_q, recv_q, q_ssem, q_rsem).wait_send()

    def finish(n, carry):
        j = lax.rem(me + 1 + n, SPACE)
        o_copy(j).wait_send()
        pltpu.make_async_remote_copy(
            src_ref=send_o.at[j], dst_ref=out.at[j], send_sem=o_ssem.at[j],
            recv_sem=o_rsem.at[j], device_id={"space": j}, device_id_type=MESH,
        ).wait_recv()
        return carry

    lax.fori_loop(0, SPACE - 1, finish, 0)


def space_attention(video, pos, table, shift, scale, w):
    vmem = pl.BlockSpec(memory_space=pltpu.VMEM)
    dma = pltpu.SemaphoreType.DMA
    tokens = SPACE * PATCHES
    return pl.pallas_call(
        space_kernel,
        out_shape=jax.ShapeDtypeStruct((SPACE, PAIR, PATCHES), BF16),
        in_specs=[vmem] * 5 + [pl.BlockSpec(memory_space=pl.ANY)],
        out_specs=vmem,
        scratch_shapes=[
            pltpu.VMEM((4, 4, 2 * PAIR, PATCHES), BF16),
            pltpu.VMEM((4, 4, PAIR, PATCHES), BF16),
            pltpu.VMEM((SPACE, 2 * PAIR, PATCHES), BF16),
            pltpu.VMEM((SPACE, PAIR, PATCHES), BF16),
            pltpu.VMEM((SPACE, PAIR, PATCHES), BF16),
            pltpu.VMEM((tokens, PAIR), BF16),
            pltpu.VMEM((tokens, PAIR), BF16),
            pltpu.VMEM((PAIR + 16, tokens), BF16),
            pltpu.VMEM((3 * INNER, D), BF16),
            dma((4, 4)), dma((SPACE,)), dma((4, 4)), dma((SPACE,)), dma((SPACE,)), dma((SPACE,)), dma, dma((3,)),
        ],
        compiler_params=pltpu.CompilerParams(
            collective_id=1, has_side_effects=True, vmem_limit_bytes=52 * 2**20
        ),
        name="space_attention",
    )(video, pos, table, shift, scale, w)


def time_kernel(
    attended, video, frame_pos, table, gate_s, out_s, shift, scale, gate_t, w, out_t, out,
    w_held, out_held, after, send, recv, total, send_o, recv_o,
    ssem, rsem, o_ssem, o_rsem, w_sem,
):
    me = lax.axis_index("tm")

    loads = []
    for n, (here, there) in enumerate(((0, 0), (2, 1), (1, 2))):
        loads.append(
            pltpu.make_async_copy(
                w.at[pl.ds(here * INNER, INNER)], w_held.at[pl.ds(there * INNER, INNER)], w_sem.at[n]
            )
        )
    loads.append(pltpu.make_async_copy(out_t, out_held.at[pl.ds(HALF, INNER)], w_sem.at[3]))
    for load in loads:
        load.start()
    w_held[3 * INNER :] = jnp.zeros((HALF, D), BF16)
    out_held[0:HALF] = jnp.zeros((HALF, D), BF16)

    barrier = pltpu.get_barrier_semaphore()
    for k in range(1, TM):
        other = lax.rem(me + k, TM)
        pl.semaphore_signal(barrier, 1, device_id={"tm": other}, device_id_type=MESH)

    angles = frame_pos[:, 0:1] * table[0:1, :]
    cosine = jnp.cos(angles)
    sine = jnp.sin(angles)
    lead = sine * table[1:2, :]
    trail = sine * table[2:3, :]

    def send_copy(i, k):
        d = lax.rem(me + k, TM)
        return pltpu.make_async_remote_copy(
            src_ref=send.at[i, d], dst_ref=recv.at[i, me], send_sem=ssem.at[i, d],
            recv_sem=rsem.at[i, me], device_id={"tm": d}, device_id_type=MESH,
        )

    for i in range(2):
        mixed = jnp.concatenate(
            [jnp.transpose(attended[2 * i + e].astype(F32)).astype(BF16) for e in range(2)], axis=0
        )
        branch = jnp.dot(mixed, out_s[...], preferred_element_type=F32)
        stream = video[2 * i : 2 * i + 2].reshape(2 * PATCHES, D).astype(F32)
        stream = (stream + gate_s[...] * branch).astype(BF16)
        after[2 * i : 2 * i + 2] = stream.reshape(2, PATCHES, D)
        modulated = (normalize(stream) * (1.0 + scale[...]) + shift[...]).astype(BF16)
        if i == 0:
            for load in loads[:3]:
                load.wait()
        y = lax.dot_general(
            modulated, w_held[...], (((1,), (1,)), ((), ())), preferred_element_type=F32
        )
        sides = []
        for e in range(2):
            f = 2 * i + e
            rows = y[e * PATCHES : (e + 1) * PATCHES]
            angle = (cosine[f : f + 1], lead[f : f + 1], trail[f : f + 1])
            side = jnp.concatenate(
                [
                    rotated(rows[:, 0:WIDE], *angle, HD // 2, 1),
                    rows[:, WIDE : 2 * INNER],
                    rotated(rows[:, 2 * INNER :], *angle, HD // 2, 1),
                ],
                axis=1,
            )
            sides.append(side.reshape(TM, 8, LANES))
        send[i] = jnp.stack(sides, axis=1).reshape(TM, 16, LANES).astype(BF16)
        if i == 0:
            pl.semaphore_wait(barrier, TM - 1)
        for k in range(1, TM):
            send_copy(i, k).start()
        recv[i, me] = send[i, me]

    def wait_rows(k, carry):
        j = lax.rem(me + k, TM)
        for i in range(2):
            pltpu.make_async_remote_copy(
                src_ref=send.at[i, j], dst_ref=recv.at[i, j], send_sem=ssem.at[i, j],
                recv_sem=rsem.at[i, j], device_id={"tm": j}, device_id_type=MESH,
            ).wait_recv()
        return carry

    lax.fori_loop(1, TM, wait_rows, 0)

    count = 4 * TM * 8
    factor = math.log2(math.e) / math.sqrt(HD)
    same = lax.rem(lax.broadcasted_iota(jnp.int32, (count, count), 0), 8) == lax.rem(
        lax.broadcasted_iota(jnp.int32, (count, count), 1), 8
    )

    def window(start):
        low = start // 128 * 128
        high = (start + HD + 127) // 128 * 128
        lane = lax.broadcasted_iota(jnp.int32, (count, high - low), 1)
        return low, high, (lane >= start - low) & (lane < start - low + HD)

    total[...] = jnp.zeros((count, WIDE), F32)
    for h in range(HEADS):
        low, high, inside = window(h * HD)
        queries = recv[:, :, :, low:high].reshape(count, high - low)
        keys = recv[:, :, :, 2 * INNER + low : 2 * INNER + high].reshape(count, high - low)
        keys = jnp.where(inside, keys, jnp.zeros_like(keys))
        scores = lax.dot_general(
            queries, keys, (((1,), (1,)), ((), ())), preferred_element_type=F32
        )
        scores = jnp.where(same, scores, -1e30)
        top = jnp.max(scores, axis=1, keepdims=True)
        weights = jnp.exp2((scores - top) * factor)
        sums = jnp.sum(weights, axis=1, keepdims=True)
        low, high, inside = window(HALF + h * HD)
        base = INNER - HALF
        values = recv[:, :, :, base + low : base + high].reshape(count, high - low)
        part = jnp.dot(weights.astype(BF16), values, preferred_element_type=F32)
        total[:, low:high] += jnp.where(inside, part / sums, 0.0)
    send_o[...] = total[...].astype(BF16).reshape(2, TM, 16, WIDE)

    def o_copy(k):
        d = lax.rem(me + k, TM)
        return pltpu.make_async_remote_copy(
            src_ref=send_o.at[:, d], dst_ref=recv_o.at[:, me], send_sem=o_ssem.at[d],
            recv_sem=o_rsem.at[me], device_id={"tm": d}, device_id_type=MESH,
        )

    for k in range(1, TM):
        o_copy(k).start()
    recv_o[:, me] = send_o[:, me]

    def wait_o(k, carry):
        j = lax.rem(me + k, TM)
        pltpu.make_async_remote_copy(
            src_ref=send_o.at[:, j], dst_ref=recv_o.at[:, j], send_sem=o_ssem.at[j],
            recv_sem=o_rsem.at[j], device_id={"tm": j}, device_id_type=MESH,
        ).wait_recv()
        return carry

    lax.fori_loop(1, TM, wait_o, 0)
    loads[3].wait()
    for i in range(2):
        branch = jnp.dot(
            recv_o[i].reshape(2 * PATCHES, WIDE), out_held[...], preferred_element_type=F32
        ).reshape(TM, 2, 8, D)
        for e in range(2):
            f = 2 * i + e
            part = branch[:, e].reshape(PATCHES, D)
            out[f] = (after[f].astype(F32) + gate_t[...] * part).astype(BF16)

    def wait_sends(k, carry):
        d = lax.rem(me + k, TM)
        for i in range(2):
            pltpu.make_async_remote_copy(
                src_ref=send.at[i, d], dst_ref=recv.at[i, me], send_sem=ssem.at[i, d],
                recv_sem=rsem.at[i, me], device_id={"tm": d}, device_id_type=MESH,
            ).wait_send()
        o_copy(k).wait_send()
        return carry

    lax.fori_loop(1, TM, wait_sends, 0)


def time_attention(attended, video, frame_pos, table, gate_s, out_s, shift, scale, gate_t, w, out_t):
    vmem = pl.BlockSpec(memory_space=pltpu.VMEM)
    hbm = pl.BlockSpec(memory_space=pl.ANY)
    dma = pltpu.SemaphoreType.DMA
    return pl.pallas_call(
        time_kernel,
        out_shape=jax.ShapeDtypeStruct((FRAMES, PATCHES, D), BF16),
        in_specs=[vmem] * 9 + [hbm] * 2,
        out_specs=vmem,
        scratch_shapes=[
            pltpu.VMEM((LANES, D), BF16),
            pltpu.VMEM((WIDE, D), BF16),
            pltpu.VMEM((FRAMES, PATCHES, D), BF16),
            pltpu.VMEM((2, TM, 16, LANES), BF16),
            pltpu.VMEM((2, TM, 16, LANES), BF16),
            pltpu.VMEM((4 * TM * 8, WIDE), F32),
            pltpu.VMEM((2, TM, 16, WIDE), BF16),
            pltpu.VMEM((2, TM, 16, WIDE), BF16),
            dma((2, TM)), dma((2, TM)), dma((TM,)), dma((TM,)), dma((4,)),
        ],
        compiler_params=pltpu.CompilerParams(
            collective_id=2, has_side_effects=True, vmem_limit_bytes=52 * 2**20
        ),
        name="time_attention",
    )(attended, video, frame_pos, table, gate_s, out_s, shift, scale, gate_t, w, out_t)


def space_table():
    f = 10000.0 ** (-np.arange(HD // 4, dtype=np.float32) / (HD // 4))
    zero = np.zeros_like(f)
    one = np.ones_like(f)
    table = np.zeros((HD, 8), np.float32)
    table[:, 0] = np.concatenate([f, f, zero, zero])
    table[:, 1] = np.concatenate([zero, zero, f, f])
    table[:, 2] = np.concatenate([-one, zero, -one, zero])
    table[:, 3] = np.concatenate([zero, one, zero, one])
    return jnp.asarray(table)


def time_table():
    f = 10000.0 ** (-np.arange(HD // 2, dtype=np.float32) / (HD // 2))
    zero = np.zeros_like(f)
    one = np.ones_like(f)
    table = np.zeros((8, WIDE), np.float32)
    table[0, :INNER] = np.tile(np.concatenate([f, f]), HEADS)
    table[1, :INNER] = np.tile(np.concatenate([-one, zero]), HEADS)
    table[2, :INNER] = np.tile(np.concatenate([zero, one]), HEADS)
    return jnp.asarray(table)


def body(
    video,
    row_index,
    col_index,
    frame_index,
    spatial_shift,
    spatial_scale,
    spatial_gate,
    spatial_qkv,
    spatial_out,
    temporal_shift,
    temporal_scale,
    temporal_gate,
    temporal_qkv,
    temporal_out,
):
    pos = jnp.stack([row_index, col_index], axis=0).astype(F32)
    attended = space_attention(
        video, pos, space_table(), spatial_shift[None], spatial_scale[None], spatial_qkv.T
    )
    return time_attention(
        attended.reshape(FRAMES, INNER, PATCHES),
        video,
        frame_index.astype(F32)[:, None],
        time_table(),
        spatial_gate[None],
        spatial_out,
        temporal_shift[None],
        temporal_scale[None],
        temporal_gate[None],
        temporal_qkv.T,
        temporal_out,
    )


def solution(mesh):
    return jax.shard_map(
        body,
        mesh=mesh,
        in_specs=(P("tm", "space", None), P("space"), P("space"), P("tm")) + (P(),) * 10,
        out_specs=P("tm", "space", None),
        check_vma=False,
    )
```

```python
import math

import jax
import jax.numpy as jnp
import numpy as np
from jax import lax
from jax.experimental import pallas as pl
from jax.experimental.pallas import tpu as pltpu
from jax.sharding import PartitionSpec as P

HEADS = 8
HD = 72
D = 1152
INNER = HEADS * HD
FRAMES = 4
PATCHES = 128
SPACE = 16
PAIR = 2 * HD
TM = 16
NEAR = 8
TOKENS = FRAMES * PATCHES
KEYS = SPACE * PATCHES
HALF = INNER % 128
WIDE = INNER + HALF
LANES = 3 * INNER + HALF
FACTOR = math.log2(math.e) / math.sqrt(HD)
CHUNK = 512
EPSILON = 1e-06
MESH = pl.DeviceIdType.MESH
BF16 = jnp.bfloat16
F32 = jnp.float32


def modulated(stream, scale, shift):
    stream = stream.astype(F32)
    centre = stream - jnp.mean(stream, axis=-1, keepdims=True)
    spread = jnp.mean(centre * centre, axis=-1, keepdims=True)
    normal = centre * lax.rsqrt(spread + EPSILON)
    return (normal * (1.0 + scale) + shift).astype(BF16)


def rotated(u, cosine, lead, trail, half, axis):
    ahead = pltpu.roll(u, u.shape[axis] - half, axis)
    behind = pltpu.roll(u, half, axis)
    return u * cosine + ahead * lead + behind * trail


def matmul(a, b):
    return jnp.dot(a, b, preferred_element_type=F32)


def matmul_t(a, b):
    return lax.dot_general(a, b, (((1,), (1,)), ((), ())), preferred_element_type=F32)


def kernel(
    video, row_index, col_index, frame_index,
    shift_s, scale_s, gate_s, w_s, out_s, shift_t, scale_t, gate_t, w_t, out_t, table_s, table_t,
    out,
    video_held, w_s_held, out_s_held, w_t_held, out_t_held,
    pos, z_recv, pos_recv, frame_recv, frame_rows, time_rows, time_tables,
    x_send, x_recv, key_a, key_b, value_t, score_a, score_b, o_send, o_recv,
    t_send, t_recv, joined, total, r_send, r_recv,
    l_sem, z_ssem, z_rsem, p_ssem, p_rsem, f_ssem, f_rsem, x_ssem, x_rsem,
    o_ssem, o_rsem, t_ssem, t_rsem, r_ssem, r_rsem,
):
    tm = lax.axis_index("tm")
    space = lax.axis_index("space")
    zh = space // 4
    x = lax.rem(space, 4)
    zl = tm // NEAR
    yc = lax.rem(tm, NEAR)

    def remote(src, dst, ssem, rsem, **device):
        return pltpu.make_async_remote_copy(
            src_ref=src, dst_ref=dst, send_sem=ssem, recv_sem=rsem, device_id=device, device_id_type=MESH
        )

    barrier = pltpu.get_barrier_semaphore()
    for k in range(1, SPACE):
        other = {"space": lax.rem(space + k, SPACE)}
        pl.semaphore_signal(barrier, 1, device_id=other, device_id_type=MESH)
    for k in range(1, TM):
        other = {"tm": lax.rem(tm + k, TM)}
        pl.semaphore_signal(barrier, 1, device_id=other, device_id_type=MESH)

    def load(n, src, dst):
        copy = pltpu.make_async_copy(src, dst, l_sem.at[n])
        copy.start()
        return copy

    load_own = load(0, video.at[zh], video_held.at[zh])
    load_w_s = load(1, w_s, w_s_held)
    load_rest = [
        load(1 + k, video.at[lax.rem(zh + k, 4)], video_held.at[lax.rem(zh + k, 4)])
        for k in range(1, 4)
    ]
    load_out_s = load(5, out_s, out_s_held)
    load_w_t = [
        load(6 + n, w_t.at[pl.ds(here * INNER, INNER)], w_t_held.at[pl.ds(there * INNER, INNER)])
        for n, (here, there) in enumerate(((0, 0), (2, 1), (1, 2)))
    ]
    load_out_t = load(9, out_t, out_t_held.at[pl.ds(HALF, INNER)])

    row = lax.broadcasted_iota(jnp.int32, (8, PATCHES), 0)
    here = jnp.where(
        row == 0, row_index[...].reshape(1, PATCHES), col_index[...].reshape(1, PATCHES)
    )
    pos[...] = here.astype(F32)
    times = jnp.zeros((8, 128), jnp.int32)
    for f in range(FRAMES):
        times = jnp.where(row == f, frame_index[f], times)
    frame_recv[tm] = times.astype(F32)

    def z_copy(n):
        f = lax.rem(zh + (1, 3, 2)[n], 4)
        to = {"space": f * 4 + x}
        slot = (1, 0, 2)[n]
        return (
            remote(video.at[f], z_recv.at[slot], z_ssem.at[n], z_rsem.at[slot], **to),
            remote(pos, pos_recv.at[slot], p_ssem.at[n], p_rsem.at[slot], **to),
        )

    def frame_copy(k):
        d = lax.rem(tm + k, TM)
        return remote(
            frame_recv.at[tm], frame_recv.at[tm], f_ssem.at[d], f_rsem.at[tm], tm=d
        )

    pl.semaphore_wait(barrier, SPACE + TM - 2)
    for n in range(3):
        for copy in z_copy(n):
            copy.start()
    for k in range(1, TM):
        frame_copy(k).start()

    offsets = (0, 1, 3, 2)

    def block(c, column):
        return lax.rem(zh + offsets[c], 4) * 4 + column

    def x_copy(c, k):
        d = lax.rem(x + k, 4)
        mine = block(c, x)
        return remote(
            x_send.at[c, d], x_recv.at[mine], x_ssem.at[c, k], x_rsem.at[mine], space=zh * 4 + d
        )

    head_row = lax.broadcasted_iota(jnp.int32, (PATCHES, PAIR), 1) < HD

    def place(c, column, held):
        b = block(c, column)
        rows = pl.ds(pl.multiple_of(b * PATCHES, PATCHES), PATCHES)
        keys = jnp.transpose(held[PAIR : 2 * PAIR].astype(F32))
        key_a[rows] = jnp.where(head_row, keys, 0.0).astype(BF16)
        key_b[rows] = jnp.where(head_row, 0.0, keys).astype(BF16)
        value_t[0:PAIR, rows] = held[2 * PAIR :]

    def project(first, streams, places):
        y = matmul_t(
            w_s_held[...],
            jnp.concatenate(
                [modulated(s, scale_s[...].reshape(1, D), shift_s[...].reshape(1, D)) for s in streams],
                axis=0,
            ),
        )
        for e, at in enumerate(places):
            angles = table_s[:, 0:1] * at[0:1, :] + table_s[:, 1:2] * at[1:2, :]
            cosine = jnp.cos(angles)
            sine = jnp.sin(angles)
            lead = sine * table_s[:, 2:3]
            trail = sine * table_s[:, 3:4]
            part = y[:, e * PATCHES : (e + 1) * PATCHES]

            def turned(n):
                return rotated(part[n * HD : (n + 1) * HD], cosine, lead, trail, HD // 4, 0)

            for d in range(4):
                for n in range(2):
                    base = n * HEADS + 2 * d
                    x_send[first + e, d, n * PAIR : (n + 1) * PAIR] = jnp.concatenate(
                        [turned(base), turned(base + 1)], axis=0
                    ).astype(BF16)
                rows = slice(2 * INNER + d * PAIR, 2 * INNER + (d + 1) * PAIR)
                x_send[first + e, d, 2 * PAIR :] = part[rows].astype(BF16)
        for e in range(len(streams)):
            for k in (1, 3, 2):
                x_copy(first + e, k).start()
        for e in range(len(streams)):
            c = first + e
            place(c, x, x_send[c, x])
            x_recv[block(c, x), 0:PAIR] = x_send[c, x, 0:PAIR]

    def gather(c):
        for k in (1, 3, 2):
            column = lax.rem(x + k, 4)
            b = block(c, column)
            remote(x_send.at[c, k], x_recv.at[b], x_ssem.at[c, k], x_rsem.at[b], space=b).wait_recv()
            place(c, column, x_recv[b])

    def z_arrived(slot):
        f = lax.rem(zh + (1, 3, 2)[slot], 4)
        to = {"space": f * 4 + x}
        remote(video.at[f], z_recv.at[slot], z_ssem.at[slot], z_rsem.at[slot], **to).wait_recv()
        remote(pos, pos_recv.at[slot], p_ssem.at[slot], p_rsem.at[slot], **to).wait_recv()

    load_own.wait()
    load_w_s.wait()
    project(0, [video_held[zh]], [pos[...]])

    w_t_held[3 * INNER :] = jnp.zeros((HALF, D), BF16)
    out_t_held[0:HALF] = jnp.zeros((HALF, D), BF16)
    value_t[PAIR:] = jnp.where(
        lax.broadcasted_iota(jnp.int32, (16, KEYS), 0) == 0, 1.0, 0.0
    ).astype(BF16)

    def frame_arrived(k, carry):
        j = lax.rem(tm + k, TM)
        remote(frame_recv.at[tm], frame_recv.at[j], f_ssem.at[j], f_rsem.at[j], tm=j).wait_recv()
        return carry

    lax.fori_loop(1, TM, frame_arrived, 0)

    def side(s):
        return lax.rem(zl + s, 2) * NEAR

    for s in range(2):
        for n in range(NEAR):
            for i in range(2):
                at = s * 32 + i * 16 + n * 2
                frame_rows[at : at + 2] = frame_recv[side(s) + n, 2 * i : 2 * i + 2]
    angles = frame_rows[:, 0:1] * table_t[0:1, :]
    sine = jnp.sin(angles)
    time_rows[0] = jnp.cos(angles)
    time_rows[1] = sine * table_t[1:2, :]
    time_rows[2] = sine * table_t[2:3, :]

    def widen(g, carry):
        rows = pl.ds(pl.multiple_of(g * 8, 8), 8)
        for n in range(3):
            time_tables[n, rows] = jnp.broadcast_to(time_rows[n, pl.ds(g, 1)], (8, WIDE))
        return carry

    lax.fori_loop(0, 64, widen, 0)

    gather(0)
    z_arrived(0)
    z_arrived(1)
    project(1, [z_recv[0], z_recv[1]], [pos_recv[0], pos_recv[1]])
    gather(1)
    gather(2)
    z_arrived(2)
    project(3, [z_recv[2]], [pos_recv[2]])
    gather(3)

    def o_copy(j):
        return remote(o_send.at[j], o_recv.at[space], o_ssem.at[j], o_rsem.at[space], space=j)

    pair_row = lax.broadcasted_iota(jnp.int32, (PAIR, 2 * PATCHES), 0) < HD
    chunks = [slice(n * CHUNK, (n + 1) * CHUNK) for n in range(KEYS // CHUNK)]

    def attend(n, carry):
        b = lax.rem(space // 2 + 1 + n, SPACE // 2)
        queries = jnp.concatenate([x_recv[2 * b, 0:PAIR], x_recv[2 * b + 1, 0:PAIR]], axis=1)
        tops = []
        for keys, scores in ((key_a, score_a), (key_b, score_b)):
            top = None
            for rows in chunks:
                product = matmul(keys[rows], queries)
                scores[rows] = product
                high = jnp.max(product.reshape(CHUNK // 8, 8, 2 * PATCHES), axis=0)
                top = high if top is None else jnp.maximum(top, high)
            tops.append(jnp.max(top, axis=0, keepdims=True))
        mixed = []
        for scores, top in zip((score_a, score_b), tops):
            both = None
            for rows in chunks:
                weights = jnp.exp2((scores[rows] - top) * FACTOR).astype(BF16)
                product = matmul(value_t[:, rows], weights)
                both = product if both is None else both + product
            mixed.append(both[0:PAIR] / both[PAIR : PAIR + 1])
        result = jnp.where(pair_row, mixed[0], mixed[1]).astype(BF16)
        for e in range(2):
            j = 2 * b + e
            o_send[j] = result[:, e * PATCHES : (e + 1) * PATCHES]

            @pl.when(j != space)
            def _():
                o_copy(j).start()

        return carry

    lax.fori_loop(0, SPACE // 2, attend, 0)
    o_recv[space] = o_send[space]

    def t_copy(i, d):
        return remote(t_send.at[i, d], t_recv.at[i, tm], t_ssem.at[i, d], t_rsem.at[i, tm], tm=d)

    peers = [(s, r) for s in (1, 0) for r in range(NEAR) if (s, r) != (0, 0)]

    def peer(s, r):
        return side(s) + lax.rem(yc + r, NEAR)

    for copy in load_rest:
        copy.wait()
    load_out_s.wait()
    for i in range(2):

        def o_arrived(n, carry):
            j = i * 8 + n

            @pl.when(j != space)
            def _():
                remote(o_send.at[j], o_recv.at[j], o_ssem.at[j], o_rsem.at[j], space=j).wait_recv()

            return carry

        lax.fori_loop(0, 8, o_arrived, 0)
        mixed = []
        for e in range(2):
            f = 2 * i + e
            attended = o_recv[4 * f : 4 * f + 4].reshape(INNER, PATCHES)
            mixed.append(jnp.transpose(attended.astype(F32)).astype(BF16))
        branch = matmul(jnp.concatenate(mixed, axis=0), out_s_held[...])
        stream = video_held[2 * i : 2 * i + 2].reshape(2 * PATCHES, D).astype(F32)
        stream = (stream + gate_s[...].reshape(1, D) * branch).reshape(2, TM, 8, D)
        t_send[i] = jnp.stack([stream[0], stream[1]], axis=1).reshape(TM, 16, D).astype(BF16)
        for s, r in peers:
            t_copy(i, peer(s, r)).start()
        t_recv[i, tm] = t_send[i, tm]

    for copy in load_w_t:
        copy.wait()
    for s in range(2):
        for r in range(NEAR):
            if (s, r) != (0, 0):
                j = peer(s, r)
                for i in range(2):
                    remote(
                        t_send.at[i, j], t_recv.at[i, j], t_ssem.at[i, j], t_rsem.at[i, j], tm=j
                    ).wait_recv()
        rows = t_recv[:, pl.ds(side(s), NEAR)].reshape(2 * PATCHES, D)
        y = matmul_t(
            modulated(rows, scale_t[...].reshape(1, D), shift_t[...].reshape(1, D)), w_t_held[...]
        )
        angle = [time_tables[n, s * 256 : (s + 1) * 256] for n in range(3)]
        joined[s, :, 0:WIDE] = rotated(y[:, 0:WIDE], *angle, HD // 2, 1).astype(BF16)
        joined[s, :, WIDE : 2 * INNER] = y[:, WIDE : 2 * INNER].astype(BF16)
        joined[s, :, 2 * INNER :] = rotated(y[:, 2 * INNER :], *angle, HD // 2, 1).astype(BF16)

    def r_copy(s, r):
        d = peer(s, r)
        n = lax.rem(yc + r, NEAR)
        return remote(r_send.at[s, :, n], r_recv.at[:, tm], r_ssem.at[d], r_rsem.at[tm], tm=d)

    def window(start, count):
        low = start // 128 * 128
        high = (start + HD + 127) // 128 * 128
        lane = lax.broadcasted_iota(jnp.int32, (count, high - low), 1)
        return low, high, (lane >= start - low) & (lane < start - low + HD)

    same = lax.rem(lax.broadcasted_iota(jnp.int32, (256, TOKENS), 0), 8) == lax.rem(
        lax.broadcasted_iota(jnp.int32, (256, TOKENS), 1), 8
    )
    for s in (1, 0):
        total[...] = jnp.zeros((256, WIDE), F32)
        for h in range(HEADS):
            low, high, inside = window(h * HD, TOKENS)
            keys = joined[:, :, 2 * INNER + low : 2 * INNER + high].reshape(TOKENS, high - low)
            keys = jnp.where(inside, keys, jnp.zeros_like(keys))
            scores = jnp.where(same, matmul_t(joined[s, :, low:high], keys), -1e30)
            top = jnp.max(scores, axis=1, keepdims=True)
            weights = jnp.exp2((scores - top) * FACTOR)
            sums = jnp.sum(weights, axis=1, keepdims=True)
            low, high, inside = window(HALF + h * HD, 256)
            base = INNER - HALF
            values = joined[:, :, base + low : base + high].reshape(TOKENS, high - low)
            part = matmul(weights.astype(BF16), values)
            total[:, low:high] += jnp.where(inside, part / sums, 0.0)
        r_send[s] = total[...].astype(BF16).reshape(2, NEAR, 16, WIDE)
        for r in range(NEAR):
            if (s, r) != (0, 0):
                r_copy(s, r).start()
    r_recv[:, tm] = r_send[0, :, yc]

    def r_arrived(k, carry):
        j = lax.rem(tm + k, TM)
        remote(r_send.at[0, :, 0], r_recv.at[:, j], r_ssem.at[j], r_rsem.at[j], tm=j).wait_recv()
        return carry

    lax.fori_loop(1, TM, r_arrived, 0)
    load_out_t.wait()
    for i in range(2):
        branch = matmul(r_recv[i].reshape(2 * PATCHES, WIDE), out_t_held[...])
        stream = t_send[i].reshape(2 * PATCHES, D).astype(F32)
        stream = (stream + gate_t[...].reshape(1, D) * branch).reshape(TM, 2, 8, D)
        for e in range(2):
            out[2 * i + e] = stream[:, e].reshape(PATCHES, D).astype(BF16)

    for n in range(3):
        for copy in z_copy(n):
            copy.wait_send()
        for c in range(4):
            x_copy(c, n + 1).wait_send()

    def o_sent(k, carry):
        o_copy(lax.rem(space + k, SPACE)).wait_send()
        frame_copy(k).wait_send()
        return carry

    lax.fori_loop(1, SPACE, o_sent, 0)
    for s, r in peers:
        for i in range(2):
            t_copy(i, peer(s, r)).wait_send()
        r_copy(s, r).wait_send()


def block(*arrays):
    vmem = pl.BlockSpec(memory_space=pltpu.VMEM)
    smem = pl.BlockSpec(memory_space=pltpu.SMEM)
    hbm = pl.BlockSpec(memory_space=pl.ANY)
    dma = pltpu.SemaphoreType.DMA
    specs = [hbm, vmem, vmem, smem] + [vmem, vmem, vmem, hbm, hbm] * 2 + [vmem, vmem]
    held = [
        ((FRAMES, PATCHES, D), BF16),
        ((3 * INNER, D), BF16),
        ((INNER, D), BF16),
        ((LANES, D), BF16),
        ((WIDE, D), BF16),
        ((8, PATCHES), F32),
        ((3, PATCHES, D), BF16),
        ((3, 8, PATCHES), F32),
        ((TM, 8, 128), F32),
        ((64, 128), F32),
        ((3, 64, WIDE), F32),
        ((3, TOKENS, WIDE), F32),
        ((4, 4, 3 * PAIR, PATCHES), BF16),
        ((SPACE, 3 * PAIR, PATCHES), BF16),
        ((KEYS, PAIR), BF16),
        ((KEYS, PAIR), BF16),
        ((PAIR + 16, KEYS), BF16),
        ((KEYS, 2 * PATCHES), F32),
        ((KEYS, 2 * PATCHES), F32),
        ((SPACE, PAIR, PATCHES), BF16),
        ((SPACE, PAIR, PATCHES), BF16),
        ((2, TM, 16, D), BF16),
        ((2, TM, 16, D), BF16),
        ((2, 256, LANES), BF16),
        ((256, WIDE), F32),
        ((2, 2, NEAR, 16, WIDE), BF16),
        ((2, TM, 16, WIDE), BF16),
    ]
    sems = [(10,), (3,), (3,), (3,), (3,), (TM,), (TM,), (4, 4), (SPACE,)]
    sems += [(SPACE,), (SPACE,), (2, TM), (2, TM), (TM,), (TM,)]
    return pl.pallas_call(
        kernel,
        out_shape=jax.ShapeDtypeStruct((FRAMES, PATCHES, D), BF16),
        in_specs=specs,
        out_specs=vmem,
        scratch_shapes=[pltpu.VMEM(*h) for h in held] + [dma(s) for s in sems],
        compiler_params=pltpu.CompilerParams(
            collective_id=1, has_side_effects=True, vmem_limit_bytes=56 * 2**20
        ),
        name="space_time_block",
    )(*arrays)


def space_table():
    f = 10000.0 ** (-np.arange(HD // 4, dtype=np.float32) / (HD // 4))
    zero = np.zeros_like(f)
    one = np.ones_like(f)
    table = np.zeros((HD, 8), np.float32)
    table[:, 0] = np.concatenate([f, f, zero, zero])
    table[:, 1] = np.concatenate([zero, zero, f, f])
    table[:, 2] = np.concatenate([-one, zero, -one, zero])
    table[:, 3] = np.concatenate([zero, one, zero, one])
    return jnp.asarray(table)


def time_table():
    f = 10000.0 ** (-np.arange(HD // 2, dtype=np.float32) / (HD // 2))
    zero = np.zeros_like(f)
    one = np.ones_like(f)
    table = np.zeros((8, WIDE), np.float32)
    table[0, :INNER] = np.tile(np.concatenate([f, f]), HEADS)
    table[1, :INNER] = np.tile(np.concatenate([-one, zero]), HEADS)
    table[2, :INNER] = np.tile(np.concatenate([zero, one]), HEADS)
    return jnp.asarray(table)


def body(*arrays):
    arrays = list(arrays)
    for n in (7, 12):
        arrays[n] = arrays[n].T
    return block(*arrays, space_table(), time_table())


def solution(mesh):
    return jax.shard_map(
        body,
        mesh=mesh,
        in_specs=(P("tm", "space", None), P("space"), P("space"), P("tm")) + (P(),) * 10,
        out_specs=P("tm", "space", None),
        check_vma=False,
    )
```

```python
import math

import jax
import jax.numpy as jnp
import numpy as np
from jax import lax
from jax.experimental import pallas as pl
from jax.experimental.pallas import tpu as pltpu
from jax.sharding import PartitionSpec as P

HEADS = 8
HD = 72
D = 1152
INNER = HEADS * HD
FRAMES = 4
PATCHES = 128
SPACE = 16
PAIR = 2 * HD
TM = 16
NEAR = 8
TOKENS = FRAMES * PATCHES
KEYS = SPACE * PATCHES
HALF = INNER % 128
WIDE = INNER + HALF
LANES = 3 * INNER + HALF
FACTOR = math.log2(math.e) / math.sqrt(HD)
CHUNK = 512
EPSILON = 1e-06
MESH = pl.DeviceIdType.MESH
BF16 = jnp.bfloat16
F32 = jnp.float32


def modulated(stream, scale, shift):
    stream = stream.astype(F32)
    centre = stream - jnp.mean(stream, axis=-1, keepdims=True)
    spread = jnp.mean(centre * centre, axis=-1, keepdims=True)
    normal = centre * lax.rsqrt(spread + EPSILON)
    return (normal * (1.0 + scale) + shift).astype(BF16)


def rotated(u, cosine, lead, trail, half, axis):
    ahead = pltpu.roll(u, u.shape[axis] - half, axis)
    behind = pltpu.roll(u, half, axis)
    return u * cosine + ahead * lead + behind * trail


def matmul(a, b):
    return jnp.dot(a, b, preferred_element_type=F32)


def matmul_t(a, b):
    return lax.dot_general(a, b, (((1,), (1,)), ((), ())), preferred_element_type=F32)


def kernel(
    video, row_index, col_index, frame_index,
    shift_s, scale_s, gate_s, w_s, out_s, shift_t, scale_t, gate_t, w_t, out_t, table_s, table_t,
    out,
    video_held, w_s_held, out_s_held, w_t_held, out_t_held,
    pos, z_recv, pos_recv, frame_recv, frame_rows, time_rows, time_tables,
    x_send, x_recv, key_a, key_b, value_t, score_a, score_b, o_send, o_recv,
    t_send, t_recv, joined, total, r_send, r_recv,
    l_sem, z_ssem, z_rsem, p_ssem, p_rsem, f_ssem, f_rsem, x_ssem, x_rsem,
    o_ssem, o_rsem, t_ssem, t_rsem, r_ssem, r_rsem,
):
    tm = lax.axis_index("tm")
    space = lax.axis_index("space")
    zh = space // 4
    x = lax.rem(space, 4)
    zl = tm // NEAR
    yc = lax.rem(tm, NEAR)

    def remote(src, dst, ssem, rsem, **device):
        return pltpu.make_async_remote_copy(
            src_ref=src, dst_ref=dst, send_sem=ssem, recv_sem=rsem, device_id=device, device_id_type=MESH
        )

    barrier = pltpu.get_barrier_semaphore()
    for k in range(1, SPACE):
        other = {"space": lax.rem(space + k, SPACE)}
        pl.semaphore_signal(barrier, 1, device_id=other, device_id_type=MESH)
    for k in range(1, TM):
        other = {"tm": lax.rem(tm + k, TM)}
        pl.semaphore_signal(barrier, 1, device_id=other, device_id_type=MESH)

    def load(n, src, dst):
        copy = pltpu.make_async_copy(src, dst, l_sem.at[n])
        copy.start()
        return copy

    load_own = load(0, video.at[zh], video_held.at[zh])
    load_w_s = load(1, w_s, w_s_held)
    load_rest = [
        load(1 + k, video.at[lax.rem(zh + k, 4)], video_held.at[lax.rem(zh + k, 4)])
        for k in range(1, 4)
    ]
    load_out_s = load(5, out_s, out_s_held)
    load_w_t = [
        load(6 + n, w_t.at[pl.ds(here * INNER, INNER)], w_t_held.at[pl.ds(there * INNER, INNER)])
        for n, (here, there) in enumerate(((0, 0), (2, 1), (1, 2)))
    ]
    load_out_t = load(9, out_t, out_t_held.at[pl.ds(HALF, INNER)])

    row = lax.broadcasted_iota(jnp.int32, (8, PATCHES), 0)
    here = jnp.where(
        row == 0, row_index[...].reshape(1, PATCHES), col_index[...].reshape(1, PATCHES)
    )
    pos[...] = here.astype(F32)
    times = jnp.zeros((8, 128), jnp.int32)
    for f in range(FRAMES):
        times = jnp.where(row == f, frame_index[f], times)
    frame_recv[tm] = times.astype(F32)

    def z_copy(n):
        f = lax.rem(zh + (1, 3, 2)[n], 4)
        to = {"space": f * 4 + x}
        slot = (1, 0, 2)[n]
        return (
            remote(video.at[f], z_recv.at[slot], z_ssem.at[n], z_rsem.at[slot], **to),
            remote(pos, pos_recv.at[slot], p_ssem.at[n], p_rsem.at[slot], **to),
        )

    def frame_copy(k):
        d = lax.rem(tm + k, TM)
        return remote(
            frame_recv.at[tm], frame_recv.at[tm], f_ssem.at[d], f_rsem.at[tm], tm=d
        )

    pl.semaphore_wait(barrier, SPACE + TM - 2)
    for n in range(2):
        z_copy(n)[0].start()
    for n in range(3):
        z_copy(n)[1].start()
    for k in range(1, TM):
        frame_copy(k).start()

    def x_copy(c, k):
        d = lax.rem(x + k, 4)
        return remote(
            x_send.at[c, d], x_recv.at[c, x], x_ssem.at[c, k], x_rsem.at[c, x], space=zh * 4 + d
        )

    head_row = lax.broadcasted_iota(jnp.int32, (PATCHES, PAIR), 1) < HD

    def place(c, column, held):
        rows = pl.ds(pl.multiple_of((c * 4 + column) * PATCHES, PATCHES), PATCHES)
        keys = jnp.transpose(held[PAIR : 2 * PAIR].astype(F32))
        key_a[rows] = jnp.where(head_row, keys, 0.0).astype(BF16)
        key_b[rows] = jnp.where(head_row, 0.0, keys).astype(BF16)
        value_t[0:PAIR, rows] = held[2 * PAIR :]

    def project(first, streams, places):
        y = matmul_t(
            w_s_held[...],
            jnp.concatenate(
                [modulated(s, scale_s[...].reshape(1, D), shift_s[...].reshape(1, D)) for s in streams],
                axis=0,
            ),
        )
        for e, at in enumerate(places):
            angles = table_s[:, 0:1] * at[0:1, :] + table_s[:, 1:2] * at[1:2, :]
            cosine = jnp.cos(angles)
            sine = jnp.sin(angles)
            lead = sine * table_s[:, 2:3]
            trail = sine * table_s[:, 3:4]
            part = y[:, e * PATCHES : (e + 1) * PATCHES]

            def turned(n):
                return rotated(part[n * HD : (n + 1) * HD], cosine, lead, trail, HD // 4, 0)

            for d in range(4):
                for n in range(2):
                    base = n * HEADS + 2 * d
                    x_send[first + e, d, n * PAIR : (n + 1) * PAIR] = jnp.concatenate(
                        [turned(base), turned(base + 1)], axis=0
                    ).astype(BF16)
                rows = slice(2 * INNER + d * PAIR, 2 * INNER + (d + 1) * PAIR)
                x_send[first + e, d, 2 * PAIR :] = part[rows].astype(BF16)
        for e in range(len(streams)):
            for k in (1, 3, 2):
                x_copy(first + e, k).start()
        for e in range(len(streams)):
            c = first + e
            place(c, x, x_send[c, x])
            x_recv[c, x, 0:PAIR] = x_send[c, x, 0:PAIR]

    def gather(c):
        for k in (1, 3, 2):
            column = lax.rem(x + k, 4)
            remote(
                x_send.at[c, k], x_recv.at[c, column], x_ssem.at[c, k], x_rsem.at[c, column],
                space=zh * 4 + column,
            ).wait_recv()
            place(c, column, x_recv[c, column])

    def z_arrived(slot):
        f = lax.rem(zh + (1, 3, 2)[slot], 4)
        to = {"space": f * 4 + x}
        remote(video.at[f], z_recv.at[slot], z_ssem.at[slot], z_rsem.at[slot], **to).wait_recv()
        remote(pos, pos_recv.at[slot], p_ssem.at[slot], p_rsem.at[slot], **to).wait_recv()

    load_own.wait()
    load_w_s.wait()
    project(0, [video_held[zh]], [pos[...]])

    w_t_held[3 * INNER :] = jnp.zeros((HALF, D), BF16)
    out_t_held[0:HALF] = jnp.zeros((HALF, D), BF16)
    value_t[PAIR:] = jnp.where(
        lax.broadcasted_iota(jnp.int32, (16, KEYS), 0) == 0, 1.0, 0.0
    ).astype(BF16)

    def frame_arrived(k, carry):
        j = lax.rem(tm + k, TM)
        remote(frame_recv.at[tm], frame_recv.at[j], f_ssem.at[j], f_rsem.at[j], tm=j).wait_recv()
        return carry

    lax.fori_loop(1, TM, frame_arrived, 0)

    def side(s):
        return lax.rem(zl + s, 2) * NEAR

    for s in range(2):
        for n in range(NEAR):
            for i in range(2):
                at = s * 32 + i * 16 + n * 2
                frame_rows[at : at + 2] = frame_recv[side(s) + n, 2 * i : 2 * i + 2]
    angles = frame_rows[:, 0:1] * table_t[0:1, :]
    sine = jnp.sin(angles)
    time_rows[0] = jnp.cos(angles)
    time_rows[1] = sine * table_t[1:2, :]
    time_rows[2] = sine * table_t[2:3, :]

    def widen(g, carry):
        rows = pl.ds(pl.multiple_of(g * 8, 8), 8)
        for n in range(3):
            time_tables[n, rows] = jnp.broadcast_to(time_rows[n, pl.ds(g, 1)], (8, WIDE))
        return carry

    lax.fori_loop(0, 64, widen, 0)

    for n in range(2):
        z_copy(n)[0].wait_send()
    z_copy(2)[0].start()
    gather(0)
    z_arrived(0)
    z_arrived(1)
    project(1, [z_recv[0], z_recv[1]], [pos_recv[0], pos_recv[1]])
    gather(1)
    gather(2)
    z_arrived(2)
    project(3, [z_recv[2]], [pos_recv[2]])
    gather(3)

    def o_copy(j):
        return remote(o_send.at[j], o_recv.at[space], o_ssem.at[j], o_rsem.at[space], space=j)

    pair_row = lax.broadcasted_iota(jnp.int32, (PAIR, 2 * PATCHES), 0) < HD
    chunks = [slice(n * CHUNK, (n + 1) * CHUNK) for n in range(KEYS // CHUNK)]

    def attend(n, carry):
        c = 3 - n // 2
        off = jnp.where(c == 3, 2, jnp.where(c == 2, 3, c))
        first = lax.rem(n + x // 2 + 1, 2) * 2
        queries = jnp.concatenate([x_recv[c, first, 0:PAIR], x_recv[c, first + 1, 0:PAIR]], axis=1)
        tops = []
        for keys, scores in ((key_a, score_a), (key_b, score_b)):
            top = None
            for rows in chunks:
                product = matmul(keys[rows], queries)
                scores[rows] = product
                high = jnp.max(product.reshape(CHUNK // 8, 8, 2 * PATCHES), axis=0)
                top = high if top is None else jnp.maximum(top, high)
            tops.append(jnp.max(top, axis=0, keepdims=True))
        mixed = []
        for scores, top in zip((score_a, score_b), tops):
            both = None
            for rows in chunks:
                weights = jnp.exp2((scores[rows] - top) * FACTOR).astype(BF16)
                product = matmul(value_t[:, rows], weights)
                both = product if both is None else both + product
            mixed.append(both[0:PAIR] / both[PAIR : PAIR + 1])
        result = jnp.where(pair_row, mixed[0], mixed[1]).astype(BF16)
        for e in range(2):
            j = lax.rem(zh + off, 4) * 4 + first + e
            o_send[j] = result[:, e * PATCHES : (e + 1) * PATCHES]

            @pl.when(j != space)
            def _():
                o_copy(j).start()

        return carry

    lax.fori_loop(0, SPACE // 2, attend, 0)
    o_recv[space] = o_send[space]

    def t_copy(i, d):
        return remote(t_send.at[i, d], t_recv.at[i, tm], t_ssem.at[i, d], t_rsem.at[i, tm], tm=d)

    peers = [(s, r) for s in (1, 0) for r in range(NEAR) if (s, r) != (0, 0)]

    def peer(s, r):
        return side(s) + lax.rem(yc + r, NEAR)

    for copy in load_rest:
        copy.wait()
    load_out_s.wait()
    for i in range(2):

        def o_arrived(n, carry):
            j = i * 8 + n

            @pl.when(j != space)
            def _():
                remote(o_send.at[j], o_recv.at[j], o_ssem.at[j], o_rsem.at[j], space=j).wait_recv()

            return carry

        lax.fori_loop(0, 8, o_arrived, 0)
        mixed = []
        for e in range(2):
            f = 2 * i + e
            attended = o_recv[4 * f : 4 * f + 4].reshape(INNER, PATCHES)
            mixed.append(jnp.transpose(attended.astype(F32)).astype(BF16))
        branch = matmul(jnp.concatenate(mixed, axis=0), out_s_held[...])
        stream = video_held[2 * i : 2 * i + 2].reshape(2 * PATCHES, D).astype(F32)
        stream = (stream + gate_s[...].reshape(1, D) * branch).reshape(2, TM, 8, D)
        t_send[i] = jnp.stack([stream[0], stream[1]], axis=1).reshape(TM, 16, D).astype(BF16)
        for s, r in peers:
            t_copy(i, peer(s, r)).start()
        t_recv[i, tm] = t_send[i, tm]

    for copy in load_w_t:
        copy.wait()
    for s in range(2):
        for r in range(NEAR):
            if (s, r) != (0, 0):
                j = peer(s, r)
                for i in range(2):
                    remote(
                        t_send.at[i, j], t_recv.at[i, j], t_ssem.at[i, j], t_rsem.at[i, j], tm=j
                    ).wait_recv()
        rows = t_recv[:, pl.ds(side(s), NEAR)].reshape(2 * PATCHES, D)
        y = matmul_t(
            modulated(rows, scale_t[...].reshape(1, D), shift_t[...].reshape(1, D)), w_t_held[...]
        )
        angle = [time_tables[n, s * 256 : (s + 1) * 256] for n in range(3)]
        joined[s, :, 0:WIDE] = rotated(y[:, 0:WIDE], *angle, HD // 2, 1).astype(BF16)
        joined[s, :, WIDE : 2 * INNER] = y[:, WIDE : 2 * INNER].astype(BF16)
        joined[s, :, 2 * INNER :] = rotated(y[:, 2 * INNER :], *angle, HD // 2, 1).astype(BF16)

    def r_copy(s, r):
        d = peer(s, r)
        n = lax.rem(yc + r, NEAR)
        return remote(r_send.at[s, :, n], r_recv.at[:, tm], r_ssem.at[d], r_rsem.at[tm], tm=d)

    def window(start, count):
        low = start // 128 * 128
        high = (start + HD + 127) // 128 * 128
        lane = lax.broadcasted_iota(jnp.int32, (count, high - low), 1)
        return low, high, (lane >= start - low) & (lane < start - low + HD)

    same = lax.rem(lax.broadcasted_iota(jnp.int32, (256, TOKENS), 0), 8) == lax.rem(
        lax.broadcasted_iota(jnp.int32, (256, TOKENS), 1), 8
    )
    for s in (1, 0):
        total[...] = jnp.zeros((256, WIDE), F32)
        for h in range(HEADS):
            low, high, inside = window(h * HD, TOKENS)
            keys = joined[:, :, 2 * INNER + low : 2 * INNER + high].reshape(TOKENS, high - low)
            keys = jnp.where(inside, keys, jnp.zeros_like(keys))
            scores = jnp.where(same, matmul_t(joined[s, :, low:high], keys), -1e30)
            top = jnp.max(scores, axis=1, keepdims=True)
            weights = jnp.exp2((scores - top) * FACTOR)
            sums = jnp.sum(weights, axis=1, keepdims=True)
            low, high, inside = window(HALF + h * HD, 256)
            base = INNER - HALF
            values = joined[:, :, base + low : base + high].reshape(TOKENS, high - low)
            part = matmul(weights.astype(BF16), values)
            total[:, low:high] += jnp.where(inside, part / sums, 0.0)
        r_send[s] = total[...].astype(BF16).reshape(2, NEAR, 16, WIDE)
        for r in range(NEAR):
            if (s, r) != (0, 0):
                r_copy(s, r).start()
    r_recv[:, tm] = r_send[0, :, yc]

    def r_arrived(k, carry):
        j = lax.rem(tm + k, TM)
        remote(r_send.at[0, :, 0], r_recv.at[:, j], r_ssem.at[j], r_rsem.at[j], tm=j).wait_recv()
        return carry

    lax.fori_loop(1, TM, r_arrived, 0)
    load_out_t.wait()
    for i in range(2):
        branch = matmul(r_recv[i].reshape(2 * PATCHES, WIDE), out_t_held[...])
        stream = t_send[i].reshape(2 * PATCHES, D).astype(F32)
        stream = (stream + gate_t[...].reshape(1, D) * branch).reshape(TM, 2, 8, D)
        for e in range(2):
            out[2 * i + e] = stream[:, e].reshape(PATCHES, D).astype(BF16)

    z_copy(2)[0].wait_send()
    for n in range(3):
        z_copy(n)[1].wait_send()
        for c in range(4):
            x_copy(c, n + 1).wait_send()

    def o_sent(k, carry):
        o_copy(lax.rem(space + k, SPACE)).wait_send()
        frame_copy(k).wait_send()
        return carry

    lax.fori_loop(1, SPACE, o_sent, 0)
    for s, r in peers:
        for i in range(2):
            t_copy(i, peer(s, r)).wait_send()
        r_copy(s, r).wait_send()


def block(*arrays):
    vmem = pl.BlockSpec(memory_space=pltpu.VMEM)
    smem = pl.BlockSpec(memory_space=pltpu.SMEM)
    hbm = pl.BlockSpec(memory_space=pl.ANY)
    dma = pltpu.SemaphoreType.DMA
    specs = [hbm, vmem, vmem, smem] + [vmem, vmem, vmem, hbm, hbm] * 2 + [vmem, vmem]
    held = [
        ((FRAMES, PATCHES, D), BF16),
        ((3 * INNER, D), BF16),
        ((INNER, D), BF16),
        ((LANES, D), BF16),
        ((WIDE, D), BF16),
        ((8, PATCHES), F32),
        ((3, PATCHES, D), BF16),
        ((3, 8, PATCHES), F32),
        ((TM, 8, 128), F32),
        ((64, 128), F32),
        ((3, 64, WIDE), F32),
        ((3, TOKENS, WIDE), F32),
        ((4, 4, 3 * PAIR, PATCHES), BF16),
        ((4, 4, 3 * PAIR, PATCHES), BF16),
        ((KEYS, PAIR), BF16),
        ((KEYS, PAIR), BF16),
        ((PAIR + 16, KEYS), BF16),
        ((KEYS, 2 * PATCHES), F32),
        ((KEYS, 2 * PATCHES), F32),
        ((SPACE, PAIR, PATCHES), BF16),
        ((SPACE, PAIR, PATCHES), BF16),
        ((2, TM, 16, D), BF16),
        ((2, TM, 16, D), BF16),
        ((2, 256, LANES), BF16),
        ((256, WIDE), F32),
        ((2, 2, NEAR, 16, WIDE), BF16),
        ((2, TM, 16, WIDE), BF16),
    ]
    sems = [(10,), (3,), (3,), (3,), (3,), (TM,), (TM,), (4, 4), (4, 4)]
    sems += [(SPACE,), (SPACE,), (2, TM), (2, TM), (TM,), (TM,)]
    return pl.pallas_call(
        kernel,
        out_shape=jax.ShapeDtypeStruct((FRAMES, PATCHES, D), BF16),
        in_specs=specs,
        out_specs=vmem,
        scratch_shapes=[pltpu.VMEM(*h) for h in held] + [dma(s) for s in sems],
        compiler_params=pltpu.CompilerParams(
            collective_id=1, has_side_effects=True, vmem_limit_bytes=56 * 2**20
        ),
        name="space_time_block",
    )(*arrays)


def space_table():
    f = 10000.0 ** (-np.arange(HD // 4, dtype=np.float32) / (HD // 4))
    zero = np.zeros_like(f)
    one = np.ones_like(f)
    table = np.zeros((HD, 8), np.float32)
    table[:, 0] = np.concatenate([f, f, zero, zero])
    table[:, 1] = np.concatenate([zero, zero, f, f])
    table[:, 2] = np.concatenate([-one, zero, -one, zero])
    table[:, 3] = np.concatenate([zero, one, zero, one])
    return jnp.asarray(table)


def time_table():
    f = 10000.0 ** (-np.arange(HD // 2, dtype=np.float32) / (HD // 2))
    zero = np.zeros_like(f)
    one = np.ones_like(f)
    table = np.zeros((8, WIDE), np.float32)
    table[0, :INNER] = np.tile(np.concatenate([f, f]), HEADS)
    table[1, :INNER] = np.tile(np.concatenate([-one, zero]), HEADS)
    table[2, :INNER] = np.tile(np.concatenate([zero, one]), HEADS)
    return jnp.asarray(table)


def body(*arrays):
    arrays = list(arrays)
    for n in (7, 12):
        arrays[n] = arrays[n].T
    return block(*arrays, space_table(), time_table())


def solution(mesh):
    return jax.shard_map(
        body,
        mesh=mesh,
        in_specs=(P("tm", "space", None), P("space"), P("space"), P("tm")) + (P(),) * 10,
        out_specs=P("tm", "space", None),
        check_vma=False,
    )
```

```python
import math

import jax
import jax.numpy as jnp
import numpy as np
from jax import lax
from jax.experimental import pallas as pl
from jax.experimental.pallas import tpu as pltpu
from jax.sharding import PartitionSpec as P

HEADS = 8
HD = 72
D = 1152
INNER = HEADS * HD
FRAMES = 4
PATCHES = 128
SPACE = 16
PAIR = 2 * HD
TM = 16
NEAR = 8
TOKENS = FRAMES * PATCHES
KEYS = SPACE * PATCHES
HALF = INNER % 128
WIDE = INNER + HALF
LANES = 3 * INNER + HALF
FACTOR = math.log2(math.e) / math.sqrt(HD)
CHUNK = 512
EARLY = 2
EPSILON = 1e-06
MESH = pl.DeviceIdType.MESH
BF16 = jnp.bfloat16
F32 = jnp.float32


def modulated(stream, scale, shift):
    stream = stream.astype(F32)
    centre = stream - jnp.mean(stream, axis=-1, keepdims=True)
    spread = jnp.mean(centre * centre, axis=-1, keepdims=True)
    normal = centre * lax.rsqrt(spread + EPSILON)
    return (normal * (1.0 + scale) + shift).astype(BF16)


def rotated(u, cosine, lead, trail, half, axis):
    ahead = pltpu.roll(u, u.shape[axis] - half, axis)
    behind = pltpu.roll(u, half, axis)
    return u * cosine + ahead * lead + behind * trail


def matmul(a, b):
    return jnp.dot(a, b, preferred_element_type=F32)


def matmul_t(a, b):
    return lax.dot_general(a, b, (((1,), (1,)), ((), ())), preferred_element_type=F32)


def kernel(
    video, row_index, col_index, frame_index,
    shift_s, scale_s, gate_s, w_s, out_s, shift_t, scale_t, gate_t, w_t, out_t, table_s, table_t,
    out,
    video_held, w_s_held, out_s_held, w_t_held, out_t_held,
    pos, z_recv, pos_recv, frame_recv, frame_rows, time_rows, time_tables,
    x_send, x_recv, key_a, key_b, value_t, score_a, score_b, early_top, early_sum, o_send, o_recv,
    t_send, t_recv, joined, total, r_send, r_recv,
    l_sem, z_ssem, z_rsem, p_ssem, p_rsem, f_ssem, f_rsem, x_ssem, x_rsem,
    o_ssem, o_rsem, t_ssem, t_rsem, r_ssem, r_rsem,
):
    tm = lax.axis_index("tm")
    space = lax.axis_index("space")
    zh = space // 4
    x = lax.rem(space, 4)
    zl = tm // NEAR
    yc = lax.rem(tm, NEAR)

    def remote(src, dst, ssem, rsem, **device):
        return pltpu.make_async_remote_copy(
            src_ref=src, dst_ref=dst, send_sem=ssem, recv_sem=rsem, device_id=device, device_id_type=MESH
        )

    barrier = pltpu.get_barrier_semaphore()
    for k in range(1, SPACE):
        other = {"space": lax.rem(space + k, SPACE)}
        pl.semaphore_signal(barrier, 1, device_id=other, device_id_type=MESH)
    for k in range(1, TM):
        other = {"tm": lax.rem(tm + k, TM)}
        pl.semaphore_signal(barrier, 1, device_id=other, device_id_type=MESH)

    def load(n, src, dst):
        copy = pltpu.make_async_copy(src, dst, l_sem.at[n])
        copy.start()
        return copy

    load_own = load(0, video.at[zh], video_held.at[zh])
    load_w_s = load(1, w_s, w_s_held)
    load_rest = [
        load(1 + k, video.at[lax.rem(zh + k, 4)], video_held.at[lax.rem(zh + k, 4)])
        for k in range(1, 4)
    ]
    load_out_s = load(5, out_s, out_s_held)
    load_w_t = [
        load(6 + n, w_t.at[pl.ds(here * INNER, INNER)], w_t_held.at[pl.ds(there * INNER, INNER)])
        for n, (here, there) in enumerate(((0, 0), (2, 1), (1, 2)))
    ]
    load_out_t = load(9, out_t, out_t_held.at[pl.ds(HALF, INNER)])

    row = lax.broadcasted_iota(jnp.int32, (8, PATCHES), 0)
    here = jnp.where(
        row == 0, row_index[...].reshape(1, PATCHES), col_index[...].reshape(1, PATCHES)
    )
    pos[...] = here.astype(F32)
    times = jnp.zeros((8, 128), jnp.int32)
    for f in range(FRAMES):
        times = jnp.where(row == f, frame_index[f], times)
    frame_recv[tm] = times.astype(F32)

    def z_copy(n):
        f = lax.rem(zh + (1, 3, 2)[n], 4)
        to = {"space": f * 4 + x}
        slot = (1, 0, 2)[n]
        return (
            remote(video.at[f], z_recv.at[slot], z_ssem.at[n], z_rsem.at[slot], **to),
            remote(pos, pos_recv.at[slot], p_ssem.at[n], p_rsem.at[slot], **to),
        )

    def frame_copy(k):
        d = lax.rem(tm + k, TM)
        return remote(
            frame_recv.at[tm], frame_recv.at[tm], f_ssem.at[d], f_rsem.at[tm], tm=d
        )

    pl.semaphore_wait(barrier, SPACE + TM - 2)
    for n in range(2):
        z_copy(n)[0].start()
    for n in range(3):
        z_copy(n)[1].start()
    for k in range(1, TM):
        frame_copy(k).start()

    def parts(c):
        return [(c, slice(0, 3 * PAIR))] if c < 3 else [(3, slice(PAIR, 3 * PAIR)), (4, slice(0, PAIR))]

    def x_copies(c, k):
        d = lax.rem(x + k, 4)
        return [
            remote(
                x_send.at[c, d, rows], x_recv.at[c, x, rows], x_ssem.at[n, k], x_rsem.at[n, x],
                space=zh * 4 + d,
            )
            for n, rows in parts(c)
        ]

    def x_arrived(c, column, part):
        n, rows = parts(c)[part]
        remote(
            x_send.at[c, column, rows], x_recv.at[c, column, rows], x_ssem.at[n, column],
            x_rsem.at[n, column], space=zh * 4 + column,
        ).wait_recv()

    head_row = lax.broadcasted_iota(jnp.int32, (PATCHES, PAIR), 1) < HD

    def place(c, column, held):
        rows = pl.ds(pl.multiple_of((c * 4 + column) * PATCHES, PATCHES), PATCHES)
        keys = jnp.transpose(held[0:PAIR].astype(F32))
        key_a[rows] = jnp.where(head_row, keys, 0.0).astype(BF16)
        key_b[rows] = jnp.where(head_row, 0.0, keys).astype(BF16)
        value_t[0:PAIR, rows] = held[PAIR:]

    def project(first, streams, places):
        y = matmul_t(
            w_s_held[...],
            jnp.concatenate(
                [modulated(s, scale_s[...].reshape(1, D), shift_s[...].reshape(1, D)) for s in streams],
                axis=0,
            ),
        )
        for e, at in enumerate(places):
            angles = table_s[:, 0:1] * at[0:1, :] + table_s[:, 1:2] * at[1:2, :]
            cosine = jnp.cos(angles)
            sine = jnp.sin(angles)
            lead = sine * table_s[:, 2:3]
            trail = sine * table_s[:, 3:4]
            part = y[:, e * PATCHES : (e + 1) * PATCHES]

            def turned(n):
                return rotated(part[n * HD : (n + 1) * HD], cosine, lead, trail, HD // 4, 0)

            for d in range(4):
                for n in range(2):
                    base = n * HEADS + 2 * d
                    x_send[first + e, d, n * PAIR : (n + 1) * PAIR] = jnp.concatenate(
                        [turned(base), turned(base + 1)], axis=0
                    ).astype(BF16)
                rows = slice(2 * INNER + d * PAIR, 2 * INNER + (d + 1) * PAIR)
                x_send[first + e, d, 2 * PAIR :] = part[rows].astype(BF16)
        for e in range(len(streams)):
            for part in range(len(parts(first + e))):
                for k in (1, 3, 2):
                    x_copies(first + e, k)[part].start()
        for e in range(len(streams)):
            c = first + e
            place(c, x, x_send[c, x, PAIR:])
            x_recv[c, x, 0:PAIR] = x_send[c, x, 0:PAIR]

    def gather(c):
        for k in (1, 3, 2):
            column = lax.rem(x + k, 4)
            x_arrived(c, column, 0)
            place(c, column, x_recv[c, column, PAIR:])

    def z_arrived(slot):
        f = lax.rem(zh + (1, 3, 2)[slot], 4)
        to = {"space": f * 4 + x}
        remote(video.at[f], z_recv.at[slot], z_ssem.at[slot], z_rsem.at[slot], **to).wait_recv()
        remote(pos, pos_recv.at[slot], p_ssem.at[slot], p_rsem.at[slot], **to).wait_recv()

    load_own.wait()
    load_w_s.wait()
    project(0, [video_held[zh]], [pos[...]])

    w_t_held[3 * INNER :] = jnp.zeros((HALF, D), BF16)
    out_t_held[0:HALF] = jnp.zeros((HALF, D), BF16)
    value_t[PAIR:] = jnp.where(
        lax.broadcasted_iota(jnp.int32, (16, KEYS), 0) == 0, 1.0, 0.0
    ).astype(BF16)

    def frame_arrived(k, carry):
        j = lax.rem(tm + k, TM)
        remote(frame_recv.at[tm], frame_recv.at[j], f_ssem.at[j], f_rsem.at[j], tm=j).wait_recv()
        return carry

    lax.fori_loop(1, TM, frame_arrived, 0)

    def side(s):
        return lax.rem(zl + s, 2) * NEAR

    for s in range(2):
        for n in range(NEAR):
            for i in range(2):
                at = s * 32 + i * 16 + n * 2
                frame_rows[at : at + 2] = frame_recv[side(s) + n, 2 * i : 2 * i + 2]
    angles = frame_rows[:, 0:1] * table_t[0:1, :]
    sine = jnp.sin(angles)
    time_rows[0] = jnp.cos(angles)
    time_rows[1] = sine * table_t[1:2, :]
    time_rows[2] = sine * table_t[2:3, :]

    def widen(g, carry):
        rows = pl.ds(pl.multiple_of(g * 8, 8), 8)
        for n in range(3):
            time_tables[n, rows] = jnp.broadcast_to(time_rows[n, pl.ds(g, 1)], (8, WIDE))
        return carry

    lax.fori_loop(0, 64, widen, 0)

    for n in range(2):
        z_copy(n)[0].wait_send()
    z_copy(2)[0].start()
    gather(0)
    z_arrived(0)
    z_arrived(1)
    project(1, [z_recv[0], z_recv[1]], [pos_recv[0], pos_recv[1]])
    def o_copy(j):
        return remote(o_send.at[j], o_recv.at[space], o_ssem.at[j], o_rsem.at[space], space=j)

    pair_row = lax.broadcasted_iota(jnp.int32, (PAIR, 2 * PATCHES), 0) < HD
    heads = ((key_a, score_a), (key_b, score_b))

    def queries_of(c, half):
        return jnp.concatenate(
            [x_recv[c, 2 * half, 0:PAIR], x_recv[c, 2 * half + 1, 0:PAIR]], axis=1
        )

    def score(queries, blocks):
        tops = []
        for keys, scores in heads:
            top = None
            for n in blocks:
                rows = slice(n * CHUNK, (n + 1) * CHUNK)
                product = matmul(keys[rows], queries)
                scores[rows] = product
                high = jnp.max(product.reshape(CHUNK // 8, 8, 2 * PATCHES), axis=0)
                top = high if top is None else jnp.maximum(top, high)
            tops.append(jnp.max(top, axis=0, keepdims=True))
        return tops

    def mix(tops, blocks):
        sums = []
        for (_, scores), top in zip(heads, tops):
            both = None
            for n in blocks:
                rows = slice(n * CHUNK, (n + 1) * CHUNK)
                weights = jnp.exp2((scores[rows] - top) * FACTOR).astype(BF16)
                product = matmul(value_t[:, rows], weights)
                both = product if both is None else both + product
            sums.append(both)
        return sums

    def early(n, carry):
        tops = score(queries_of(n // 2, lax.rem(n, 2)), (0, 1, 2))
        for h, (top, both) in enumerate(zip(tops, mix(tops, (0, 1, 2)))):
            early_top[n, h] = jnp.broadcast_to(top, (8, 2 * PATCHES))
            early_sum[n, h] = both
        return carry

    def finish(c, n):
        half = lax.rem(n + x // 2 + 1, 2)
        queries = queries_of(c, half)
        if c == 3:
            sums = mix(score(queries, (0, 1, 2, 3)), (0, 1, 2, 3))
        else:
            tops = []
            scales = []
            for h, top in enumerate(score(queries, (3,))):
                old = early_top[2 * c + half, h, 0:1]
                tops.append(jnp.maximum(old, top))
                scales.append(jnp.exp2((old - tops[h]) * FACTOR))
            sums = [
                both + early_sum[2 * c + half, h] * scales[h]
                for h, both in enumerate(mix(tops, (3,)))
            ]
        mixed = [both[0:PAIR] / both[PAIR : PAIR + 1] for both in sums]
        result = jnp.where(pair_row, mixed[0], mixed[1]).astype(BF16)
        for e in range(2):
            j = lax.rem(zh + (0, 1, 3, 2)[c], 4) * 4 + 2 * half + e
            o_send[j] = result[:, e * PATCHES : (e + 1) * PATCHES]
            if c:
                o_copy(j).start()
            else:

                @pl.when(j != space)
                def _():
                    o_copy(j).start()

    gather(1)
    gather(2)
    lax.fori_loop(0, EARLY, early, 0)
    z_arrived(2)
    project(3, [z_recv[2]], [pos_recv[2]])
    lax.fori_loop(EARLY, 6, early, 0)
    gather(3)
    for c in (2, 1, 3, 0):
        if c == 3:
            for k in (1, 3, 2):
                x_arrived(3, lax.rem(x + k, 4), 1)

        def step(n, carry, c=c):
            finish(c, n)
            return carry

        lax.fori_loop(0, 2, step, 0)
    o_recv[space] = o_send[space]

    def t_copy(i, d):
        return remote(t_send.at[i, d], t_recv.at[i, tm], t_ssem.at[i, d], t_rsem.at[i, tm], tm=d)

    peers = [(s, r) for s in (1, 0) for r in range(NEAR) if (s, r) != (0, 0)]

    def peer(s, r):
        return side(s) + lax.rem(yc + r, NEAR)

    for copy in load_rest:
        copy.wait()
    load_out_s.wait()
    for i in range(2):

        def o_arrived(n, carry):
            j = i * 8 + n

            @pl.when(j != space)
            def _():
                remote(o_send.at[j], o_recv.at[j], o_ssem.at[j], o_rsem.at[j], space=j).wait_recv()

            return carry

        lax.fori_loop(0, 8, o_arrived, 0)
        mixed = []
        for e in range(2):
            f = 2 * i + e
            attended = o_recv[4 * f : 4 * f + 4].reshape(INNER, PATCHES)
            mixed.append(jnp.transpose(attended.astype(F32)).astype(BF16))
        branch = matmul(jnp.concatenate(mixed, axis=0), out_s_held[...])
        stream = video_held[2 * i : 2 * i + 2].reshape(2 * PATCHES, D).astype(F32)
        stream = (stream + gate_s[...].reshape(1, D) * branch).reshape(2, TM, 8, D)
        t_send[i] = jnp.stack([stream[0], stream[1]], axis=1).reshape(TM, 16, D).astype(BF16)
        for s, r in peers:
            t_copy(i, peer(s, r)).start()
        t_recv[i, tm] = t_send[i, tm]

    for copy in load_w_t:
        copy.wait()
    for s in range(2):
        for r in range(NEAR):
            if (s, r) != (0, 0):
                j = peer(s, r)
                for i in range(2):
                    remote(
                        t_send.at[i, j], t_recv.at[i, j], t_ssem.at[i, j], t_rsem.at[i, j], tm=j
                    ).wait_recv()
        rows = t_recv[:, pl.ds(side(s), NEAR)].reshape(2 * PATCHES, D)
        y = matmul_t(
            modulated(rows, scale_t[...].reshape(1, D), shift_t[...].reshape(1, D)), w_t_held[...]
        )
        angle = [time_tables[n, s * 256 : (s + 1) * 256] for n in range(3)]
        joined[s, :, 0:WIDE] = rotated(y[:, 0:WIDE], *angle, HD // 2, 1).astype(BF16)
        joined[s, :, WIDE : 2 * INNER] = y[:, WIDE : 2 * INNER].astype(BF16)
        joined[s, :, 2 * INNER :] = rotated(y[:, 2 * INNER :], *angle, HD // 2, 1).astype(BF16)

    def r_copy(s, r):
        d = peer(s, r)
        n = lax.rem(yc + r, NEAR)
        return remote(r_send.at[s, :, n], r_recv.at[:, tm], r_ssem.at[d], r_rsem.at[tm], tm=d)

    def window(start, count):
        low = start // 128 * 128
        high = (start + HD + 127) // 128 * 128
        lane = lax.broadcasted_iota(jnp.int32, (count, high - low), 1)
        return low, high, (lane >= start - low) & (lane < start - low + HD)

    same = lax.rem(lax.broadcasted_iota(jnp.int32, (256, TOKENS), 0), 8) == lax.rem(
        lax.broadcasted_iota(jnp.int32, (256, TOKENS), 1), 8
    )
    for s in (1, 0):
        total[...] = jnp.zeros((256, WIDE), F32)
        for h in range(HEADS):
            low, high, inside = window(h * HD, TOKENS)
            keys = joined[:, :, 2 * INNER + low : 2 * INNER + high].reshape(TOKENS, high - low)
            keys = jnp.where(inside, keys, jnp.zeros_like(keys))
            scores = jnp.where(same, matmul_t(joined[s, :, low:high], keys), -1e30)
            top = jnp.max(scores, axis=1, keepdims=True)
            weights = jnp.exp2((scores - top) * FACTOR)
            sums = jnp.sum(weights, axis=1, keepdims=True)
            low, high, inside = window(HALF + h * HD, 256)
            base = INNER - HALF
            values = joined[:, :, base + low : base + high].reshape(TOKENS, high - low)
            part = matmul(weights.astype(BF16), values)
            total[:, low:high] += jnp.where(inside, part / sums, 0.0)
        r_send[s] = total[...].astype(BF16).reshape(2, NEAR, 16, WIDE)
        for r in range(NEAR):
            if (s, r) != (0, 0):
                r_copy(s, r).start()
    r_recv[:, tm] = r_send[0, :, yc]

    load_out_t.wait()
    for s in range(2):
        for r in range(NEAR):
            if (s, r) != (0, 0):
                j = peer(s, r)
                remote(
                    r_send.at[0, :, 0], r_recv.at[:, j], r_ssem.at[j], r_rsem.at[j], tm=j
                ).wait_recv()
        near = pl.ds(side(s), NEAR)
        branch = matmul(r_recv[:, near].reshape(2 * PATCHES, WIDE), out_t_held[...])
        stream = t_send[:, near].reshape(2 * PATCHES, D).astype(F32)
        stream = (stream + gate_t[...].reshape(1, D) * branch).reshape(2, NEAR, 2, 8, D)
        patches = pl.ds(pl.multiple_of(side(s) * 8, 64), 64)
        for i in range(2):
            for e in range(2):
                out[2 * i + e, patches] = stream[i, :, e].reshape(64, D).astype(BF16)

    z_copy(2)[0].wait_send()
    for n in range(3):
        z_copy(n)[1].wait_send()
        for c in range(4):
            for copy in x_copies(c, n + 1):
                copy.wait_send()

    def o_sent(k, carry):
        o_copy(lax.rem(space + k, SPACE)).wait_send()
        frame_copy(k).wait_send()
        return carry

    lax.fori_loop(1, SPACE, o_sent, 0)
    for s, r in peers:
        for i in range(2):
            t_copy(i, peer(s, r)).wait_send()
        r_copy(s, r).wait_send()


def block(*arrays):
    vmem = pl.BlockSpec(memory_space=pltpu.VMEM)
    smem = pl.BlockSpec(memory_space=pltpu.SMEM)
    hbm = pl.BlockSpec(memory_space=pl.ANY)
    dma = pltpu.SemaphoreType.DMA
    specs = [hbm, vmem, vmem, smem] + [vmem, vmem, vmem, hbm, hbm] * 2 + [vmem, vmem]
    held = [
        ((FRAMES, PATCHES, D), BF16),
        ((3 * INNER, D), BF16),
        ((INNER, D), BF16),
        ((LANES, D), BF16),
        ((WIDE, D), BF16),
        ((8, PATCHES), F32),
        ((3, PATCHES, D), BF16),
        ((3, 8, PATCHES), F32),
        ((TM, 8, 128), F32),
        ((64, 128), F32),
        ((3, 64, WIDE), F32),
        ((3, TOKENS, WIDE), F32),
        ((4, 4, 3 * PAIR, PATCHES), BF16),
        ((4, 4, 3 * PAIR, PATCHES), BF16),
        ((KEYS, PAIR), BF16),
        ((KEYS, PAIR), BF16),
        ((PAIR + 16, KEYS), BF16),
        ((KEYS, 2 * PATCHES), F32),
        ((KEYS, 2 * PATCHES), F32),
        ((6, 2, 8, 2 * PATCHES), F32),
        ((6, 2, PAIR + 16, 2 * PATCHES), F32),
        ((SPACE, PAIR, PATCHES), BF16),
        ((SPACE, PAIR, PATCHES), BF16),
        ((2, TM, 16, D), BF16),
        ((2, TM, 16, D), BF16),
        ((2, 256, LANES), BF16),
        ((256, WIDE), F32),
        ((2, 2, NEAR, 16, WIDE), BF16),
        ((2, TM, 16, WIDE), BF16),
    ]
    sems = [(10,), (3,), (3,), (3,), (3,), (TM,), (TM,), (5, 4), (5, 4)]
    sems += [(SPACE,), (SPACE,), (2, TM), (2, TM), (TM,), (TM,)]
    return pl.pallas_call(
        kernel,
        out_shape=jax.ShapeDtypeStruct((FRAMES, PATCHES, D), BF16),
        in_specs=specs,
        out_specs=vmem,
        scratch_shapes=[pltpu.VMEM(*h) for h in held] + [dma(s) for s in sems],
        compiler_params=pltpu.CompilerParams(
            collective_id=1, has_side_effects=True, vmem_limit_bytes=56 * 2**20
        ),
        name="space_time_block",
    )(*arrays)


def space_table():
    f = 10000.0 ** (-np.arange(HD // 4, dtype=np.float32) / (HD // 4))
    zero = np.zeros_like(f)
    one = np.ones_like(f)
    table = np.zeros((HD, 8), np.float32)
    table[:, 0] = np.concatenate([f, f, zero, zero])
    table[:, 1] = np.concatenate([zero, zero, f, f])
    table[:, 2] = np.concatenate([-one, zero, -one, zero])
    table[:, 3] = np.concatenate([zero, one, zero, one])
    return jnp.asarray(table)


def time_table():
    f = 10000.0 ** (-np.arange(HD // 2, dtype=np.float32) / (HD // 2))
    zero = np.zeros_like(f)
    one = np.ones_like(f)
    table = np.zeros((8, WIDE), np.float32)
    table[0, :INNER] = np.tile(np.concatenate([f, f]), HEADS)
    table[1, :INNER] = np.tile(np.concatenate([-one, zero]), HEADS)
    table[2, :INNER] = np.tile(np.concatenate([zero, one]), HEADS)
    return jnp.asarray(table)


def body(*arrays):
    arrays = list(arrays)
    for n in (7, 12):
        arrays[n] = arrays[n].T
    return block(*arrays, space_table(), time_table())


def solution(mesh):
    return jax.shard_map(
        body,
        mesh=mesh,
        in_specs=(P("tm", "space", None), P("space"), P("space"), P("tm")) + (P(),) * 10,
        out_specs=P("tm", "space", None),
        check_vma=False,
    )
```

```python
import math

import jax
import jax.numpy as jnp
import numpy as np
from jax import lax
from jax.experimental import pallas as pl
from jax.experimental.pallas import tpu as pltpu
from jax.sharding import PartitionSpec as P

HEADS = 8
HD = 72
D = 1152
INNER = HEADS * HD
FRAMES = 4
PATCHES = 128
SPACE = 16
PAIR = 2 * HD
TM = 16
NEAR = 8
TOKENS = FRAMES * PATCHES
KEYS = SPACE * PATCHES
HALF = INNER % 128
WIDE = INNER + HALF
LANES = 3 * INNER + HALF
FACTOR = math.log2(math.e) / math.sqrt(HD)
CHUNK = 512
EPSILON = 1e-06
MESH = pl.DeviceIdType.MESH
BF16 = jnp.bfloat16
F32 = jnp.float32


def modulated(stream, scale, shift):
    stream = stream.astype(F32)
    centre = stream - jnp.mean(stream, axis=-1, keepdims=True)
    spread = jnp.mean(centre * centre, axis=-1, keepdims=True)
    normal = centre * lax.rsqrt(spread + EPSILON)
    return (normal * (1.0 + scale) + shift).astype(BF16)


def rotated(u, cosine, lead, trail, half, axis):
    ahead = pltpu.roll(u, u.shape[axis] - half, axis)
    behind = pltpu.roll(u, half, axis)
    return u * cosine + ahead * lead + behind * trail


def matmul(a, b):
    return jnp.dot(a, b, preferred_element_type=F32)


def matmul_t(a, b):
    return lax.dot_general(a, b, (((1,), (1,)), ((), ())), preferred_element_type=F32)


def kernel(
    video, row_index_in, col_index_in, frame_index,
    shift_s_in, scale_s_in, gate_s_in, w_s, out_s, shift_t_in, scale_t_in, gate_t_in, w_t, out_t,
    table_s_in, table_t_in,
    out,
    row_index, col_index, shift_s, scale_s, gate_s, shift_t, scale_t, gate_t, table_s, table_t,
    video_held, w_s_held, out_s_held, w_t_held, out_t_held,
    pos, z_recv, pos_recv, frame_recv, frame_rows, time_rows, time_tables,
    x_send, x_recv, key_a, key_b, value_t, score_a, score_b, early_top, early_sum, o_send, o_recv,
    t_send, t_recv, joined, total, r_send, r_recv, result,
    l_sem, z_ssem, z_rsem, p_ssem, p_rsem, f_ssem, f_rsem, x_ssem, x_rsem,
    o_ssem, o_rsem, t_ssem, t_rsem, r_ssem, r_rsem,
):
    tm = lax.axis_index("tm")
    space = lax.axis_index("space")
    zh = space // 4
    x = lax.rem(space, 4)
    zl = tm // NEAR
    yc = lax.rem(tm, NEAR)

    def remote(src, dst, ssem, rsem, **device):
        return pltpu.make_async_remote_copy(
            src_ref=src, dst_ref=dst, send_sem=ssem, recv_sem=rsem, device_id=device, device_id_type=MESH
        )

    barrier = pltpu.get_barrier_semaphore()
    for k in range(1, SPACE):
        other = {"space": lax.rem(space + k, SPACE)}
        pl.semaphore_signal(barrier, 1, device_id=other, device_id_type=MESH)
    for k in range(1, TM):
        other = {"tm": lax.rem(tm + k, TM)}
        pl.semaphore_signal(barrier, 1, device_id=other, device_id_type=MESH)

    def load(n, src, dst):
        copy = pltpu.make_async_copy(src, dst, l_sem.at[n])
        copy.start()
        return copy

    small = [
        load(10 + n, *pair)
        for n, pair in enumerate(
            (
                (row_index_in, row_index), (col_index_in, col_index), (table_s_in, table_s),
                (shift_s_in, shift_s), (scale_s_in, scale_s), (table_t_in, table_t),
                (gate_s_in, gate_s), (shift_t_in, shift_t), (scale_t_in, scale_t), (gate_t_in, gate_t),
            )
        )
    ]
    load_own = load(0, video.at[zh], video_held.at[zh])
    load_w_s = load(1, w_s, w_s_held)
    load_rest = [
        load(1 + k, video.at[lax.rem(zh + k, 4)], video_held.at[lax.rem(zh + k, 4)])
        for k in range(1, 4)
    ]
    load_out_s = load(5, out_s, out_s_held)
    load_w_t = [
        load(6 + n, w_t.at[pl.ds(here * INNER, INNER)], w_t_held.at[pl.ds(there * INNER, INNER)])
        for n, (here, there) in enumerate(((0, 0), (2, 1), (1, 2)))
    ]
    load_out_t = load(9, out_t, out_t_held.at[pl.ds(HALF, INNER)])

    def z_copy(n):
        f = lax.rem(zh + (1, 3, 2)[n], 4)
        to = {"space": f * 4 + x}
        slot = (1, 0, 2)[n]
        return (
            remote(video.at[f], z_recv.at[slot], z_ssem.at[n], z_rsem.at[slot], **to),
            remote(pos, pos_recv.at[slot], p_ssem.at[n], p_rsem.at[slot], **to),
        )

    def frame_copy(k):
        d = lax.rem(tm + k, TM)
        return remote(
            frame_recv.at[tm], frame_recv.at[tm], f_ssem.at[d], f_rsem.at[tm], tm=d
        )

    pl.semaphore_wait(barrier, SPACE + TM - 2)
    for n in range(2):
        z_copy(n)[0].start()
    for copy in small:
        copy.wait()

    row = lax.broadcasted_iota(jnp.int32, (8, PATCHES), 0)
    here = jnp.where(
        row == 0, row_index[...].reshape(1, PATCHES), col_index[...].reshape(1, PATCHES)
    )
    pos[...] = here.astype(F32)
    times = jnp.zeros((8, 128), jnp.int32)
    for f in range(FRAMES):
        times = jnp.where(row == f, frame_index[f], times)
    frame_recv[tm] = times.astype(F32)

    for n in range(3):
        z_copy(n)[1].start()
    for k in range(1, TM):
        frame_copy(k).start()

    def parts(c):
        return [(c, slice(0, 3 * PAIR))] if c < 3 else [(3, slice(PAIR, 3 * PAIR)), (4, slice(0, PAIR))]

    def x_copies(c, k):
        d = lax.rem(x + k, 4)
        return [
            remote(
                x_send.at[c, d, rows], x_recv.at[c, x, rows], x_ssem.at[n, k], x_rsem.at[n, x],
                space=zh * 4 + d,
            )
            for n, rows in parts(c)
        ]

    def x_arrived(c, column, part):
        n, rows = parts(c)[part]
        remote(
            x_send.at[c, column, rows], x_recv.at[c, column, rows], x_ssem.at[n, column],
            x_rsem.at[n, column], space=zh * 4 + column,
        ).wait_recv()

    head_row = lax.broadcasted_iota(jnp.int32, (PATCHES, PAIR), 1) < HD

    def place(c, column, held):
        rows = pl.ds(pl.multiple_of((c * 4 + column) * PATCHES, PATCHES), PATCHES)
        keys = jnp.transpose(held[0:PAIR].astype(F32))
        key_a[rows] = jnp.where(head_row, keys, 0.0).astype(BF16)
        key_b[rows] = jnp.where(head_row, 0.0, keys).astype(BF16)
        value_t[0:PAIR, rows] = held[PAIR:]

    def project(first, streams, places):
        y = matmul_t(
            w_s_held[...],
            jnp.concatenate(
                [modulated(s, scale_s[...].reshape(1, D), shift_s[...].reshape(1, D)) for s in streams],
                axis=0,
            ),
        )
        for e, at in enumerate(places):
            angles = table_s[:, 0:1] * at[0:1, :] + table_s[:, 1:2] * at[1:2, :]
            cosine = jnp.cos(angles)
            sine = jnp.sin(angles)
            lead = sine * table_s[:, 2:3]
            trail = sine * table_s[:, 3:4]
            part = y[:, e * PATCHES : (e + 1) * PATCHES]

            def turned(n):
                return rotated(part[n * HD : (n + 1) * HD], cosine, lead, trail, HD // 4, 0)

            for d in range(4):
                for n in range(2):
                    base = n * HEADS + 2 * d
                    x_send[first + e, d, n * PAIR : (n + 1) * PAIR] = jnp.concatenate(
                        [turned(base), turned(base + 1)], axis=0
                    ).astype(BF16)
                rows = slice(2 * INNER + d * PAIR, 2 * INNER + (d + 1) * PAIR)
                x_send[first + e, d, 2 * PAIR :] = part[rows].astype(BF16)
        for e in range(len(streams)):
            for part in range(len(parts(first + e))):
                for k in (1, 3, 2):
                    x_copies(first + e, k)[part].start()
        for e in range(len(streams)):
            c = first + e
            place(c, x, x_send[c, x, PAIR:])
            x_recv[c, x, 0:PAIR] = x_send[c, x, 0:PAIR]

    def gather(c):
        for k in (1, 3, 2):
            column = lax.rem(x + k, 4)
            x_arrived(c, column, 0)
            place(c, column, x_recv[c, column, PAIR:])

    def z_arrived(slot):
        f = lax.rem(zh + (1, 3, 2)[slot], 4)
        to = {"space": f * 4 + x}
        remote(video.at[f], z_recv.at[slot], z_ssem.at[slot], z_rsem.at[slot], **to).wait_recv()
        remote(pos, pos_recv.at[slot], p_ssem.at[slot], p_rsem.at[slot], **to).wait_recv()

    load_own.wait()
    load_w_s.wait()
    project(0, [video_held[zh]], [pos[...]])

    w_t_held[3 * INNER :] = jnp.zeros((HALF, D), BF16)
    out_t_held[0:HALF] = jnp.zeros((HALF, D), BF16)
    value_t[PAIR:] = jnp.where(
        lax.broadcasted_iota(jnp.int32, (16, KEYS), 0) == 0, 1.0, 0.0
    ).astype(BF16)

    def frame_arrived(k, carry):
        j = lax.rem(tm + k, TM)
        remote(frame_recv.at[tm], frame_recv.at[j], f_ssem.at[j], f_rsem.at[j], tm=j).wait_recv()
        return carry

    lax.fori_loop(1, TM, frame_arrived, 0)

    def side(s):
        return lax.rem(zl + s, 2) * NEAR

    for s in range(2):
        for n in range(NEAR):
            for i in range(2):
                at = s * 32 + i * 16 + n * 2
                frame_rows[at : at + 2] = frame_recv[side(s) + n, 2 * i : 2 * i + 2]
    angles = frame_rows[:, 0:1] * table_t[0:1, :]
    sine = jnp.sin(angles)
    time_rows[0] = jnp.cos(angles)
    time_rows[1] = sine * table_t[1:2, :]
    time_rows[2] = sine * table_t[2:3, :]

    def widen(g, carry):
        rows = pl.ds(pl.multiple_of(g * 8, 8), 8)
        for n in range(3):
            time_tables[n, rows] = jnp.broadcast_to(time_rows[n, pl.ds(g, 1)], (8, WIDE))
        return carry

    lax.fori_loop(0, 64, widen, 0)

    for n in range(2):
        z_copy(n)[0].wait_send()
    z_copy(2)[0].start()
    gather(0)
    z_arrived(0)
    z_arrived(1)
    project(1, [z_recv[0], z_recv[1]], [pos_recv[0], pos_recv[1]])
    def o_copy(j):
        return remote(o_send.at[j], o_recv.at[space], o_ssem.at[j], o_rsem.at[space], space=j)

    pair_row = lax.broadcasted_iota(jnp.int32, (PAIR, 2 * PATCHES), 0) < HD
    heads = ((key_a, score_a), (key_b, score_b))

    def queries_of(c, half):
        return jnp.concatenate(
            [x_recv[c, 2 * half, 0:PAIR], x_recv[c, 2 * half + 1, 0:PAIR]], axis=1
        )

    def score(queries, blocks):
        tops = []
        for keys, scores in heads:
            top = None
            for n in blocks:
                rows = slice(n * CHUNK, (n + 1) * CHUNK)
                product = matmul(keys[rows], queries)
                scores[rows] = product
                high = jnp.max(product.reshape(CHUNK // 8, 8, 2 * PATCHES), axis=0)
                top = high if top is None else jnp.maximum(top, high)
            tops.append(jnp.max(top, axis=0, keepdims=True))
        return tops

    def mix(tops, blocks):
        sums = []
        for (_, scores), top in zip(heads, tops):
            both = None
            for n in blocks:
                rows = slice(n * CHUNK, (n + 1) * CHUNK)
                weights = jnp.exp2((scores[rows] - top) * FACTOR).astype(BF16)
                product = matmul(value_t[:, rows], weights)
                both = product if both is None else both + product
            sums.append(both)
        return sums

    def early(n, carry):
        tops = score(queries_of(n // 2 + 1, lax.rem(n, 2)), (0, 1, 2))
        for h, (top, both) in enumerate(zip(tops, mix(tops, (0, 1, 2)))):
            early_top[n, h] = jnp.broadcast_to(top, (8, 2 * PATCHES))
            early_sum[n, h] = both
        return carry

    def finish(c, n):
        half = lax.rem(n + x // 2 + 1, 2)
        queries = queries_of(c, half)
        if c in (0, 3):
            sums = mix(score(queries, (0, 1, 2, 3)), (0, 1, 2, 3))
        else:
            tops = []
            scales = []
            for h, top in enumerate(score(queries, (3,))):
                old = early_top[2 * c - 2 + half, h, 0:1]
                tops.append(jnp.maximum(old, top))
                scales.append(jnp.exp2((old - tops[h]) * FACTOR))
            sums = [
                both + early_sum[2 * c - 2 + half, h] * scales[h]
                for h, both in enumerate(mix(tops, (3,)))
            ]
        mixed = [both[0:PAIR] / both[PAIR : PAIR + 1] for both in sums]
        result = jnp.where(pair_row, mixed[0], mixed[1]).astype(BF16)
        for e in range(2):
            j = lax.rem(zh + (0, 1, 3, 2)[c], 4) * 4 + 2 * half + e
            o_send[j] = result[:, e * PATCHES : (e + 1) * PATCHES]
            if c:
                o_copy(j).start()
            else:

                @pl.when(j != space)
                def _():
                    o_copy(j).start()

    z_arrived(2)
    project(3, [z_recv[2]], [pos_recv[2]])
    gather(1)
    gather(2)
    lax.fori_loop(0, 4, early, 0)
    gather(3)
    for c in (2, 1, 3, 0):
        if c == 3:
            for k in (1, 3, 2):
                x_arrived(3, lax.rem(x + k, 4), 1)

        def step(n, carry, c=c):
            finish(c, n)
            return carry

        lax.fori_loop(0, 2, step, 0)
    o_recv[space] = o_send[space]

    def t_copy(i, d):
        return remote(t_send.at[i, d], t_recv.at[i, tm], t_ssem.at[i, d], t_rsem.at[i, tm], tm=d)

    peers = [(s, r) for s in (1, 0) for r in range(NEAR) if (s, r) != (0, 0)]

    def peer(s, r):
        return side(s) + lax.rem(yc + r, NEAR)

    for copy in load_rest:
        copy.wait()
    load_out_s.wait()
    for i in range(2):

        def o_arrived(n, carry):
            j = i * 8 + n

            @pl.when(j != space)
            def _():
                remote(o_send.at[j], o_recv.at[j], o_ssem.at[j], o_rsem.at[j], space=j).wait_recv()

            return carry

        lax.fori_loop(0, 8, o_arrived, 0)
        mixed = []
        for e in range(2):
            f = 2 * i + e
            attended = o_recv[4 * f : 4 * f + 4].reshape(INNER, PATCHES)
            mixed.append(jnp.transpose(attended.astype(F32)).astype(BF16))
        branch = matmul(jnp.concatenate(mixed, axis=0), out_s_held[...])
        stream = video_held[2 * i : 2 * i + 2].reshape(2 * PATCHES, D).astype(F32)
        stream = (stream + gate_s[...].reshape(1, D) * branch).reshape(2, TM, 8, D)
        t_send[i] = jnp.stack([stream[0], stream[1]], axis=1).reshape(TM, 16, D).astype(BF16)
        for s, r in peers:
            t_copy(i, peer(s, r)).start()
        t_recv[i, tm] = t_send[i, tm]

    for copy in load_w_t:
        copy.wait()
    for s in range(2):
        for r in range(NEAR):
            if (s, r) != (0, 0):
                j = peer(s, r)
                for i in range(2):
                    remote(
                        t_send.at[i, j], t_recv.at[i, j], t_ssem.at[i, j], t_rsem.at[i, j], tm=j
                    ).wait_recv()
        rows = t_recv[:, pl.ds(side(s), NEAR)].reshape(2 * PATCHES, D)
        y = matmul_t(
            modulated(rows, scale_t[...].reshape(1, D), shift_t[...].reshape(1, D)), w_t_held[...]
        )
        angle = [time_tables[n, s * 256 : (s + 1) * 256] for n in range(3)]
        joined[s, :, 0:WIDE] = rotated(y[:, 0:WIDE], *angle, HD // 2, 1).astype(BF16)
        joined[s, :, WIDE : 2 * INNER] = y[:, WIDE : 2 * INNER].astype(BF16)
        joined[s, :, 2 * INNER :] = rotated(y[:, 2 * INNER :], *angle, HD // 2, 1).astype(BF16)

    def r_copy(s, r):
        d = peer(s, r)
        n = lax.rem(yc + r, NEAR)
        return remote(r_send.at[s, :, n], r_recv.at[:, tm], r_ssem.at[d], r_rsem.at[tm], tm=d)

    def window(start, count):
        low = start // 128 * 128
        high = (start + HD + 127) // 128 * 128
        lane = lax.broadcasted_iota(jnp.int32, (count, high - low), 1)
        return low, high, (lane >= start - low) & (lane < start - low + HD)

    same = lax.rem(lax.broadcasted_iota(jnp.int32, (256, TOKENS), 0), 8) == lax.rem(
        lax.broadcasted_iota(jnp.int32, (256, TOKENS), 1), 8
    )
    for s in (1, 0):
        total[...] = jnp.zeros((256, WIDE), F32)
        for h in range(HEADS):
            low, high, inside = window(h * HD, TOKENS)
            keys = joined[:, :, 2 * INNER + low : 2 * INNER + high].reshape(TOKENS, high - low)
            keys = jnp.where(inside, keys, jnp.zeros_like(keys))
            scores = jnp.where(same, matmul_t(joined[s, :, low:high], keys), -1e30)
            top = jnp.max(scores, axis=1, keepdims=True)
            weights = jnp.exp2((scores - top) * FACTOR)
            sums = jnp.sum(weights, axis=1, keepdims=True)
            low, high, inside = window(HALF + h * HD, 256)
            base = INNER - HALF
            values = joined[:, :, base + low : base + high].reshape(TOKENS, high - low)
            part = matmul(weights.astype(BF16), values)
            total[:, low:high] += jnp.where(inside, part / sums, 0.0)
        r_send[s] = total[...].astype(BF16).reshape(2, NEAR, 16, WIDE)
        for r in range(NEAR):
            if (s, r) != (0, 0):
                r_copy(s, r).start()
    r_recv[:, tm] = r_send[0, :, yc]

    load_out_t.wait()
    stores = []
    for s in range(2):
        for r in range(NEAR):
            if (s, r) != (0, 0):
                j = peer(s, r)
                remote(
                    r_send.at[0, :, 0], r_recv.at[:, j], r_ssem.at[j], r_rsem.at[j], tm=j
                ).wait_recv()
        near = pl.ds(side(s), NEAR)
        branch = matmul(r_recv[:, near].reshape(2 * PATCHES, WIDE), out_t_held[...])
        stream = t_send[:, near].reshape(2 * PATCHES, D).astype(F32)
        stream = (stream + gate_t[...].reshape(1, D) * branch).reshape(2, NEAR, 2, 8, D)
        patches = pl.ds(pl.multiple_of(side(s) * 8, 64), 64)
        for i in range(2):
            for e in range(2):
                result[2 * i + e, patches] = stream[i, :, e].reshape(64, D).astype(BF16)
        store = pltpu.make_async_copy(result.at[:, patches], out.at[:, patches], l_sem.at[s])
        store.start()
        stores.append(store)

    for store in stores:
        store.wait()
    z_copy(2)[0].wait_send()
    for n in range(3):
        z_copy(n)[1].wait_send()
        for c in range(4):
            for copy in x_copies(c, n + 1):
                copy.wait_send()

    def o_sent(k, carry):
        o_copy(lax.rem(space + k, SPACE)).wait_send()
        frame_copy(k).wait_send()
        return carry

    lax.fori_loop(1, SPACE, o_sent, 0)
    for s, r in peers:
        for i in range(2):
            t_copy(i, peer(s, r)).wait_send()
        r_copy(s, r).wait_send()


def block(*arrays):
    smem = pl.BlockSpec(memory_space=pltpu.SMEM)
    hbm = pl.BlockSpec(memory_space=pl.ANY)
    dma = pltpu.SemaphoreType.DMA
    specs = [hbm, hbm, hbm, smem] + [hbm] * 12
    held = [((PATCHES,), jnp.int32)] * 2 + [((D,), F32)] * 6 + [((HD, 8), F32), ((8, WIDE), F32)]
    held += [
        ((FRAMES, PATCHES, D), BF16),
        ((3 * INNER, D), BF16),
        ((INNER, D), BF16),
        ((LANES, D), BF16),
        ((WIDE, D), BF16),
        ((8, PATCHES), F32),
        ((3, PATCHES, D), BF16),
        ((3, 8, PATCHES), F32),
        ((TM, 8, 128), F32),
        ((64, 128), F32),
        ((3, 64, WIDE), F32),
        ((3, TOKENS, WIDE), F32),
        ((4, 4, 3 * PAIR, PATCHES), BF16),
        ((4, 4, 3 * PAIR, PATCHES), BF16),
        ((KEYS, PAIR), BF16),
        ((KEYS, PAIR), BF16),
        ((PAIR + 16, KEYS), BF16),
        ((KEYS, 2 * PATCHES), F32),
        ((KEYS, 2 * PATCHES), F32),
        ((4, 2, 8, 2 * PATCHES), F32),
        ((4, 2, PAIR + 16, 2 * PATCHES), F32),
        ((SPACE, PAIR, PATCHES), BF16),
        ((SPACE, PAIR, PATCHES), BF16),
        ((2, TM, 16, D), BF16),
        ((2, TM, 16, D), BF16),
        ((2, 256, LANES), BF16),
        ((256, WIDE), F32),
        ((2, 2, NEAR, 16, WIDE), BF16),
        ((2, TM, 16, WIDE), BF16),
        ((FRAMES, PATCHES, D), BF16),
    ]
    sems = [(20,), (3,), (3,), (3,), (3,), (TM,), (TM,), (5, 4), (5, 4)]
    sems += [(SPACE,), (SPACE,), (2, TM), (2, TM), (TM,), (TM,)]
    return pl.pallas_call(
        kernel,
        out_shape=jax.ShapeDtypeStruct((FRAMES, PATCHES, D), BF16),
        in_specs=specs,
        out_specs=hbm,
        scratch_shapes=[pltpu.VMEM(*h) for h in held] + [dma(s) for s in sems],
        compiler_params=pltpu.CompilerParams(
            collective_id=1, has_side_effects=True, vmem_limit_bytes=56 * 2**20
        ),
        name="space_time_block",
    )(*arrays)


def space_table():
    f = 10000.0 ** (-np.arange(HD // 4, dtype=np.float32) / (HD // 4))
    zero = np.zeros_like(f)
    one = np.ones_like(f)
    table = np.zeros((HD, 8), np.float32)
    table[:, 0] = np.concatenate([f, f, zero, zero])
    table[:, 1] = np.concatenate([zero, zero, f, f])
    table[:, 2] = np.concatenate([-one, zero, -one, zero])
    table[:, 3] = np.concatenate([zero, one, zero, one])
    return jnp.asarray(table)


def time_table():
    f = 10000.0 ** (-np.arange(HD // 2, dtype=np.float32) / (HD // 2))
    zero = np.zeros_like(f)
    one = np.ones_like(f)
    table = np.zeros((8, WIDE), np.float32)
    table[0, :INNER] = np.tile(np.concatenate([f, f]), HEADS)
    table[1, :INNER] = np.tile(np.concatenate([-one, zero]), HEADS)
    table[2, :INNER] = np.tile(np.concatenate([zero, one]), HEADS)
    return jnp.asarray(table)


def body(*arrays):
    arrays = list(arrays)
    for n in (7, 12):
        arrays[n] = arrays[n].T
    return block(*arrays, space_table(), time_table())


def solution(mesh):
    return jax.shard_map(
        body,
        mesh=mesh,
        in_specs=(P("tm", "space", None), P("space"), P("space"), P("tm")) + (P(),) * 10,
        out_specs=P("tm", "space", None),
        check_vma=False,
    )
```

```python
import math

import jax
import jax.numpy as jnp
import numpy as np
from jax import lax
from jax.experimental import pallas as pl
from jax.experimental.pallas import tpu as pltpu
from jax.sharding import PartitionSpec as P

HEADS = 8
HD = 72
D = 1152
INNER = HEADS * HD
FRAMES = 4
PATCHES = 128
SPACE = 16
PAIR = 2 * HD
TM = 16
NEAR = 8
TOKENS = FRAMES * PATCHES
KEYS = SPACE * PATCHES
HALF = INNER % 128
WIDE = INNER + HALF
LANES = 3 * INNER + HALF
FACTOR = math.log2(math.e) / math.sqrt(HD)
CHUNK = 512
EPSILON = 1e-06
MESH = pl.DeviceIdType.MESH
BF16 = jnp.bfloat16
F32 = jnp.float32


def modulated(stream, scale, shift):
    stream = stream.astype(F32)
    centre = stream - jnp.mean(stream, axis=-1, keepdims=True)
    spread = jnp.mean(centre * centre, axis=-1, keepdims=True)
    normal = centre * lax.rsqrt(spread + EPSILON)
    return (normal * (1.0 + scale) + shift).astype(BF16)


def rotated(u, cosine, lead, trail, half, axis):
    ahead = pltpu.roll(u, u.shape[axis] - half, axis)
    behind = pltpu.roll(u, half, axis)
    return u * cosine + ahead * lead + behind * trail


def matmul(a, b):
    return jnp.dot(a, b, preferred_element_type=F32)


def matmul_t(a, b):
    return lax.dot_general(a, b, (((1,), (1,)), ((), ())), preferred_element_type=F32)


def kernel(
    video, row_index_in, col_index_in, frame_index,
    shift_s_in, scale_s_in, gate_s_in, w_s, out_s, shift_t_in, scale_t_in, gate_t_in, w_t, out_t,
    table_s_in, table_t_in,
    out,
    row_index, col_index, shift_s, scale_s, gate_s, shift_t, scale_t, gate_t, table_s, table_t,
    video_held, w_s_held, out_s_held, w_t_held, out_t_held,
    pos, z_recv, pos_recv, frame_recv, frame_rows, time_rows, time_tables,
    x_send, x_recv, key_a, key_b, value_t, score_a, score_b, o_send, o_recv,
    t_send, t_recv, joined, total, r_send, r_recv, result,
    l_sem, z_ssem, z_rsem, p_ssem, p_rsem, f_ssem, f_rsem, x_ssem, x_rsem,
    o_ssem, o_rsem, t_ssem, t_rsem, r_ssem, r_rsem,
):
    tm = lax.axis_index("tm")
    space = lax.axis_index("space")
    zh = space // 4
    x = lax.rem(space, 4)
    zl = tm // NEAR
    yc = lax.rem(tm, NEAR)

    def remote(src, dst, ssem, rsem, **device):
        return pltpu.make_async_remote_copy(
            src_ref=src, dst_ref=dst, send_sem=ssem, recv_sem=rsem, device_id=device, device_id_type=MESH
        )

    barrier = pltpu.get_barrier_semaphore()
    for k in range(1, SPACE):
        other = {"space": lax.rem(space + k, SPACE)}
        pl.semaphore_signal(barrier, 1, device_id=other, device_id_type=MESH)
    for k in range(1, TM):
        other = {"tm": lax.rem(tm + k, TM)}
        pl.semaphore_signal(barrier, 1, device_id=other, device_id_type=MESH)

    def load(n, src, dst):
        copy = pltpu.make_async_copy(src, dst, l_sem.at[n])
        copy.start()
        return copy

    small = [
        load(10 + n, *pair)
        for n, pair in enumerate(
            (
                (row_index_in, row_index), (col_index_in, col_index), (table_s_in, table_s),
                (shift_s_in, shift_s), (scale_s_in, scale_s), (table_t_in, table_t),
                (gate_s_in, gate_s), (shift_t_in, shift_t), (scale_t_in, scale_t), (gate_t_in, gate_t),
            )
        )
    ]
    load_own, load_far = (
        load(2 * k, video.at[lax.rem(zh + 2 * k, 4)], video_held.at[lax.rem(zh + 2 * k, 4)])
        for k in range(2)
    )
    load_w_s = load(1, w_s, w_s_held)
    load_rest = [
        load(3 + k, video.at[lax.rem(zh + 1 + 2 * k, 4)], video_held.at[lax.rem(zh + 1 + 2 * k, 4)])
        for k in range(2)
    ]
    load_out_s = load(5, out_s, out_s_held)
    load_w_t = [
        load(6 + n, w_t.at[pl.ds(here * INNER, INNER)], w_t_held.at[pl.ds(there * INNER, INNER)])
        for n, (here, there) in enumerate(((0, 0), (2, 1), (1, 2)))
    ]
    load_out_t = load(9, out_t, out_t_held.at[pl.ds(HALF, INNER)])

    def z_copy(n):
        f = lax.rem(zh + (1, 3)[n], 4)
        to = {"space": f * 4 + x}
        slot = 1 - n
        return (
            remote(video.at[f], z_recv.at[slot], z_ssem.at[n], z_rsem.at[slot], **to),
            remote(pos, pos_recv.at[slot], p_ssem.at[n], p_rsem.at[slot], **to),
        )

    def frame_copy(k):
        d = lax.rem(tm + k, TM)
        return remote(
            frame_recv.at[tm], frame_recv.at[tm], f_ssem.at[d], f_rsem.at[tm], tm=d
        )

    pl.semaphore_wait(barrier, SPACE + TM - 2)
    for n in range(2):
        z_copy(n)[0].start()
    for copy in small:
        copy.wait()

    row = lax.broadcasted_iota(jnp.int32, (8, PATCHES), 0)
    here = jnp.where(
        row == 0, row_index[...].reshape(1, PATCHES), col_index[...].reshape(1, PATCHES)
    )
    pos[...] = here.astype(F32)
    times = jnp.zeros((8, 128), jnp.int32)
    for f in range(FRAMES):
        times = jnp.where(row == f, frame_index[f], times)
    frame_recv[tm] = times.astype(F32)

    for n in range(2):
        z_copy(n)[1].start()

    def parts(c):
        return [(c, slice(0, 3 * PAIR))] if c < 3 else [(3, slice(PAIR, 3 * PAIR)), (4, slice(0, PAIR))]

    def x_copies(c, k):
        d = lax.rem(x + k, 4)
        to = lax.rem(zh + 2, 4) if c == 3 else zh
        return [
            remote(
                x_send.at[c, d, rows], x_recv.at[c, x, rows], x_ssem.at[n, k], x_rsem.at[n, x],
                space=to * 4 + d,
            )
            for n, rows in parts(c)
        ]

    def x_arrived(c, column, part):
        n, rows = parts(c)[part]
        to = lax.rem(zh + 2, 4) if c == 3 else zh
        remote(
            x_send.at[c, column, rows], x_recv.at[c, column, rows], x_ssem.at[n, column],
            x_rsem.at[n, column], space=to * 4 + column,
        ).wait_recv()

    head_row = lax.broadcasted_iota(jnp.int32, (PATCHES, PAIR), 1) < HD

    def place(c, column, held):
        rows = pl.ds(pl.multiple_of((c * 4 + column) * PATCHES, PATCHES), PATCHES)
        keys = jnp.transpose(held[0:PAIR].astype(F32))
        key_a[rows] = jnp.where(head_row, keys, 0.0).astype(BF16)
        key_b[rows] = jnp.where(head_row, 0.0, keys).astype(BF16)
        value_t[0:PAIR, rows] = held[PAIR:]

    def project(blocks, streams, places):
        y = matmul_t(
            w_s_held[...],
            jnp.concatenate(
                [modulated(s, scale_s[...].reshape(1, D), shift_s[...].reshape(1, D)) for s in streams],
                axis=0,
            ),
        )
        for e, at in enumerate(places):
            angles = table_s[:, 0:1] * at[0:1, :] + table_s[:, 1:2] * at[1:2, :]
            cosine = jnp.cos(angles)
            sine = jnp.sin(angles)
            lead = sine * table_s[:, 2:3]
            trail = sine * table_s[:, 3:4]
            part = y[:, e * PATCHES : (e + 1) * PATCHES]

            def turned(n):
                return rotated(part[n * HD : (n + 1) * HD], cosine, lead, trail, HD // 4, 0)

            for d in range(4):
                for n in range(2):
                    base = n * HEADS + 2 * d
                    x_send[blocks[e], d, n * PAIR : (n + 1) * PAIR] = jnp.concatenate(
                        [turned(base), turned(base + 1)], axis=0
                    ).astype(BF16)
                rows = slice(2 * INNER + d * PAIR, 2 * INNER + (d + 1) * PAIR)
                x_send[blocks[e], d, 2 * PAIR :] = part[rows].astype(BF16)
        for c in blocks:
            if c < 3:
                for k in (1, 3, 2):
                    x_copies(c, k)[0].start()
        for c in blocks:
            if c < 3:
                place(c, x, x_send[c, x, PAIR:])
                x_recv[c, x, 0:PAIR] = x_send[c, x, 0:PAIR]

    def gather(c):
        for k in (0, 1, 3, 2) if c == 3 else (1, 3, 2):
            column = lax.rem(x + k, 4)
            x_arrived(c, column, 0)
            place(c, column, x_recv[c, column, PAIR:])

    def z_arrived(slot):
        f = lax.rem(zh + (1, 3)[slot], 4)
        to = {"space": f * 4 + x}
        remote(video.at[f], z_recv.at[slot], z_ssem.at[slot], z_rsem.at[slot], **to).wait_recv()
        remote(pos, pos_recv.at[slot], p_ssem.at[slot], p_rsem.at[slot], **to).wait_recv()

    load_own.wait()
    load_far.wait()
    load_w_s.wait()
    project((0, 3), [video_held[zh], video_held[lax.rem(zh + 2, 4)]], [pos[...], pos[...]])

    w_t_held[3 * INNER :] = jnp.zeros((HALF, D), BF16)
    out_t_held[0:HALF] = jnp.zeros((HALF, D), BF16)
    value_t[PAIR:] = jnp.where(
        lax.broadcasted_iota(jnp.int32, (16, KEYS), 0) == 0, 1.0, 0.0
    ).astype(BF16)

    for n in range(2):
        z_copy(n)[0].wait_send()
    for part in range(2):
        for k in range(4):
            x_copies(3, k)[part].start()
    for k in range(1, TM):
        frame_copy(k).start()
    gather(0)
    z_arrived(0)
    z_arrived(1)
    project((1, 2), [z_recv[0], z_recv[1]], [pos_recv[0], pos_recv[1]])

    def frame_arrived(k, carry):
        j = lax.rem(tm + k, TM)
        remote(frame_recv.at[tm], frame_recv.at[j], f_ssem.at[j], f_rsem.at[j], tm=j).wait_recv()
        return carry

    lax.fori_loop(1, TM, frame_arrived, 0)

    def side(s):
        return lax.rem(zl + s, 2) * NEAR

    for s in range(2):
        for n in range(NEAR):
            for i in range(2):
                at = s * 32 + i * 16 + n * 2
                frame_rows[at : at + 2] = frame_recv[side(s) + n, 2 * i : 2 * i + 2]
    angles = frame_rows[:, 0:1] * table_t[0:1, :]
    sine = jnp.sin(angles)
    time_rows[0] = jnp.cos(angles)
    time_rows[1] = sine * table_t[1:2, :]
    time_rows[2] = sine * table_t[2:3, :]

    def widen(g, carry):
        rows = pl.ds(pl.multiple_of(g * 8, 8), 8)
        for n in range(3):
            time_tables[n, rows] = jnp.broadcast_to(time_rows[n, pl.ds(g, 1)], (8, WIDE))
        return carry

    lax.fori_loop(0, 64, widen, 0)

    gather(1)
    gather(2)
    gather(3)

    def o_copy(j):
        return remote(o_send.at[j], o_recv.at[space], o_ssem.at[j], o_rsem.at[space], space=j)

    pair_row = lax.broadcasted_iota(jnp.int32, (PAIR, 2 * PATCHES), 0) < HD
    chunks = [slice(n * CHUNK, (n + 1) * CHUNK) for n in range(KEYS // CHUNK)]

    def attend(n, carry):
        c = jnp.where(n < 4, 2 - n // 2, jnp.where(n < 6, 3, 0))
        off = jnp.where(c == 3, 2, jnp.where(c == 2, 3, c))
        first = lax.rem(n + x // 2 + 1, 2) * 2
        queries = jnp.concatenate([x_recv[c, first, 0:PAIR], x_recv[c, first + 1, 0:PAIR]], axis=1)
        tops = []
        for keys, scores in ((key_a, score_a), (key_b, score_b)):
            top = None
            for rows in chunks:
                product = matmul(keys[rows], queries)
                scores[rows] = product
                high = jnp.max(product.reshape(CHUNK // 8, 8, 2 * PATCHES), axis=0)
                top = high if top is None else jnp.maximum(top, high)
            tops.append(jnp.max(top, axis=0, keepdims=True))
        mixed = []
        for scores, top in zip((score_a, score_b), tops):
            both = None
            for rows in chunks:
                weights = jnp.exp2((scores[rows] - top) * FACTOR).astype(BF16)
                product = matmul(value_t[:, rows], weights)
                both = product if both is None else both + product
            mixed.append(both[0:PAIR] / both[PAIR : PAIR + 1])
        result = jnp.where(pair_row, mixed[0], mixed[1]).astype(BF16)
        for e in range(2):
            j = lax.rem(zh + off, 4) * 4 + first + e
            o_send[j] = result[:, e * PATCHES : (e + 1) * PATCHES]

            @pl.when(j != space)
            def _():
                o_copy(j).start()

        return carry

    lax.fori_loop(0, 4, attend, 0)
    for k in range(4):
        x_arrived(3, lax.rem(x + k, 4), 1)
    lax.fori_loop(4, 8, attend, 0)
    o_recv[space] = o_send[space]

    def t_copy(i, d):
        return remote(t_send.at[i, d], t_recv.at[i, tm], t_ssem.at[i, d], t_rsem.at[i, tm], tm=d)

    peers = [(s, r) for s in (1, 0) for r in range(NEAR) if (s, r) != (0, 0)]

    def peer(s, r):
        return side(s) + lax.rem(yc + r, NEAR)

    for copy in load_rest:
        copy.wait()
    load_out_s.wait()
    for i in range(2):

        def o_arrived(n, carry):
            j = i * 8 + n

            @pl.when(j != space)
            def _():
                remote(o_send.at[j], o_recv.at[j], o_ssem.at[j], o_rsem.at[j], space=j).wait_recv()

            return carry

        lax.fori_loop(0, 8, o_arrived, 0)
        mixed = []
        for e in range(2):
            f = 2 * i + e
            attended = o_recv[4 * f : 4 * f + 4].reshape(INNER, PATCHES)
            mixed.append(jnp.transpose(attended.astype(F32)).astype(BF16))
        branch = matmul(jnp.concatenate(mixed, axis=0), out_s_held[...])
        stream = video_held[2 * i : 2 * i + 2].reshape(2 * PATCHES, D).astype(F32)
        stream = (stream + gate_s[...].reshape(1, D) * branch).reshape(2, TM, 8, D)
        t_send[i] = jnp.stack([stream[0], stream[1]], axis=1).reshape(TM, 16, D).astype(BF16)
        for s, r in peers:
            t_copy(i, peer(s, r)).start()
        t_recv[i, tm] = t_send[i, tm]

    for copy in load_w_t:
        copy.wait()
    for s in range(2):
        for r in range(NEAR):
            if (s, r) != (0, 0):
                j = peer(s, r)
                for i in range(2):
                    remote(
                        t_send.at[i, j], t_recv.at[i, j], t_ssem.at[i, j], t_rsem.at[i, j], tm=j
                    ).wait_recv()
        rows = t_recv[:, pl.ds(side(s), NEAR)].reshape(2 * PATCHES, D)
        y = matmul_t(
            modulated(rows, scale_t[...].reshape(1, D), shift_t[...].reshape(1, D)), w_t_held[...]
        )
        angle = [time_tables[n, s * 256 : (s + 1) * 256] for n in range(3)]
        joined[s, :, 0:WIDE] = rotated(y[:, 0:WIDE], *angle, HD // 2, 1).astype(BF16)
        joined[s, :, WIDE : 2 * INNER] = y[:, WIDE : 2 * INNER].astype(BF16)
        joined[s, :, 2 * INNER :] = rotated(y[:, 2 * INNER :], *angle, HD // 2, 1).astype(BF16)

    def r_copy(s, r):
        d = peer(s, r)
        n = lax.rem(yc + r, NEAR)
        return remote(r_send.at[s, :, n], r_recv.at[:, tm], r_ssem.at[d], r_rsem.at[tm], tm=d)

    def window(start, count):
        low = start // 128 * 128
        high = (start + HD + 127) // 128 * 128
        lane = lax.broadcasted_iota(jnp.int32, (count, high - low), 1)
        return low, high, (lane >= start - low) & (lane < start - low + HD)

    same = lax.rem(lax.broadcasted_iota(jnp.int32, (256, TOKENS), 0), 8) == lax.rem(
        lax.broadcasted_iota(jnp.int32, (256, TOKENS), 1), 8
    )
    for s in (1, 0):
        total[...] = jnp.zeros((256, WIDE), F32)
        for h in range(HEADS):
            low, high, inside = window(h * HD, TOKENS)
            keys = joined[:, :, 2 * INNER + low : 2 * INNER + high].reshape(TOKENS, high - low)
            keys = jnp.where(inside, keys, jnp.zeros_like(keys))
            scores = jnp.where(same, matmul_t(joined[s, :, low:high], keys), -1e30)
            top = jnp.max(scores, axis=1, keepdims=True)
            weights = jnp.exp2((scores - top) * FACTOR)
            sums = jnp.sum(weights, axis=1, keepdims=True)
            low, high, inside = window(HALF + h * HD, 256)
            base = INNER - HALF
            values = joined[:, :, base + low : base + high].reshape(TOKENS, high - low)
            part = matmul(weights.astype(BF16), values)
            total[:, low:high] += jnp.where(inside, part / sums, 0.0)
        r_send[s] = total[...].astype(BF16).reshape(2, NEAR, 16, WIDE)
        for r in range(NEAR):
            if (s, r) != (0, 0):
                r_copy(s, r).start()
    r_recv[:, tm] = r_send[0, :, yc]

    load_out_t.wait()
    stores = []
    for s in range(2):
        for r in range(NEAR):
            if (s, r) != (0, 0):
                j = peer(s, r)
                remote(
                    r_send.at[0, :, 0], r_recv.at[:, j], r_ssem.at[j], r_rsem.at[j], tm=j
                ).wait_recv()
        near = pl.ds(side(s), NEAR)
        branch = matmul(r_recv[:, near].reshape(2 * PATCHES, WIDE), out_t_held[...])
        stream = t_send[:, near].reshape(2 * PATCHES, D).astype(F32)
        stream = (stream + gate_t[...].reshape(1, D) * branch).reshape(2, NEAR, 2, 8, D)
        patches = pl.ds(pl.multiple_of(side(s) * 8, 64), 64)
        for i in range(2):
            for e in range(2):
                result[2 * i + e, patches] = stream[i, :, e].reshape(64, D).astype(BF16)
        store = pltpu.make_async_copy(result.at[:, patches], out.at[:, patches], l_sem.at[s])
        store.start()
        stores.append(store)

    for store in stores:
        store.wait()
    for n in range(2):
        z_copy(n)[1].wait_send()
    for c in range(4):
        for k in range(0 if c == 3 else 1, 4):
            for copy in x_copies(c, k):
                copy.wait_send()

    def o_sent(k, carry):
        o_copy(lax.rem(space + k, SPACE)).wait_send()
        frame_copy(k).wait_send()
        return carry

    lax.fori_loop(1, SPACE, o_sent, 0)
    for s, r in peers:
        for i in range(2):
            t_copy(i, peer(s, r)).wait_send()
        r_copy(s, r).wait_send()


def block(*arrays):
    smem = pl.BlockSpec(memory_space=pltpu.SMEM)
    hbm = pl.BlockSpec(memory_space=pl.ANY)
    dma = pltpu.SemaphoreType.DMA
    specs = [hbm, hbm, hbm, smem] + [hbm] * 12
    held = [((PATCHES,), jnp.int32)] * 2 + [((D,), F32)] * 6 + [((HD, 8), F32), ((8, WIDE), F32)]
    held += [
        ((FRAMES, PATCHES, D), BF16),
        ((3 * INNER, D), BF16),
        ((INNER, D), BF16),
        ((LANES, D), BF16),
        ((WIDE, D), BF16),
        ((8, PATCHES), F32),
        ((2, PATCHES, D), BF16),
        ((2, 8, PATCHES), F32),
        ((TM, 8, 128), F32),
        ((64, 128), F32),
        ((3, 64, WIDE), F32),
        ((3, TOKENS, WIDE), F32),
        ((4, 4, 3 * PAIR, PATCHES), BF16),
        ((4, 4, 3 * PAIR, PATCHES), BF16),
        ((KEYS, PAIR), BF16),
        ((KEYS, PAIR), BF16),
        ((PAIR + 16, KEYS), BF16),
        ((KEYS, 2 * PATCHES), F32),
        ((KEYS, 2 * PATCHES), F32),
        ((SPACE, PAIR, PATCHES), BF16),
        ((SPACE, PAIR, PATCHES), BF16),
        ((2, TM, 16, D), BF16),
        ((2, TM, 16, D), BF16),
        ((2, 256, LANES), BF16),
        ((256, WIDE), F32),
        ((2, 2, NEAR, 16, WIDE), BF16),
        ((2, TM, 16, WIDE), BF16),
        ((FRAMES, PATCHES, D), BF16),
    ]
    sems = [(20,), (2,), (2,), (2,), (2,), (TM,), (TM,), (5, 4), (5, 4)]
    sems += [(SPACE,), (SPACE,), (2, TM), (2, TM), (TM,), (TM,)]
    return pl.pallas_call(
        kernel,
        out_shape=jax.ShapeDtypeStruct((FRAMES, PATCHES, D), BF16),
        in_specs=specs,
        out_specs=hbm,
        scratch_shapes=[pltpu.VMEM(*h) for h in held] + [dma(s) for s in sems],
        compiler_params=pltpu.CompilerParams(
            collective_id=1, has_side_effects=True, vmem_limit_bytes=56 * 2**20
        ),
        name="space_time_block",
    )(*arrays)


def space_table():
    f = 10000.0 ** (-np.arange(HD // 4, dtype=np.float32) / (HD // 4))
    zero = np.zeros_like(f)
    one = np.ones_like(f)
    table = np.zeros((HD, 8), np.float32)
    table[:, 0] = np.concatenate([f, f, zero, zero])
    table[:, 1] = np.concatenate([zero, zero, f, f])
    table[:, 2] = np.concatenate([-one, zero, -one, zero])
    table[:, 3] = np.concatenate([zero, one, zero, one])
    return jnp.asarray(table)


def time_table():
    f = 10000.0 ** (-np.arange(HD // 2, dtype=np.float32) / (HD // 2))
    zero = np.zeros_like(f)
    one = np.ones_like(f)
    table = np.zeros((8, WIDE), np.float32)
    table[0, :INNER] = np.tile(np.concatenate([f, f]), HEADS)
    table[1, :INNER] = np.tile(np.concatenate([-one, zero]), HEADS)
    table[2, :INNER] = np.tile(np.concatenate([zero, one]), HEADS)
    return jnp.asarray(table)


def body(*arrays):
    arrays = list(arrays)
    for n in (7, 12):
        arrays[n] = arrays[n].T
    return block(*arrays, space_table(), time_table())


def solution(mesh):
    return jax.shard_map(
        body,
        mesh=mesh,
        in_specs=(P("tm", "space", None), P("space"), P("space"), P("tm")) + (P(),) * 10,
        out_specs=P("tm", "space", None),
        check_vma=False,
    )
```

```python
import math

import jax
import jax.numpy as jnp
import numpy as np
from jax import lax
from jax.experimental import pallas as pl
from jax.experimental.pallas import tpu as pltpu
from jax.sharding import PartitionSpec as P

HEADS = 8
HD = 72
D = 1152
INNER = HEADS * HD
FRAMES = 4
PATCHES = 128
SPACE = 16
PAIR = 2 * HD
TM = 16
NEAR = 8
TOKENS = FRAMES * PATCHES
KEYS = SPACE * PATCHES
HALF = INNER % 128
WIDE = INNER + HALF
LANES = 3 * INNER + HALF
FACTOR = math.log2(math.e) / math.sqrt(HD)
SIDE = PATCHES // 2
CHUNK = 512
EPSILON = 1e-06
MESH = pl.DeviceIdType.MESH
BF16 = jnp.bfloat16
F32 = jnp.float32


def modulated(stream, scale, shift):
    stream = stream.astype(F32)
    centre = stream - jnp.mean(stream, axis=-1, keepdims=True)
    spread = jnp.mean(centre * centre, axis=-1, keepdims=True)
    normal = centre * lax.rsqrt(spread + EPSILON)
    return (normal * (1.0 + scale) + shift).astype(BF16)


def rotated(u, cosine, lead, trail, half, axis):
    ahead = pltpu.roll(u, u.shape[axis] - half, axis)
    behind = pltpu.roll(u, half, axis)
    return u * cosine + ahead * lead + behind * trail


def matmul(a, b):
    return jnp.dot(a, b, preferred_element_type=F32)


def matmul_t(a, b):
    return lax.dot_general(a, b, (((1,), (1,)), ((), ())), preferred_element_type=F32)


def kernel(
    video, row_index_in, col_index_in, frame_index,
    shift_s_in, scale_s_in, gate_s_in, w_s, out_s, shift_t_in, scale_t_in, gate_t_in, w_t, out_t,
    table_s_in, table_t_in,
    out,
    row_index, col_index, shift_s, scale_s, gate_s, shift_t, scale_t, gate_t, table_s, table_t,
    video_held, w_s_held, out_s_held, w_t_held, out_t_held,
    pos, z_recv, pos_recv, frame_recv, frame_rows, time_rows, time_tables,
    x_send, x_recv, key_a, key_b, value_t, score_a, score_b, early_top, early_sum, o_send, o_recv,
    t_send, t_recv, joined, total, r_send, r_recv, result,
    l_sem, z_ssem, z_rsem, p_ssem, p_rsem, f_ssem, f_rsem, x_ssem, x_rsem,
    o_ssem, o_rsem, t_ssem, t_rsem, r_ssem, r_rsem,
):
    tm = lax.axis_index("tm")
    space = lax.axis_index("space")
    zh = space // 4
    x = lax.rem(space, 4)
    zl = tm // NEAR
    yc = lax.rem(tm, NEAR)

    def remote(src, dst, ssem, rsem, **device):
        return pltpu.make_async_remote_copy(
            src_ref=src, dst_ref=dst, send_sem=ssem, recv_sem=rsem, device_id=device, device_id_type=MESH
        )

    barrier = pltpu.get_barrier_semaphore()
    for k in range(1, SPACE):
        other = {"space": lax.rem(space + k, SPACE)}
        pl.semaphore_signal(barrier, 1, device_id=other, device_id_type=MESH)
    for k in range(1, TM):
        other = {"tm": lax.rem(tm + k, TM)}
        pl.semaphore_signal(barrier, 1, device_id=other, device_id_type=MESH)

    def load(n, src, dst):
        copy = pltpu.make_async_copy(src, dst, l_sem.at[n])
        copy.start()
        return copy

    small = [
        load(10 + n, *pair)
        for n, pair in enumerate(
            (
                (row_index_in, row_index), (col_index_in, col_index), (table_s_in, table_s),
                (shift_s_in, shift_s), (scale_s_in, scale_s), (table_t_in, table_t),
                (gate_s_in, gate_s), (shift_t_in, shift_t), (scale_t_in, scale_t), (gate_t_in, gate_t),
            )
        )
    ]
    load_own, load_far = (
        load(2 * k, video.at[lax.rem(zh + 2 * k, 4)], video_held.at[lax.rem(zh + 2 * k, 4)])
        for k in range(2)
    )
    load_w_s = load(1, w_s, w_s_held)
    load_rest = [
        load(3 + k, video.at[lax.rem(zh + 1 + 2 * k, 4)], video_held.at[lax.rem(zh + 1 + 2 * k, 4)])
        for k in range(2)
    ]
    load_out_s = load(5, out_s, out_s_held)
    load_w_t = [
        load(6 + n, w_t.at[pl.ds(here * INNER, INNER)], w_t_held.at[pl.ds(there * INNER, INNER)])
        for n, (here, there) in enumerate(((0, 0), (2, 1), (1, 2)))
    ]
    load_out_t = load(9, out_t, out_t_held.at[pl.ds(HALF, INNER)])

    def near_copy(h, n):
        f = lax.rem(zh + (1, 3)[n], 4)
        return remote(
            video.at[f, h * SIDE : (h + 1) * SIDE],
            z_recv.at[h, (1 - n) * SIDE : (2 - n) * SIDE],
            z_ssem.at[h, n], z_rsem.at[h, 1 - n], space=f * 4 + x,
        )

    def pos_copy(n):
        f = lax.rem(zh + (1, 3)[n], 4)
        return remote(pos, pos_recv.at[1 - n], p_ssem.at[n], p_rsem.at[1 - n], space=f * 4 + x)

    def frame_copy(k):
        d = lax.rem(tm + k, TM)
        return remote(
            frame_recv.at[tm], frame_recv.at[tm], f_ssem.at[d], f_rsem.at[tm], tm=d
        )

    pl.semaphore_wait(barrier, SPACE + TM - 2)
    for n in range(2):
        near_copy(0, n).start()
    for copy in small:
        copy.wait()

    row = lax.broadcasted_iota(jnp.int32, (8, PATCHES), 0)
    here = jnp.where(
        row == 0, row_index[...].reshape(1, PATCHES), col_index[...].reshape(1, PATCHES)
    )
    pos[...] = here.astype(F32)
    times = jnp.zeros((8, 128), jnp.int32)
    for f in range(FRAMES):
        times = jnp.where(row == f, frame_index[f], times)
    frame_recv[tm] = times.astype(F32)

    for n in range(2):
        pos_copy(n).start()

    def parts(c):
        return [(c, slice(0, 3 * PAIR))] if c < 3 else [(3, slice(PAIR, 3 * PAIR)), (4, slice(0, PAIR))]

    def x_copies(c, k):
        d = lax.rem(x + k, 4)
        to = lax.rem(zh + 2, 4) if c == 3 else zh
        return [
            remote(
                x_send.at[c, d, rows], x_recv.at[c, x, rows], x_ssem.at[n, k], x_rsem.at[n, x],
                space=to * 4 + d,
            )
            for n, rows in parts(c)
        ]

    def x_arrived(c, column, part):
        n, rows = parts(c)[part]
        to = lax.rem(zh + 2, 4) if c == 3 else zh
        remote(
            x_send.at[c, column, rows], x_recv.at[c, column, rows], x_ssem.at[n, column],
            x_rsem.at[n, column], space=to * 4 + column,
        ).wait_recv()

    head_row = lax.broadcasted_iota(jnp.int32, (PATCHES, PAIR), 1) < HD

    def place(c, column, held):
        rows = pl.ds(pl.multiple_of((c * 4 + column) * PATCHES, PATCHES), PATCHES)
        keys = jnp.transpose(held[0:PAIR].astype(F32))
        key_a[rows] = jnp.where(head_row, keys, 0.0).astype(BF16)
        key_b[rows] = jnp.where(head_row, 0.0, keys).astype(BF16)
        value_t[0:PAIR, rows] = held[PAIR:]

    def project(blocks, streams, places):
        y = matmul_t(
            w_s_held[...],
            jnp.concatenate(
                [modulated(s, scale_s[...].reshape(1, D), shift_s[...].reshape(1, D)) for s in streams],
                axis=0,
            ),
        )
        for e, at in enumerate(places):
            angles = table_s[:, 0:1] * at[0:1, :] + table_s[:, 1:2] * at[1:2, :]
            cosine = jnp.cos(angles)
            sine = jnp.sin(angles)
            lead = sine * table_s[:, 2:3]
            trail = sine * table_s[:, 3:4]
            part = y[:, e * PATCHES : (e + 1) * PATCHES]

            def turned(n):
                return rotated(part[n * HD : (n + 1) * HD], cosine, lead, trail, HD // 4, 0)

            for d in range(4):
                for n in range(2):
                    base = n * HEADS + 2 * d
                    x_send[blocks[e], d, n * PAIR : (n + 1) * PAIR] = jnp.concatenate(
                        [turned(base), turned(base + 1)], axis=0
                    ).astype(BF16)
                rows = slice(2 * INNER + d * PAIR, 2 * INNER + (d + 1) * PAIR)
                x_send[blocks[e], d, 2 * PAIR :] = part[rows].astype(BF16)
        for c in blocks:
            if c < 3:
                for k in (1, 3, 2):
                    x_copies(c, k)[0].start()
        for c in blocks:
            if c < 3:
                place(c, x, x_send[c, x, PAIR:])
                x_recv[c, x, 0:PAIR] = x_send[c, x, 0:PAIR]

    def gather(c):
        for k in (0, 1, 3, 2) if c == 3 else (1, 3, 2):
            column = lax.rem(x + k, 4)
            x_arrived(c, column, 0)
            place(c, column, x_recv[c, column, PAIR:])

    def near_arrived(h):
        for slot in range(2):
            f = lax.rem(zh + (1, 3)[slot], 4)
            remote(
                video.at[f, 0:SIDE], z_recv.at[h, slot * SIDE : (slot + 1) * SIDE],
                z_ssem.at[h, slot], z_rsem.at[h, slot], space=f * 4 + x,
            ).wait_recv()
            if h == 0:
                remote(
                    pos, pos_recv.at[slot], p_ssem.at[slot], p_rsem.at[slot], space=f * 4 + x
                ).wait_recv()

    def project_near(h):
        lanes = slice(h * SIDE, (h + 1) * SIDE)
        at = jnp.concatenate([pos_recv[0][:, lanes], pos_recv[1][:, lanes]], axis=1)
        project((1 + h,), [z_recv[h]], [at])

    load_own.wait()
    load_far.wait()
    load_w_s.wait()
    project((0, 3), [video_held[zh], video_held[lax.rem(zh + 2, 4)]], [pos[...], pos[...]])

    w_t_held[3 * INNER :] = jnp.zeros((HALF, D), BF16)
    out_t_held[0:HALF] = jnp.zeros((HALF, D), BF16)
    value_t[PAIR:] = jnp.where(
        lax.broadcasted_iota(jnp.int32, (16, KEYS), 0) == 0, 1.0, 0.0
    ).astype(BF16)

    for n in range(2):
        near_copy(0, n).wait_send()
    for n in range(2):
        near_copy(1, n).start()
    gather(0)
    near_arrived(0)
    project_near(0)
    for n in range(2):
        near_copy(1, n).wait_send()
    for part in range(2):
        for k in range(4):
            x_copies(3, k)[part].start()
    for k in range(1, TM):
        frame_copy(k).start()
    near_arrived(1)
    project_near(1)

    def frame_arrived(k, carry):
        j = lax.rem(tm + k, TM)
        remote(frame_recv.at[tm], frame_recv.at[j], f_ssem.at[j], f_rsem.at[j], tm=j).wait_recv()
        return carry

    lax.fori_loop(1, TM, frame_arrived, 0)

    def side(s):
        return lax.rem(zl + s, 2) * NEAR

    for s in range(2):
        for n in range(NEAR):
            for i in range(2):
                at = s * 32 + i * 16 + n * 2
                frame_rows[at : at + 2] = frame_recv[side(s) + n, 2 * i : 2 * i + 2]
    angles = frame_rows[:, 0:1] * table_t[0:1, :]
    sine = jnp.sin(angles)
    time_rows[0] = jnp.cos(angles)
    time_rows[1] = sine * table_t[1:2, :]
    time_rows[2] = sine * table_t[2:3, :]

    def widen(g, carry):
        rows = pl.ds(pl.multiple_of(g * 8, 8), 8)
        for n in range(3):
            time_tables[n, rows] = jnp.broadcast_to(time_rows[n, pl.ds(g, 1)], (8, WIDE))
        return carry

    lax.fori_loop(0, 64, widen, 0)

    def o_copy(j):
        return remote(o_send.at[j], o_recv.at[space], o_ssem.at[j], o_rsem.at[space], space=j)

    pair_row = lax.broadcasted_iota(jnp.int32, (PAIR, 2 * PATCHES), 0) < HD
    heads = ((key_a, score_a), (key_b, score_b))

    def queries_of(first, second):
        return jnp.concatenate(
            [x_recv[first[0], first[1], 0:PAIR], x_recv[second[0], second[1], 0:PAIR]], axis=1
        )

    def score(queries, blocks):
        tops = []
        for keys, scores in heads:
            top = None
            for n in blocks:
                rows = slice(n * CHUNK, (n + 1) * CHUNK)
                product = matmul(keys[rows], queries)
                scores[rows] = product
                high = jnp.max(product.reshape(CHUNK // 8, 8, 2 * PATCHES), axis=0)
                top = high if top is None else jnp.maximum(top, high)
            tops.append(jnp.max(top, axis=0, keepdims=True))
        return tops

    def mix(tops, blocks):
        sums = []
        for (_, scores), top in zip(heads, tops):
            both = None
            for n in blocks:
                rows = slice(n * CHUNK, (n + 1) * CHUNK)
                weights = jnp.exp2((scores[rows] - top) * FACTOR).astype(BF16)
                product = matmul(value_t[:, rows], weights)
                both = product if both is None else both + product
            sums.append(both)
        return sums

    def early(column, carry):
        tops = score(queries_of((1, column), (2, column)), (0, 1, 2))
        for h, (top, both) in enumerate(zip(tops, mix(tops, (0, 1, 2)))):
            early_top[column, h] = jnp.broadcast_to(top, (8, 2 * PATCHES))
            early_sum[column, h] = both
        return carry

    def divided(sums):
        mixed = [both[0:PAIR] / both[PAIR : PAIR + 1] for both in sums]
        return jnp.where(pair_row, mixed[0], mixed[1])

    def finish_near(n, carry):
        column = lax.rem(x + n, 4)
        tops = []
        scales = []
        for h, top in enumerate(score(queries_of((1, column), (2, column)), (3,))):
            old = early_top[column, h, 0:1]
            tops.append(jnp.maximum(old, top))
            scales.append(jnp.exp2((old - tops[h]) * FACTOR))
        result = divided(
            [both + early_sum[column, h] * scales[h] for h, both in enumerate(mix(tops, (3,)))]
        )
        for slot in range(2):
            j = lax.rem(zh + (1, 3)[slot], 4) * 4 + column
            low = slot * SIDE
            o_send[j] = jnp.concatenate(
                [result[:, low : low + SIDE], result[:, low + 2 * SIDE : low + 3 * SIDE]], axis=1
            ).astype(BF16)
            o_copy(j).start()
        return carry

    def finish_whole(c, n):
        first = lax.rem(n + x // 2 + 1, 2) * 2
        blocks = (0, 1, 2, 3)
        result = divided(mix(score(queries_of((c, first), (c, first + 1)), blocks), blocks)).astype(BF16)
        for e in range(2):
            j = lax.rem(zh + 2, 4) * 4 + first + e if c else zh * 4 + first + e
            o_send[j] = result[:, e * PATCHES : (e + 1) * PATCHES]
            if c:
                o_copy(j).start()
            else:

                @pl.when(j != space)
                def _():
                    o_copy(j).start()

    gather(1)
    gather(2)
    lax.fori_loop(0, 4, early, 0)
    gather(3)
    lax.fori_loop(0, 4, finish_near, 0)
    for k in range(4):
        x_arrived(3, lax.rem(x + k, 4), 1)
    for c in (3, 0):

        def step(n, carry, c=c):
            finish_whole(c, n)
            return carry

        lax.fori_loop(0, 2, step, 0)
    o_recv[space] = o_send[space]

    def t_copy(i, d):
        return remote(t_send.at[i, d], t_recv.at[i, tm], t_ssem.at[i, d], t_rsem.at[i, tm], tm=d)

    peers = [(s, r) for s in (1, 0) for r in range(NEAR) if (s, r) != (0, 0)]

    def peer(s, r):
        return side(s) + lax.rem(yc + r, NEAR)

    for copy in load_rest:
        copy.wait()
    load_out_s.wait()
    for i in range(2):

        def o_arrived(n, carry):
            j = i * 8 + n

            @pl.when(j != space)
            def _():
                remote(o_send.at[j], o_recv.at[j], o_ssem.at[j], o_rsem.at[j], space=j).wait_recv()

            return carry

        lax.fori_loop(0, 8, o_arrived, 0)
        mixed = []
        for e in range(2):
            f = 2 * i + e
            attended = o_recv[4 * f : 4 * f + 4].reshape(INNER, PATCHES)
            mixed.append(jnp.transpose(attended.astype(F32)).astype(BF16))
        branch = matmul(jnp.concatenate(mixed, axis=0), out_s_held[...])
        stream = video_held[2 * i : 2 * i + 2].reshape(2 * PATCHES, D).astype(F32)
        stream = (stream + gate_s[...].reshape(1, D) * branch).reshape(2, TM, 8, D)
        t_send[i] = jnp.stack([stream[0], stream[1]], axis=1).reshape(TM, 16, D).astype(BF16)
        for s, r in peers:
            t_copy(i, peer(s, r)).start()
        t_recv[i, tm] = t_send[i, tm]

    for copy in load_w_t:
        copy.wait()
    for s in range(2):
        for r in range(NEAR):
            if (s, r) != (0, 0):
                j = peer(s, r)
                for i in range(2):
                    remote(
                        t_send.at[i, j], t_recv.at[i, j], t_ssem.at[i, j], t_rsem.at[i, j], tm=j
                    ).wait_recv()
        rows = t_recv[:, pl.ds(side(s), NEAR)].reshape(2 * PATCHES, D)
        y = matmul_t(
            modulated(rows, scale_t[...].reshape(1, D), shift_t[...].reshape(1, D)), w_t_held[...]
        )
        angle = [time_tables[n, s * 256 : (s + 1) * 256] for n in range(3)]
        joined[s, :, 0:WIDE] = rotated(y[:, 0:WIDE], *angle, HD // 2, 1).astype(BF16)
        joined[s, :, WIDE : 2 * INNER] = y[:, WIDE : 2 * INNER].astype(BF16)
        joined[s, :, 2 * INNER :] = rotated(y[:, 2 * INNER :], *angle, HD // 2, 1).astype(BF16)

    def r_copy(s, r):
        d = peer(s, r)
        n = lax.rem(yc + r, NEAR)
        return remote(r_send.at[s, :, n], r_recv.at[:, tm], r_ssem.at[d], r_rsem.at[tm], tm=d)

    def window(start, count):
        low = start // 128 * 128
        high = (start + HD + 127) // 128 * 128
        lane = lax.broadcasted_iota(jnp.int32, (count, high - low), 1)
        return low, high, (lane >= start - low) & (lane < start - low + HD)

    same = lax.rem(lax.broadcasted_iota(jnp.int32, (256, TOKENS), 0), 8) == lax.rem(
        lax.broadcasted_iota(jnp.int32, (256, TOKENS), 1), 8
    )
    for s in (1, 0):
        total[...] = jnp.zeros((256, WIDE), F32)
        for h in range(HEADS):
            low, high, inside = window(h * HD, TOKENS)
            keys = joined[:, :, 2 * INNER + low : 2 * INNER + high].reshape(TOKENS, high - low)
            keys = jnp.where(inside, keys, jnp.zeros_like(keys))
            scores = jnp.where(same, matmul_t(joined[s, :, low:high], keys), -1e30)
            top = jnp.max(scores, axis=1, keepdims=True)
            weights = jnp.exp2((scores - top) * FACTOR)
            sums = jnp.sum(weights, axis=1, keepdims=True)
            low, high, inside = window(HALF + h * HD, 256)
            base = INNER - HALF
            values = joined[:, :, base + low : base + high].reshape(TOKENS, high - low)
            part = matmul(weights.astype(BF16), values)
            total[:, low:high] += jnp.where(inside, part / sums, 0.0)
        r_send[s] = total[...].astype(BF16).reshape(2, NEAR, 16, WIDE)
        for r in range(NEAR):
            if (s, r) != (0, 0):
                r_copy(s, r).start()
    r_recv[:, tm] = r_send[0, :, yc]

    load_out_t.wait()
    stores = []
    for s in range(2):
        for r in range(NEAR):
            if (s, r) != (0, 0):
                j = peer(s, r)
                remote(
                    r_send.at[0, :, 0], r_recv.at[:, j], r_ssem.at[j], r_rsem.at[j], tm=j
                ).wait_recv()
        near = pl.ds(side(s), NEAR)
        branch = matmul(r_recv[:, near].reshape(2 * PATCHES, WIDE), out_t_held[...])
        stream = t_send[:, near].reshape(2 * PATCHES, D).astype(F32)
        stream = (stream + gate_t[...].reshape(1, D) * branch).reshape(2, NEAR, 2, 8, D)
        patches = pl.ds(pl.multiple_of(side(s) * 8, 64), 64)
        for i in range(2):
            for e in range(2):
                result[2 * i + e, patches] = stream[i, :, e].reshape(64, D).astype(BF16)
        store = pltpu.make_async_copy(result.at[:, patches], out.at[:, patches], l_sem.at[s])
        store.start()
        stores.append(store)

    for store in stores:
        store.wait()
    for n in range(2):
        pos_copy(n).wait_send()
    for c in range(4):
        for k in range(0 if c == 3 else 1, 4):
            for copy in x_copies(c, k):
                copy.wait_send()

    def o_sent(k, carry):
        o_copy(lax.rem(space + k, SPACE)).wait_send()
        frame_copy(k).wait_send()
        return carry

    lax.fori_loop(1, SPACE, o_sent, 0)
    for s, r in peers:
        for i in range(2):
            t_copy(i, peer(s, r)).wait_send()
        r_copy(s, r).wait_send()


def block(*arrays):
    smem = pl.BlockSpec(memory_space=pltpu.SMEM)
    hbm = pl.BlockSpec(memory_space=pl.ANY)
    dma = pltpu.SemaphoreType.DMA
    specs = [hbm, hbm, hbm, smem] + [hbm] * 12
    held = [((PATCHES,), jnp.int32)] * 2 + [((D,), F32)] * 6 + [((HD, 8), F32), ((8, WIDE), F32)]
    held += [
        ((FRAMES, PATCHES, D), BF16),
        ((3 * INNER, D), BF16),
        ((INNER, D), BF16),
        ((LANES, D), BF16),
        ((WIDE, D), BF16),
        ((8, PATCHES), F32),
        ((2, PATCHES, D), BF16),
        ((2, 8, PATCHES), F32),
        ((TM, 8, 128), F32),
        ((64, 128), F32),
        ((3, 64, WIDE), F32),
        ((3, TOKENS, WIDE), F32),
        ((4, 4, 3 * PAIR, PATCHES), BF16),
        ((4, 4, 3 * PAIR, PATCHES), BF16),
        ((KEYS, PAIR), BF16),
        ((KEYS, PAIR), BF16),
        ((PAIR + 16, KEYS), BF16),
        ((KEYS, 2 * PATCHES), F32),
        ((KEYS, 2 * PATCHES), F32),
        ((4, 2, 8, 2 * PATCHES), F32),
        ((4, 2, PAIR + 16, 2 * PATCHES), F32),
        ((SPACE, PAIR, PATCHES), BF16),
        ((SPACE, PAIR, PATCHES), BF16),
        ((2, TM, 16, D), BF16),
        ((2, TM, 16, D), BF16),
        ((2, 256, LANES), BF16),
        ((256, WIDE), F32),
        ((2, 2, NEAR, 16, WIDE), BF16),
        ((2, TM, 16, WIDE), BF16),
        ((FRAMES, PATCHES, D), BF16),
    ]
    sems = [(20,), (2, 2), (2, 2), (2,), (2,), (TM,), (TM,), (5, 4), (5, 4)]
    sems += [(SPACE,), (SPACE,), (2, TM), (2, TM), (TM,), (TM,)]
    return pl.pallas_call(
        kernel,
        out_shape=jax.ShapeDtypeStruct((FRAMES, PATCHES, D), BF16),
        in_specs=specs,
        out_specs=hbm,
        scratch_shapes=[pltpu.VMEM(*h) for h in held] + [dma(s) for s in sems],
        compiler_params=pltpu.CompilerParams(
            collective_id=1, has_side_effects=True, vmem_limit_bytes=56 * 2**20
        ),
        name="space_time_block",
    )(*arrays)


def space_table():
    f = 10000.0 ** (-np.arange(HD // 4, dtype=np.float32) / (HD // 4))
    zero = np.zeros_like(f)
    one = np.ones_like(f)
    table = np.zeros((HD, 8), np.float32)
    table[:, 0] = np.concatenate([f, f, zero, zero])
    table[:, 1] = np.concatenate([zero, zero, f, f])
    table[:, 2] = np.concatenate([-one, zero, -one, zero])
    table[:, 3] = np.concatenate([zero, one, zero, one])
    return jnp.asarray(table)


def time_table():
    f = 10000.0 ** (-np.arange(HD // 2, dtype=np.float32) / (HD // 2))
    zero = np.zeros_like(f)
    one = np.ones_like(f)
    table = np.zeros((8, WIDE), np.float32)
    table[0, :INNER] = np.tile(np.concatenate([f, f]), HEADS)
    table[1, :INNER] = np.tile(np.concatenate([-one, zero]), HEADS)
    table[2, :INNER] = np.tile(np.concatenate([zero, one]), HEADS)
    return jnp.asarray(table)


def body(*arrays):
    arrays = list(arrays)
    for n in (7, 12):
        arrays[n] = arrays[n].T
    return block(*arrays, space_table(), time_table())


def solution(mesh):
    return jax.shard_map(
        body,
        mesh=mesh,
        in_specs=(P("tm", "space", None), P("space"), P("space"), P("tm")) + (P(),) * 10,
        out_specs=P("tm", "space", None),
        check_vma=False,
    )
```

```python
import math

import jax
import jax.numpy as jnp
import numpy as np
from jax import lax
from jax.experimental import pallas as pl
from jax.experimental.pallas import tpu as pltpu
from jax.sharding import PartitionSpec as P

HEADS = 8
HD = 72
D = 1152
INNER = HEADS * HD
FRAMES = 4
PATCHES = 128
SPACE = 16
PAIR = 2 * HD
TM = 16
NEAR = 8
TOKENS = FRAMES * PATCHES
KEYS = SPACE * PATCHES
HALF = INNER % 128
WIDE = INNER + HALF
LANES = 3 * INNER + HALF
FACTOR = math.log2(math.e) / math.sqrt(HD)
SIDE = PATCHES // 2
CHUNK = 512
EPSILON = 1e-06
MESH = pl.DeviceIdType.MESH
BF16 = jnp.bfloat16
F32 = jnp.float32


def modulated(stream, scale, shift):
    stream = stream.astype(F32)
    centre = stream - jnp.mean(stream, axis=-1, keepdims=True)
    spread = jnp.mean(centre * centre, axis=-1, keepdims=True)
    normal = centre * lax.rsqrt(spread + EPSILON)
    return (normal * (1.0 + scale) + shift).astype(BF16)


def rotated(u, cosine, lead, trail, half, axis):
    ahead = pltpu.roll(u, u.shape[axis] - half, axis)
    behind = pltpu.roll(u, half, axis)
    return u * cosine + ahead * lead + behind * trail


def matmul(a, b):
    return jnp.dot(a, b, preferred_element_type=F32)


def matmul_t(a, b):
    return lax.dot_general(a, b, (((1,), (1,)), ((), ())), preferred_element_type=F32)


def kernel(
    video, row_index_in, col_index_in, frame_index,
    shift_s_in, scale_s_in, gate_s_in, w_s, out_s, shift_t_in, scale_t_in, gate_t_in, w_t, out_t,
    table_s_in, table_t_in,
    out,
    row_index, col_index, shift_s, scale_s, gate_s, shift_t, scale_t, gate_t, table_s, table_t,
    video_held, w_s_held, out_s_held, w_t_held, out_t_held,
    pos, z_recv, pos_recv, frame_recv, frame_rows, time_rows, time_tables,
    x_send, x_recv, key_a, key_b, value_t, score_a, score_b, early_top, early_sum, o_send, o_recv,
    t_send, t_recv, joined, total, r_send, r_recv, result,
    l_sem, z_ssem, z_rsem, p_ssem, p_rsem, f_ssem, f_rsem, x_ssem, x_rsem,
    o_ssem, o_rsem, t_ssem, t_rsem, r_ssem, r_rsem,
):
    tm = lax.axis_index("tm")
    space = lax.axis_index("space")
    zh = space // 4
    x = lax.rem(space, 4)
    zl = tm // NEAR
    yc = lax.rem(tm, NEAR)

    def remote(src, dst, ssem, rsem, **device):
        return pltpu.make_async_remote_copy(
            src_ref=src, dst_ref=dst, send_sem=ssem, recv_sem=rsem, device_id=device, device_id_type=MESH
        )

    barrier = pltpu.get_barrier_semaphore()
    for k in range(1, SPACE):
        other = {"space": lax.rem(space + k, SPACE)}
        pl.semaphore_signal(barrier, 1, device_id=other, device_id_type=MESH)
    for k in range(1, TM):
        other = {"tm": lax.rem(tm + k, TM)}
        pl.semaphore_signal(barrier, 1, device_id=other, device_id_type=MESH)

    def load(n, src, dst):
        copy = pltpu.make_async_copy(src, dst, l_sem.at[n])
        copy.start()
        return copy

    small = [
        load(10 + n, *pair)
        for n, pair in enumerate(
            (
                (row_index_in, row_index), (col_index_in, col_index), (table_s_in, table_s),
                (shift_s_in, shift_s), (scale_s_in, scale_s), (table_t_in, table_t),
                (gate_s_in, gate_s), (shift_t_in, shift_t), (scale_t_in, scale_t), (gate_t_in, gate_t),
            )
        )
    ]
    load_own, load_far = (
        load(2 * k, video.at[lax.rem(zh + 2 * k, 4)], video_held.at[lax.rem(zh + 2 * k, 4)])
        for k in range(2)
    )
    load_w_s = load(1, w_s, w_s_held)
    load_rest = [
        load(3 + k, video.at[lax.rem(zh + 1 + 2 * k, 4)], video_held.at[lax.rem(zh + 1 + 2 * k, 4)])
        for k in range(2)
    ]
    load_out_s = load(5, out_s, out_s_held)
    load_w_t = [
        load(6 + n, w_t.at[pl.ds(here * INNER, INNER)], w_t_held.at[pl.ds(there * INNER, INNER)])
        for n, (here, there) in enumerate(((0, 0), (2, 1), (1, 2)))
    ]
    load_out_t = load(9, out_t, out_t_held.at[pl.ds(HALF, INNER)])

    def near_copy(h, n):
        f = lax.rem(zh + (1, 3)[n], 4)
        return remote(
            video.at[f, h * SIDE : (h + 1) * SIDE],
            z_recv.at[h, (1 - n) * SIDE : (2 - n) * SIDE],
            z_ssem.at[h, n], z_rsem.at[h, 1 - n], space=f * 4 + x,
        )

    def pos_copy(n):
        f = lax.rem(zh + (1, 3)[n], 4)
        return remote(pos, pos_recv.at[1 - n], p_ssem.at[n], p_rsem.at[1 - n], space=f * 4 + x)

    def frame_copy(k):
        d = lax.rem(tm + k, TM)
        return remote(
            frame_recv.at[tm], frame_recv.at[tm], f_ssem.at[d], f_rsem.at[tm], tm=d
        )

    pl.semaphore_wait(barrier, SPACE + TM - 2)
    for n in range(2):
        near_copy(0, n).start()
    for copy in small:
        copy.wait()

    row = lax.broadcasted_iota(jnp.int32, (8, PATCHES), 0)
    here = jnp.where(
        row == 0, row_index[...].reshape(1, PATCHES), col_index[...].reshape(1, PATCHES)
    )
    pos[...] = here.astype(F32)
    times = jnp.zeros((8, 128), jnp.int32)
    for f in range(FRAMES):
        times = jnp.where(row == f, frame_index[f], times)
    frame_recv[tm] = times.astype(F32)

    for n in range(2):
        pos_copy(n).start()

    def parts(c):
        return [(c, slice(0, 3 * PAIR))] if c < 3 else [(3, slice(PAIR, 3 * PAIR)), (4, slice(0, PAIR))]

    def x_copies(c, k):
        d = lax.rem(x + k, 4)
        to = lax.rem(zh + 2, 4) if c == 3 else zh
        return [
            remote(
                x_send.at[c, d, rows], x_recv.at[c, x, rows], x_ssem.at[n, k], x_rsem.at[n, x],
                space=to * 4 + d,
            )
            for n, rows in parts(c)
        ]

    def x_arrived(c, column, part):
        n, rows = parts(c)[part]
        to = lax.rem(zh + 2, 4) if c == 3 else zh
        remote(
            x_send.at[c, column, rows], x_recv.at[c, column, rows], x_ssem.at[n, column],
            x_rsem.at[n, column], space=to * 4 + column,
        ).wait_recv()

    head_row = lax.broadcasted_iota(jnp.int32, (PATCHES, PAIR), 1) < HD

    def place(c, column, held):
        rows = pl.ds(pl.multiple_of((c * 4 + column) * PATCHES, PATCHES), PATCHES)
        keys = jnp.transpose(held[0:PAIR].astype(F32))
        key_a[rows] = jnp.where(head_row, keys, 0.0).astype(BF16)
        key_b[rows] = jnp.where(head_row, 0.0, keys).astype(BF16)
        value_t[0:PAIR, rows] = held[PAIR:]

    def project(blocks, streams, places):
        y = matmul_t(
            w_s_held[...],
            jnp.concatenate(
                [modulated(s, scale_s[...].reshape(1, D), shift_s[...].reshape(1, D)) for s in streams],
                axis=0,
            ),
        )
        for e, at in enumerate(places):
            angles = table_s[:, 0:1] * at[0:1, :] + table_s[:, 1:2] * at[1:2, :]
            cosine = jnp.cos(angles)
            sine = jnp.sin(angles)
            lead = sine * table_s[:, 2:3]
            trail = sine * table_s[:, 3:4]
            part = y[:, e * PATCHES : (e + 1) * PATCHES]

            def turned(n):
                return rotated(part[n * HD : (n + 1) * HD], cosine, lead, trail, HD // 4, 0)

            for d in range(4):
                for n in range(2):
                    base = n * HEADS + 2 * d
                    x_send[blocks[e], d, n * PAIR : (n + 1) * PAIR] = jnp.concatenate(
                        [turned(base), turned(base + 1)], axis=0
                    ).astype(BF16)
                rows = slice(2 * INNER + d * PAIR, 2 * INNER + (d + 1) * PAIR)
                x_send[blocks[e], d, 2 * PAIR :] = part[rows].astype(BF16)
        for c in blocks:
            if c < 3:
                for k in (1, 3, 2):
                    x_copies(c, k)[0].start()
        for c in blocks:
            if c < 3:
                place(c, x, x_send[c, x, PAIR:])
                x_recv[c, x, 0:PAIR] = x_send[c, x, 0:PAIR]

    def gather(c):
        for k in (0, 1, 3, 2) if c == 3 else (1, 3, 2):
            column = lax.rem(x + k, 4)
            x_arrived(c, column, 0)
            place(c, column, x_recv[c, column, PAIR:])

    def near_arrived(h):
        for slot in range(2):
            f = lax.rem(zh + (1, 3)[slot], 4)
            remote(
                video.at[f, 0:SIDE], z_recv.at[h, slot * SIDE : (slot + 1) * SIDE],
                z_ssem.at[h, slot], z_rsem.at[h, slot], space=f * 4 + x,
            ).wait_recv()
            if h == 0:
                remote(
                    pos, pos_recv.at[slot], p_ssem.at[slot], p_rsem.at[slot], space=f * 4 + x
                ).wait_recv()

    def project_near(h):
        lanes = slice(h * SIDE, (h + 1) * SIDE)
        at = jnp.concatenate([pos_recv[0][:, lanes], pos_recv[1][:, lanes]], axis=1)
        project((1 + h,), [z_recv[h]], [at])

    load_own.wait()
    load_far.wait()
    load_w_s.wait()
    project((0, 3), [video_held[zh], video_held[lax.rem(zh + 2, 4)]], [pos[...], pos[...]])

    w_t_held[3 * INNER :] = jnp.zeros((HALF, D), BF16)
    out_t_held[0:HALF] = jnp.zeros((HALF, D), BF16)
    value_t[PAIR:] = jnp.where(
        lax.broadcasted_iota(jnp.int32, (16, KEYS), 0) == 0, 1.0, 0.0
    ).astype(BF16)

    for n in range(2):
        near_copy(0, n).wait_send()
    for n in range(2):
        near_copy(1, n).start()
    gather(0)
    near_arrived(0)
    project_near(0)
    for n in range(2):
        near_copy(1, n).wait_send()
    for part in range(2):
        for k in range(4):
            x_copies(3, k)[part].start()
    near_arrived(1)
    project_near(1)

    def side(s):
        return lax.rem(zl + s, 2) * NEAR

    def o_copy(j):
        return remote(o_send.at[j], o_recv.at[space], o_ssem.at[j], o_rsem.at[space], space=j)

    pair_row = lax.broadcasted_iota(jnp.int32, (PAIR, 2 * PATCHES), 0) < HD
    heads = ((key_a, score_a), (key_b, score_b))

    def queries_of(first, second):
        return jnp.concatenate(
            [x_recv[first[0], first[1], 0:PAIR], x_recv[second[0], second[1], 0:PAIR]], axis=1
        )

    def score(queries, blocks):
        tops = []
        for keys, scores in heads:
            top = None
            for n in blocks:
                rows = slice(n * CHUNK, (n + 1) * CHUNK)
                product = matmul(keys[rows], queries)
                scores[rows] = product
                high = jnp.max(product.reshape(CHUNK // 8, 8, 2 * PATCHES), axis=0)
                top = high if top is None else jnp.maximum(top, high)
            tops.append(jnp.max(top, axis=0, keepdims=True))
        return tops

    def mix(tops, blocks):
        sums = []
        for (_, scores), top in zip(heads, tops):
            both = None
            for n in blocks:
                rows = slice(n * CHUNK, (n + 1) * CHUNK)
                weights = jnp.exp2((scores[rows] - top) * FACTOR).astype(BF16)
                product = matmul(value_t[:, rows], weights)
                both = product if both is None else both + product
            sums.append(both)
        return sums

    def early(column, carry):
        tops = score(queries_of((1, column), (2, column)), (0, 1, 2))
        for h, (top, both) in enumerate(zip(tops, mix(tops, (0, 1, 2)))):
            early_top[column, h] = jnp.broadcast_to(top, (8, 2 * PATCHES))
            early_sum[column, h] = both
        return carry

    def divided(sums):
        mixed = [both[0:PAIR] / both[PAIR : PAIR + 1] for both in sums]
        return jnp.where(pair_row, mixed[0], mixed[1])

    def finish_near(n, carry):
        column = lax.rem(x + n, 4)
        tops = []
        scales = []
        for h, top in enumerate(score(queries_of((1, column), (2, column)), (3,))):
            old = early_top[column, h, 0:1]
            tops.append(jnp.maximum(old, top))
            scales.append(jnp.exp2((old - tops[h]) * FACTOR))
        result = divided(
            [both + early_sum[column, h] * scales[h] for h, both in enumerate(mix(tops, (3,)))]
        )
        for slot in range(2):
            j = lax.rem(zh + (1, 3)[slot], 4) * 4 + column
            low = slot * SIDE
            o_send[j] = jnp.concatenate(
                [result[:, low : low + SIDE], result[:, low + 2 * SIDE : low + 3 * SIDE]], axis=1
            ).astype(BF16)
            o_copy(j).start()
        return carry

    def finish_whole(c, n):
        first = lax.rem(n + x // 2 + 1, 2) * 2
        blocks = (0, 1, 2, 3)
        result = divided(mix(score(queries_of((c, first), (c, first + 1)), blocks), blocks)).astype(BF16)
        for e in range(2):
            j = lax.rem(zh + 2, 4) * 4 + first + e if c else zh * 4 + first + e
            o_send[j] = result[:, e * PATCHES : (e + 1) * PATCHES]
            if c:
                o_copy(j).start()
            else:

                @pl.when(j != space)
                def _():
                    o_copy(j).start()

    gather(1)
    gather(2)
    lax.fori_loop(0, 4, early, 0)
    gather(3)
    lax.fori_loop(0, 4, finish_near, 0)
    for k in range(4):
        x_arrived(3, lax.rem(x + k, 4), 1)
    for c in (3, 0):

        def step(n, carry, c=c):
            finish_whole(c, n)
            return carry

        lax.fori_loop(0, 2, step, 0)
    o_recv[space] = o_send[space]
    for k in range(1, TM):
        frame_copy(k).start()

    def t_copy(i, d):
        return remote(t_send.at[i, d], t_recv.at[i, tm], t_ssem.at[i, d], t_rsem.at[i, tm], tm=d)

    peers = [(s, r) for s in (1, 0) for r in range(NEAR) if (s, r) != (0, 0)]

    def peer(s, r):
        return side(s) + lax.rem(yc + r, NEAR)

    for copy in load_rest:
        copy.wait()
    load_out_s.wait()
    for i in range(2):

        def o_arrived(n, carry):
            j = i * 8 + n

            @pl.when(j != space)
            def _():
                remote(o_send.at[j], o_recv.at[j], o_ssem.at[j], o_rsem.at[j], space=j).wait_recv()

            return carry

        lax.fori_loop(0, 8, o_arrived, 0)
        mixed = []
        for e in range(2):
            f = 2 * i + e
            attended = o_recv[4 * f : 4 * f + 4].reshape(INNER, PATCHES)
            mixed.append(jnp.transpose(attended.astype(F32)).astype(BF16))
        branch = matmul(jnp.concatenate(mixed, axis=0), out_s_held[...])
        stream = video_held[2 * i : 2 * i + 2].reshape(2 * PATCHES, D).astype(F32)
        stream = (stream + gate_s[...].reshape(1, D) * branch).reshape(2, TM, 8, D)
        t_send[i] = jnp.stack([stream[0], stream[1]], axis=1).reshape(TM, 16, D).astype(BF16)
        for s, r in peers:
            t_copy(i, peer(s, r)).start()
        t_recv[i, tm] = t_send[i, tm]

    def frame_arrived(k, carry):
        j = lax.rem(tm + k, TM)
        remote(frame_recv.at[tm], frame_recv.at[j], f_ssem.at[j], f_rsem.at[j], tm=j).wait_recv()
        return carry

    lax.fori_loop(1, TM, frame_arrived, 0)

    for s in range(2):
        for n in range(NEAR):
            for i in range(2):
                at = s * 32 + i * 16 + n * 2
                frame_rows[at : at + 2] = frame_recv[side(s) + n, 2 * i : 2 * i + 2]
    angles = frame_rows[:, 0:1] * table_t[0:1, :]
    sine = jnp.sin(angles)
    time_rows[0] = jnp.cos(angles)
    time_rows[1] = sine * table_t[1:2, :]
    time_rows[2] = sine * table_t[2:3, :]

    def widen(g, carry):
        rows = pl.ds(pl.multiple_of(g * 8, 8), 8)
        for n in range(3):
            time_tables[n, rows] = jnp.broadcast_to(time_rows[n, pl.ds(g, 1)], (8, WIDE))
        return carry

    lax.fori_loop(0, 64, widen, 0)

    for copy in load_w_t:
        copy.wait()
    for s in range(2):
        for r in range(NEAR):
            if (s, r) != (0, 0):
                j = peer(s, r)
                for i in range(2):
                    remote(
                        t_send.at[i, j], t_recv.at[i, j], t_ssem.at[i, j], t_rsem.at[i, j], tm=j
                    ).wait_recv()
        rows = t_recv[:, pl.ds(side(s), NEAR)].reshape(2 * PATCHES, D)
        y = matmul_t(
            modulated(rows, scale_t[...].reshape(1, D), shift_t[...].reshape(1, D)), w_t_held[...]
        )
        angle = [time_tables[n, s * 256 : (s + 1) * 256] for n in range(3)]
        joined[s, :, 0:WIDE] = rotated(y[:, 0:WIDE], *angle, HD // 2, 1).astype(BF16)
        joined[s, :, WIDE : 2 * INNER] = y[:, WIDE : 2 * INNER].astype(BF16)
        joined[s, :, 2 * INNER :] = rotated(y[:, 2 * INNER :], *angle, HD // 2, 1).astype(BF16)

    def r_copy(s, r):
        d = peer(s, r)
        n = lax.rem(yc + r, NEAR)
        return remote(r_send.at[s, :, n], r_recv.at[:, tm], r_ssem.at[d], r_rsem.at[tm], tm=d)

    def window(start, count):
        low = start // 128 * 128
        high = (start + HD + 127) // 128 * 128
        lane = lax.broadcasted_iota(jnp.int32, (count, high - low), 1)
        return low, high, (lane >= start - low) & (lane < start - low + HD)

    same = lax.rem(lax.broadcasted_iota(jnp.int32, (256, TOKENS), 0), 8) == lax.rem(
        lax.broadcasted_iota(jnp.int32, (256, TOKENS), 1), 8
    )
    for s in (1, 0):
        total[...] = jnp.zeros((256, WIDE), F32)
        for h in range(HEADS):
            low, high, inside = window(h * HD, TOKENS)
            keys = joined[:, :, 2 * INNER + low : 2 * INNER + high].reshape(TOKENS, high - low)
            keys = jnp.where(inside, keys, jnp.zeros_like(keys))
            scores = jnp.where(same, matmul_t(joined[s, :, low:high], keys), -1e30)
            top = jnp.max(scores, axis=1, keepdims=True)
            weights = jnp.exp2((scores - top) * FACTOR)
            sums = jnp.sum(weights, axis=1, keepdims=True)
            low, high, inside = window(HALF + h * HD, 256)
            base = INNER - HALF
            values = joined[:, :, base + low : base + high].reshape(TOKENS, high - low)
            part = matmul(weights.astype(BF16), values)
            total[:, low:high] += jnp.where(inside, part / sums, 0.0)
        r_send[s] = total[...].astype(BF16).reshape(2, NEAR, 16, WIDE)
        for r in range(NEAR):
            if (s, r) != (0, 0):
                r_copy(s, r).start()
    r_recv[:, tm] = r_send[0, :, yc]

    load_out_t.wait()
    stores = []
    for s in range(2):
        for r in range(NEAR):
            if (s, r) != (0, 0):
                j = peer(s, r)
                remote(
                    r_send.at[0, :, 0], r_recv.at[:, j], r_ssem.at[j], r_rsem.at[j], tm=j
                ).wait_recv()
        near = pl.ds(side(s), NEAR)
        branch = matmul(r_recv[:, near].reshape(2 * PATCHES, WIDE), out_t_held[...])
        stream = t_send[:, near].reshape(2 * PATCHES, D).astype(F32)
        stream = (stream + gate_t[...].reshape(1, D) * branch).reshape(2, NEAR, 2, 8, D)
        patches = pl.ds(pl.multiple_of(side(s) * 8, 64), 64)
        for i in range(2):
            for e in range(2):
                result[2 * i + e, patches] = stream[i, :, e].reshape(64, D).astype(BF16)
        store = pltpu.make_async_copy(result.at[:, patches], out.at[:, patches], l_sem.at[s])
        store.start()
        stores.append(store)

    for store in stores:
        store.wait()
    for n in range(2):
        pos_copy(n).wait_send()
    for c in range(4):
        for k in range(0 if c == 3 else 1, 4):
            for copy in x_copies(c, k):
                copy.wait_send()

    def o_sent(k, carry):
        o_copy(lax.rem(space + k, SPACE)).wait_send()
        frame_copy(k).wait_send()
        return carry

    lax.fori_loop(1, SPACE, o_sent, 0)
    for s, r in peers:
        for i in range(2):
            t_copy(i, peer(s, r)).wait_send()
        r_copy(s, r).wait_send()


def block(*arrays):
    smem = pl.BlockSpec(memory_space=pltpu.SMEM)
    hbm = pl.BlockSpec(memory_space=pl.ANY)
    dma = pltpu.SemaphoreType.DMA
    specs = [hbm, hbm, hbm, smem] + [hbm] * 12
    held = [((PATCHES,), jnp.int32)] * 2 + [((D,), F32)] * 6 + [((HD, 8), F32), ((8, WIDE), F32)]
    held += [
        ((FRAMES, PATCHES, D), BF16),
        ((3 * INNER, D), BF16),
        ((INNER, D), BF16),
        ((LANES, D), BF16),
        ((WIDE, D), BF16),
        ((8, PATCHES), F32),
        ((2, PATCHES, D), BF16),
        ((2, 8, PATCHES), F32),
        ((TM, 8, 128), F32),
        ((64, 128), F32),
        ((3, 64, WIDE), F32),
        ((3, TOKENS, WIDE), F32),
        ((4, 4, 3 * PAIR, PATCHES), BF16),
        ((4, 4, 3 * PAIR, PATCHES), BF16),
        ((KEYS, PAIR), BF16),
        ((KEYS, PAIR), BF16),
        ((PAIR + 16, KEYS), BF16),
        ((KEYS, 2 * PATCHES), F32),
        ((KEYS, 2 * PATCHES), F32),
        ((4, 2, 8, 2 * PATCHES), F32),
        ((4, 2, PAIR + 16, 2 * PATCHES), F32),
        ((SPACE, PAIR, PATCHES), BF16),
        ((SPACE, PAIR, PATCHES), BF16),
        ((2, TM, 16, D), BF16),
        ((2, TM, 16, D), BF16),
        ((2, 256, LANES), BF16),
        ((256, WIDE), F32),
        ((2, 2, NEAR, 16, WIDE), BF16),
        ((2, TM, 16, WIDE), BF16),
        ((FRAMES, PATCHES, D), BF16),
    ]
    sems = [(20,), (2, 2), (2, 2), (2,), (2,), (TM,), (TM,), (5, 4), (5, 4)]
    sems += [(SPACE,), (SPACE,), (2, TM), (2, TM), (TM,), (TM,)]
    return pl.pallas_call(
        kernel,
        out_shape=jax.ShapeDtypeStruct((FRAMES, PATCHES, D), BF16),
        in_specs=specs,
        out_specs=hbm,
        scratch_shapes=[pltpu.VMEM(*h) for h in held] + [dma(s) for s in sems],
        compiler_params=pltpu.CompilerParams(
            collective_id=1, has_side_effects=True, vmem_limit_bytes=56 * 2**20
        ),
        name="space_time_block",
    )(*arrays)


def space_table():
    f = 10000.0 ** (-np.arange(HD // 4, dtype=np.float32) / (HD // 4))
    zero = np.zeros_like(f)
    one = np.ones_like(f)
    table = np.zeros((HD, 8), np.float32)
    table[:, 0] = np.concatenate([f, f, zero, zero])
    table[:, 1] = np.concatenate([zero, zero, f, f])
    table[:, 2] = np.concatenate([-one, zero, -one, zero])
    table[:, 3] = np.concatenate([zero, one, zero, one])
    return jnp.asarray(table)


def time_table():
    f = 10000.0 ** (-np.arange(HD // 2, dtype=np.float32) / (HD // 2))
    zero = np.zeros_like(f)
    one = np.ones_like(f)
    table = np.zeros((8, WIDE), np.float32)
    table[0, :INNER] = np.tile(np.concatenate([f, f]), HEADS)
    table[1, :INNER] = np.tile(np.concatenate([-one, zero]), HEADS)
    table[2, :INNER] = np.tile(np.concatenate([zero, one]), HEADS)
    return jnp.asarray(table)


def body(*arrays):
    arrays = list(arrays)
    for n in (7, 12):
        arrays[n] = arrays[n].T
    return block(*arrays, space_table(), time_table())


def solution(mesh):
    return jax.shard_map(
        body,
        mesh=mesh,
        in_specs=(P("tm", "space", None), P("space"), P("space"), P("tm")) + (P(),) * 10,
        out_specs=P("tm", "space", None),
        check_vma=False,
    )
```

```python
import math

import jax
import jax.numpy as jnp
import numpy as np
from jax import lax
from jax.experimental import pallas as pl
from jax.experimental.pallas import tpu as pltpu
from jax.sharding import PartitionSpec as P

HEADS = 8
HD = 72
D = 1152
INNER = HEADS * HD
FRAMES = 4
PATCHES = 128
SPACE = 16
PAIR = 2 * HD
TM = 16
NEAR = 8
TOKENS = FRAMES * PATCHES
KEYS = SPACE * PATCHES
HALF = INNER % 128
WIDE = INNER + HALF
LANES = 3 * INNER + HALF
FACTOR = math.log2(math.e) / math.sqrt(HD)
SIDE = PATCHES // 2
CHUNK = 512
EPSILON = 1e-06
MESH = pl.DeviceIdType.MESH
BF16 = jnp.bfloat16
F32 = jnp.float32


def modulated(stream, scale, shift):
    stream = stream.astype(F32)
    centre = stream - jnp.mean(stream, axis=-1, keepdims=True)
    spread = jnp.mean(centre * centre, axis=-1, keepdims=True)
    normal = centre * lax.rsqrt(spread + EPSILON)
    return (normal * (1.0 + scale) + shift).astype(BF16)


def rotated(u, cosine, lead, trail, half, axis):
    ahead = pltpu.roll(u, u.shape[axis] - half, axis)
    behind = pltpu.roll(u, half, axis)
    return u * cosine + ahead * lead + behind * trail


def matmul(a, b):
    return jnp.dot(a, b, preferred_element_type=F32)


def matmul_t(a, b):
    return lax.dot_general(a, b, (((1,), (1,)), ((), ())), preferred_element_type=F32)


def kernel(
    video, row_index_in, col_index_in, frame_index,
    shift_s_in, scale_s_in, gate_s_in, w_s, out_s, shift_t_in, scale_t_in, gate_t_in, w_t, out_t,
    table_s_in, table_t_in,
    out,
    row_index, col_index, shift_s, scale_s, gate_s, shift_t, scale_t, gate_t, table_s, table_t,
    video_held, w_s_held, out_s_held, w_t_held, out_t_held,
    pos, z_recv, pos_recv, frame_recv, frame_rows, time_rows, time_tables,
    x_send, x_recv, key_a, key_b, value_t, score_a, score_b, early_top, early_sum, o_send, o_recv,
    t_send, t_recv, joined, total, r_send, r_recv, result,
    l_sem, z_ssem, z_rsem, p_ssem, p_rsem, f_ssem, f_rsem, x_ssem, x_rsem,
    o_ssem, o_rsem, t_ssem, t_rsem, r_ssem, r_rsem,
):
    tm = lax.axis_index("tm")
    space = lax.axis_index("space")
    zh = space // 4
    x = lax.rem(space, 4)
    zl = tm // NEAR
    yc = lax.rem(tm, NEAR)

    def remote(src, dst, ssem, rsem, **device):
        return pltpu.make_async_remote_copy(
            src_ref=src, dst_ref=dst, send_sem=ssem, recv_sem=rsem, device_id=device, device_id_type=MESH
        )

    barrier = pltpu.get_barrier_semaphore()
    for k in range(1, SPACE):
        other = {"space": lax.rem(space + k, SPACE)}
        pl.semaphore_signal(barrier, 1, device_id=other, device_id_type=MESH)
    for k in range(1, TM):
        other = {"tm": lax.rem(tm + k, TM)}
        pl.semaphore_signal(barrier, 1, device_id=other, device_id_type=MESH)

    def load(n, src, dst):
        copy = pltpu.make_async_copy(src, dst, l_sem.at[n])
        copy.start()
        return copy

    small = [
        load(10 + n, *pair)
        for n, pair in enumerate(
            (
                (row_index_in, row_index), (col_index_in, col_index), (table_s_in, table_s),
                (shift_s_in, shift_s), (scale_s_in, scale_s), (table_t_in, table_t),
                (gate_s_in, gate_s), (shift_t_in, shift_t), (scale_t_in, scale_t), (gate_t_in, gate_t),
            )
        )
    ]
    load_own, load_far = (
        load(2 * k, video.at[lax.rem(zh + 2 * k, 4)], video_held.at[lax.rem(zh + 2 * k, 4)])
        for k in range(2)
    )
    load_w_s = load(1, w_s, w_s_held)
    load_rest = [
        load(3 + k, video.at[lax.rem(zh + 1 + 2 * k, 4)], video_held.at[lax.rem(zh + 1 + 2 * k, 4)])
        for k in range(2)
    ]
    load_out_s = load(5, out_s, out_s_held)
    load_w_t = [
        load(6 + n, w_t.at[pl.ds(here * INNER, INNER)], w_t_held.at[pl.ds(there * INNER, INNER)])
        for n, (here, there) in enumerate(((0, 0), (2, 1), (1, 2)))
    ]
    load_out_t = load(9, out_t, out_t_held.at[pl.ds(HALF, INNER)])

    def near_copy(h, n):
        f = lax.rem(zh + (1, 3)[n], 4)
        return remote(
            video.at[f, h * SIDE : (h + 1) * SIDE],
            z_recv.at[h, (1 - n) * SIDE : (2 - n) * SIDE],
            z_ssem.at[h, n], z_rsem.at[h, 1 - n], space=f * 4 + x,
        )

    def pos_copy(n):
        f = lax.rem(zh + (1, 3)[n], 4)
        return remote(pos, pos_recv.at[1 - n], p_ssem.at[n], p_rsem.at[1 - n], space=f * 4 + x)

    def frame_copy(k):
        d = lax.rem(tm + k, TM)
        return remote(
            frame_recv.at[tm], frame_recv.at[tm], f_ssem.at[d], f_rsem.at[tm], tm=d
        )

    pl.semaphore_wait(barrier, SPACE + TM - 2)
    for n in range(2):
        near_copy(0, n).start()
    for copy in small:
        copy.wait()

    row = lax.broadcasted_iota(jnp.int32, (8, PATCHES), 0)
    here = jnp.where(
        row == 0, row_index[...].reshape(1, PATCHES), col_index[...].reshape(1, PATCHES)
    )
    pos[...] = here.astype(F32)
    times = jnp.zeros((8, 128), jnp.int32)
    for f in range(FRAMES):
        times = jnp.where(row == f, frame_index[f], times)
    frame_recv[tm] = times.astype(F32)

    for n in range(2):
        pos_copy(n).start()

    def parts(c):
        return [(c, slice(0, 3 * PAIR))] if c < 3 else [(3, slice(PAIR, 3 * PAIR)), (4, slice(0, PAIR))]

    def x_copies(c, k):
        d = lax.rem(x + k, 4)
        to = lax.rem(zh + 2, 4) if c == 3 else zh
        return [
            remote(
                x_send.at[c, d, rows], x_recv.at[c, x, rows], x_ssem.at[n, k], x_rsem.at[n, x],
                space=to * 4 + d,
            )
            for n, rows in parts(c)
        ]

    def x_arrived(c, column, part):
        n, rows = parts(c)[part]
        to = lax.rem(zh + 2, 4) if c == 3 else zh
        remote(
            x_send.at[c, column, rows], x_recv.at[c, column, rows], x_ssem.at[n, column],
            x_rsem.at[n, column], space=to * 4 + column,
        ).wait_recv()

    head_row = lax.broadcasted_iota(jnp.int32, (PATCHES, PAIR), 1) < HD

    def place(c, column, held):
        rows = pl.ds(pl.multiple_of((c * 4 + column) * PATCHES, PATCHES), PATCHES)
        keys = jnp.transpose(held[0:PAIR].astype(F32))
        key_a[rows] = jnp.where(head_row, keys, 0.0).astype(BF16)
        key_b[rows] = jnp.where(head_row, 0.0, keys).astype(BF16)
        value_t[0:PAIR, rows] = held[PAIR:]

    def project(blocks, streams, places):
        y = matmul_t(
            w_s_held[...],
            jnp.concatenate(
                [modulated(s, scale_s[...].reshape(1, D), shift_s[...].reshape(1, D)) for s in streams],
                axis=0,
            ),
        )
        for e, at in enumerate(places):
            angles = table_s[:, 0:1] * at[0:1, :] + table_s[:, 1:2] * at[1:2, :]
            cosine = jnp.cos(angles)
            sine = jnp.sin(angles)
            lead = sine * table_s[:, 2:3]
            trail = sine * table_s[:, 3:4]
            part = y[:, e * PATCHES : (e + 1) * PATCHES]

            def turned(n):
                return rotated(part[n * HD : (n + 1) * HD], cosine, lead, trail, HD // 4, 0)

            for d in range(4):
                for n in range(2):
                    base = n * HEADS + 2 * d
                    x_send[blocks[e], d, n * PAIR : (n + 1) * PAIR] = jnp.concatenate(
                        [turned(base), turned(base + 1)], axis=0
                    ).astype(BF16)
                rows = slice(2 * INNER + d * PAIR, 2 * INNER + (d + 1) * PAIR)
                x_send[blocks[e], d, 2 * PAIR :] = part[rows].astype(BF16)
        for c in blocks:
            if c < 3:
                for k in (1, 3, 2):
                    x_copies(c, k)[0].start()
        for c in blocks:
            if c < 3:
                place(c, x, x_send[c, x, PAIR:])
                x_recv[c, x, 0:PAIR] = x_send[c, x, 0:PAIR]

    def gather(c):
        for k in (0, 1, 3, 2) if c == 3 else (1, 3, 2):
            column = lax.rem(x + k, 4)
            x_arrived(c, column, 0)
            place(c, column, x_recv[c, column, PAIR:])

    def near_arrived(h):
        for slot in range(2):
            f = lax.rem(zh + (1, 3)[slot], 4)
            remote(
                video.at[f, 0:SIDE], z_recv.at[h, slot * SIDE : (slot + 1) * SIDE],
                z_ssem.at[h, slot], z_rsem.at[h, slot], space=f * 4 + x,
            ).wait_recv()
            if h == 0:
                remote(
                    pos, pos_recv.at[slot], p_ssem.at[slot], p_rsem.at[slot], space=f * 4 + x
                ).wait_recv()

    def project_near(h):
        lanes = slice(h * SIDE, (h + 1) * SIDE)
        at = jnp.concatenate([pos_recv[0][:, lanes], pos_recv[1][:, lanes]], axis=1)
        project((1 + h,), [z_recv[h]], [at])

    load_own.wait()
    load_far.wait()
    load_w_s.wait()
    project((0, 3), [video_held[zh], video_held[lax.rem(zh + 2, 4)]], [pos[...], pos[...]])

    w_t_held[3 * INNER :] = jnp.zeros((HALF, D), BF16)
    out_t_held[0:HALF] = jnp.zeros((HALF, D), BF16)
    value_t[PAIR:] = jnp.where(
        lax.broadcasted_iota(jnp.int32, (16, KEYS), 0) == 0, 1.0, 0.0
    ).astype(BF16)

    for n in range(2):
        near_copy(0, n).wait_send()
    for n in range(2):
        near_copy(1, n).start()
    gather(0)
    near_arrived(0)
    project_near(0)
    for n in range(2):
        near_copy(1, n).wait_send()
    for part in range(2):
        for k in range(4):
            x_copies(3, k)[part].start()
    near_arrived(1)
    project_near(1)

    def side(s):
        return lax.rem(zl + s, 2) * NEAR

    def o_copy(j):
        return remote(o_send.at[j], o_recv.at[space], o_ssem.at[j], o_rsem.at[space], space=j)

    pair_row = lax.broadcasted_iota(jnp.int32, (PAIR, 2 * PATCHES), 0) < HD
    heads = ((key_a, score_a), (key_b, score_b))

    def queries_of(first, second):
        return jnp.concatenate(
            [x_recv[first[0], first[1], 0:PAIR], x_recv[second[0], second[1], 0:PAIR]], axis=1
        )

    def score(queries, blocks):
        tops = []
        for keys, scores in heads:
            top = None
            for n in blocks:
                rows = slice(n * CHUNK, (n + 1) * CHUNK)
                product = matmul(keys[rows], queries)
                scores[rows] = product
                high = jnp.max(product.reshape(CHUNK // 8, 8, 2 * PATCHES), axis=0)
                top = high if top is None else jnp.maximum(top, high)
            tops.append(jnp.max(top, axis=0, keepdims=True))
        return tops

    def mix(tops, blocks):
        sums = []
        for (_, scores), top in zip(heads, tops):
            both = None
            for n in blocks:
                rows = slice(n * CHUNK, (n + 1) * CHUNK)
                weights = jnp.exp2((scores[rows] - top) * FACTOR).astype(BF16)
                product = matmul(value_t[:, rows], weights)
                both = product if both is None else both + product
            sums.append(both)
        return sums

    def early(column, carry):
        tops = score(queries_of((1, column), (2, column)), (0, 1, 2))
        for h, (top, both) in enumerate(zip(tops, mix(tops, (0, 1, 2)))):
            early_top[column, h] = jnp.broadcast_to(top, (8, 2 * PATCHES))
            early_sum[column, h] = both
        return carry

    def divided(sums):
        mixed = [both[0:PAIR] / both[PAIR : PAIR + 1] for both in sums]
        return jnp.where(pair_row, mixed[0], mixed[1])

    def finish_near(n, carry):
        column = lax.rem(x + n, 4)
        tops = []
        scales = []
        for h, top in enumerate(score(queries_of((1, column), (2, column)), (3,))):
            old = early_top[column, h, 0:1]
            tops.append(jnp.maximum(old, top))
            scales.append(jnp.exp2((old - tops[h]) * FACTOR))
        result = divided(
            [both + early_sum[column, h] * scales[h] for h, both in enumerate(mix(tops, (3,)))]
        )
        for slot in range(2):
            j = lax.rem(zh + (1, 3)[slot], 4) * 4 + column
            low = slot * SIDE
            o_send[j] = jnp.concatenate(
                [result[:, low : low + SIDE], result[:, low + 2 * SIDE : low + 3 * SIDE]], axis=1
            ).astype(BF16)
            o_copy(j).start()
        return carry

    def finish_whole(c, n):
        first = lax.rem(n + x // 2 + 1, 2) * 2
        blocks = (0, 1, 2, 3)
        result = divided(mix(score(queries_of((c, first), (c, first + 1)), blocks), blocks)).astype(BF16)
        for e in range(2):
            j = lax.rem(zh + 2, 4) * 4 + first + e if c else zh * 4 + first + e
            o_send[j] = result[:, e * PATCHES : (e + 1) * PATCHES]
            if c:
                o_copy(j).start()
            else:

                @pl.when(j != space)
                def _():
                    o_copy(j).start()

    gather(1)
    gather(2)
    lax.fori_loop(0, 4, early, 0)
    gather(3)
    lax.fori_loop(0, 4, finish_near, 0)
    for k in range(4):
        x_arrived(3, lax.rem(x + k, 4), 1)
    for c in (3, 0):

        def step(n, carry, c=c):
            finish_whole(c, n)
            return carry

        lax.fori_loop(0, 2, step, 0)
    o_recv[space] = o_send[space]
    for k in range(1, TM):
        frame_copy(k).start()

    def t_copy(i, d):
        return remote(t_send.at[i, d], t_recv.at[i, tm], t_ssem.at[i, d], t_rsem.at[i, tm], tm=d)

    peers = [(s, r) for s in (1, 0) for r in range(NEAR) if (s, r) != (0, 0)]

    def peer(s, r):
        return side(s) + lax.rem(yc + r, NEAR)

    for copy in load_rest:
        copy.wait()
    load_out_s.wait()
    for late in range(2):
        i = lax.rem(zh // 2 + late, 2)

        def o_arrived(n, carry, i=i):
            j = i * 8 + n

            @pl.when(j != space)
            def _():
                remote(o_send.at[j], o_recv.at[j], o_ssem.at[j], o_rsem.at[j], space=j).wait_recv()

            return carry

        lax.fori_loop(0, 8, o_arrived, 0)
        mixed = []
        for e in range(2):
            f = 2 * i + e
            attended = o_recv[pl.ds(4 * f, 4)].reshape(INNER, PATCHES)
            mixed.append(jnp.transpose(attended.astype(F32)).astype(BF16))
        branch = matmul(jnp.concatenate(mixed, axis=0), out_s_held[...])
        stream = video_held[pl.ds(2 * i, 2)].reshape(2 * PATCHES, D).astype(F32)
        stream = (stream + gate_s[...].reshape(1, D) * branch).reshape(2, TM, 8, D)
        t_send[i] = jnp.stack([stream[0], stream[1]], axis=1).reshape(TM, 16, D).astype(BF16)
        for s, r in peers:
            t_copy(i, peer(s, r)).start()
        t_recv[i, tm] = t_send[i, tm]

    def frame_arrived(k, carry):
        j = lax.rem(tm + k, TM)
        remote(frame_recv.at[tm], frame_recv.at[j], f_ssem.at[j], f_rsem.at[j], tm=j).wait_recv()
        return carry

    lax.fori_loop(1, TM, frame_arrived, 0)

    for s in range(2):
        for n in range(NEAR):
            for i in range(2):
                at = s * 32 + i * 16 + n * 2
                frame_rows[at : at + 2] = frame_recv[side(s) + n, 2 * i : 2 * i + 2]
    angles = frame_rows[:, 0:1] * table_t[0:1, :]
    sine = jnp.sin(angles)
    time_rows[0] = jnp.cos(angles)
    time_rows[1] = sine * table_t[1:2, :]
    time_rows[2] = sine * table_t[2:3, :]

    def widen(g, carry):
        rows = pl.ds(pl.multiple_of(g * 8, 8), 8)
        for n in range(3):
            time_tables[n, rows] = jnp.broadcast_to(time_rows[n, pl.ds(g, 1)], (8, WIDE))
        return carry

    lax.fori_loop(0, 64, widen, 0)

    for copy in load_w_t:
        copy.wait()
    for s in range(2):
        for r in range(NEAR):
            if (s, r) != (0, 0):
                j = peer(s, r)
                for i in range(2):
                    remote(
                        t_send.at[i, j], t_recv.at[i, j], t_ssem.at[i, j], t_rsem.at[i, j], tm=j
                    ).wait_recv()
        rows = t_recv[:, pl.ds(side(s), NEAR)].reshape(2 * PATCHES, D)
        y = matmul_t(
            modulated(rows, scale_t[...].reshape(1, D), shift_t[...].reshape(1, D)), w_t_held[...]
        )
        angle = [time_tables[n, s * 256 : (s + 1) * 256] for n in range(3)]
        joined[s, :, 0:WIDE] = rotated(y[:, 0:WIDE], *angle, HD // 2, 1).astype(BF16)
        joined[s, :, WIDE : 2 * INNER] = y[:, WIDE : 2 * INNER].astype(BF16)
        joined[s, :, 2 * INNER :] = rotated(y[:, 2 * INNER :], *angle, HD // 2, 1).astype(BF16)

    def r_copy(s, r):
        d = peer(s, r)
        n = lax.rem(yc + r, NEAR)
        return remote(r_send.at[s, :, n], r_recv.at[:, tm], r_ssem.at[d], r_rsem.at[tm], tm=d)

    def window(start, count):
        low = start // 128 * 128
        high = (start + HD + 127) // 128 * 128
        lane = lax.broadcasted_iota(jnp.int32, (count, high - low), 1)
        return low, high, (lane >= start - low) & (lane < start - low + HD)

    same = lax.rem(lax.broadcasted_iota(jnp.int32, (256, TOKENS), 0), 8) == lax.rem(
        lax.broadcasted_iota(jnp.int32, (256, TOKENS), 1), 8
    )
    for s in (1, 0):
        total[...] = jnp.zeros((256, WIDE), F32)
        for h in range(HEADS):
            low, high, inside = window(h * HD, TOKENS)
            keys = joined[:, :, 2 * INNER + low : 2 * INNER + high].reshape(TOKENS, high - low)
            keys = jnp.where(inside, keys, jnp.zeros_like(keys))
            scores = jnp.where(same, matmul_t(joined[s, :, low:high], keys), -1e30)
            top = jnp.max(scores, axis=1, keepdims=True)
            weights = jnp.exp2((scores - top) * FACTOR)
            sums = jnp.sum(weights, axis=1, keepdims=True)
            low, high, inside = window(HALF + h * HD, 256)
            base = INNER - HALF
            values = joined[:, :, base + low : base + high].reshape(TOKENS, high - low)
            part = matmul(weights.astype(BF16), values)
            total[:, low:high] += jnp.where(inside, part / sums, 0.0)
        r_send[s] = total[...].astype(BF16).reshape(2, NEAR, 16, WIDE)
        for r in range(NEAR):
            if (s, r) != (0, 0):
                r_copy(s, r).start()
    r_recv[:, tm] = r_send[0, :, yc]

    load_out_t.wait()
    stores = []
    for s in range(2):
        for r in range(NEAR):
            if (s, r) != (0, 0):
                j = peer(s, r)
                remote(
                    r_send.at[0, :, 0], r_recv.at[:, j], r_ssem.at[j], r_rsem.at[j], tm=j
                ).wait_recv()
        near = pl.ds(side(s), NEAR)
        branch = matmul(r_recv[:, near].reshape(2 * PATCHES, WIDE), out_t_held[...])
        stream = t_send[:, near].reshape(2 * PATCHES, D).astype(F32)
        stream = (stream + gate_t[...].reshape(1, D) * branch).reshape(2, NEAR, 2, 8, D)
        patches = pl.ds(pl.multiple_of(side(s) * 8, 64), 64)
        for i in range(2):
            for e in range(2):
                result[2 * i + e, patches] = stream[i, :, e].reshape(64, D).astype(BF16)
        store = pltpu.make_async_copy(result.at[:, patches], out.at[:, patches], l_sem.at[s])
        store.start()
        stores.append(store)

    for store in stores:
        store.wait()
    for n in range(2):
        pos_copy(n).wait_send()
    for c in range(4):
        for k in range(0 if c == 3 else 1, 4):
            for copy in x_copies(c, k):
                copy.wait_send()

    def o_sent(k, carry):
        o_copy(lax.rem(space + k, SPACE)).wait_send()
        frame_copy(k).wait_send()
        return carry

    lax.fori_loop(1, SPACE, o_sent, 0)
    for s, r in peers:
        for i in range(2):
            t_copy(i, peer(s, r)).wait_send()
        r_copy(s, r).wait_send()


def block(*arrays):
    smem = pl.BlockSpec(memory_space=pltpu.SMEM)
    hbm = pl.BlockSpec(memory_space=pl.ANY)
    dma = pltpu.SemaphoreType.DMA
    specs = [hbm, hbm, hbm, smem] + [hbm] * 12
    held = [((PATCHES,), jnp.int32)] * 2 + [((D,), F32)] * 6 + [((HD, 8), F32), ((8, WIDE), F32)]
    held += [
        ((FRAMES, PATCHES, D), BF16),
        ((3 * INNER, D), BF16),
        ((INNER, D), BF16),
        ((LANES, D), BF16),
        ((WIDE, D), BF16),
        ((8, PATCHES), F32),
        ((2, PATCHES, D), BF16),
        ((2, 8, PATCHES), F32),
        ((TM, 8, 128), F32),
        ((64, 128), F32),
        ((3, 64, WIDE), F32),
        ((3, TOKENS, WIDE), F32),
        ((4, 4, 3 * PAIR, PATCHES), BF16),
        ((4, 4, 3 * PAIR, PATCHES), BF16),
        ((KEYS, PAIR), BF16),
        ((KEYS, PAIR), BF16),
        ((PAIR + 16, KEYS), BF16),
        ((KEYS, 2 * PATCHES), F32),
        ((KEYS, 2 * PATCHES), F32),
        ((4, 2, 8, 2 * PATCHES), F32),
        ((4, 2, PAIR + 16, 2 * PATCHES), F32),
        ((SPACE, PAIR, PATCHES), BF16),
        ((SPACE, PAIR, PATCHES), BF16),
        ((2, TM, 16, D), BF16),
        ((2, TM, 16, D), BF16),
        ((2, 256, LANES), BF16),
        ((256, WIDE), F32),
        ((2, 2, NEAR, 16, WIDE), BF16),
        ((2, TM, 16, WIDE), BF16),
        ((FRAMES, PATCHES, D), BF16),
    ]
    sems = [(20,), (2, 2), (2, 2), (2,), (2,), (TM,), (TM,), (5, 4), (5, 4)]
    sems += [(SPACE,), (SPACE,), (2, TM), (2, TM), (TM,), (TM,)]
    return pl.pallas_call(
        kernel,
        out_shape=jax.ShapeDtypeStruct((FRAMES, PATCHES, D), BF16),
        in_specs=specs,
        out_specs=hbm,
        scratch_shapes=[pltpu.VMEM(*h) for h in held] + [dma(s) for s in sems],
        compiler_params=pltpu.CompilerParams(
            collective_id=1, has_side_effects=True, vmem_limit_bytes=56 * 2**20
        ),
        name="space_time_block",
    )(*arrays)


def space_table():
    f = 10000.0 ** (-np.arange(HD // 4, dtype=np.float32) / (HD // 4))
    zero = np.zeros_like(f)
    one = np.ones_like(f)
    table = np.zeros((HD, 8), np.float32)
    table[:, 0] = np.concatenate([f, f, zero, zero])
    table[:, 1] = np.concatenate([zero, zero, f, f])
    table[:, 2] = np.concatenate([-one, zero, -one, zero])
    table[:, 3] = np.concatenate([zero, one, zero, one])
    return jnp.asarray(table)


def time_table():
    f = 10000.0 ** (-np.arange(HD // 2, dtype=np.float32) / (HD // 2))
    zero = np.zeros_like(f)
    one = np.ones_like(f)
    table = np.zeros((8, WIDE), np.float32)
    table[0, :INNER] = np.tile(np.concatenate([f, f]), HEADS)
    table[1, :INNER] = np.tile(np.concatenate([-one, zero]), HEADS)
    table[2, :INNER] = np.tile(np.concatenate([zero, one]), HEADS)
    return jnp.asarray(table)


def body(*arrays):
    arrays = list(arrays)
    for n in (7, 12):
        arrays[n] = arrays[n].T
    return block(*arrays, space_table(), time_table())


def solution(mesh):
    return jax.shard_map(
        body,
        mesh=mesh,
        in_specs=(P("tm", "space", None), P("space"), P("space"), P("tm")) + (P(),) * 10,
        out_specs=P("tm", "space", None),
        check_vma=False,
    )
```
